512 devices in a mesh: ctx: 32 (over x_hi, z), tp: 16 (over y, x_lo, core).
Axes of the slice: x: 4 (x_hi: 2, x_lo: 2; x = x_hi * 2 + x_lo), y: 4, z: 16, core: 2. Of those that a mesh axis runs over, the one named last changes fastest.
Arguments:
- queries: bfloat16 [16384, 4096], P('ctx', 'tp'), may hold values from -12 to 12
- keys: bfloat16 [16384, 512], P('ctx'), may hold values from -5 to 5
- values: bfloat16 [16384, 512], P('ctx'), may hold values from -6 to 6
- out_grad: bfloat16 [16384, 4096], P('ctx', 'tp'), may hold values from -6 to 6
- doc_lengths: int32 [32], replicated, may hold values from 1 to 2048, 16384 in all
Outputs:
- attn_out: bfloat16 [16384, 4096], P('ctx', 'tp')
- query_grad: bfloat16 [16384, 4096], P('ctx', 'tp')
- key_grad: bfloat16 [16384, 512], P('ctx')
- value_grad: bfloat16 [16384, 512], P('ctx')
The draws below stay inside these ranges and needn't reach their ends.
Inputs may be any that keep to these rules, and one draw needn't show every extreme that they name: `doc_lengths`: the lengths sum to 16384; the largest is exactly 2048.
All inputs are finite; a program needn't handle non-finite values.
Results may differ from the reference program's by a relative error of at most 0.025.
Values may be sent and summed in bfloat16 or wider, within the bound.
A program may use at most 128 MiB of HBM per device.

```python
import math
import jax
import jax.numpy as jnp
import numpy as np
from jax import lax

H = 32
KVH = 4
HD = 128
TOK_DEV = 512
REACH = 4
TOKENS = 16384
MOST = 2048
NDOC = 32


def shared_base(key):
    return jax.random.normal(key, (TOKENS, KVH * HD), jnp.float32)


def draw_keys(key, part):
    base = shared_base(key)
    key = jax.random.fold_in(key, 5)
    drawn = jnp.clip(jax.random.normal(key, base.shape, jnp.float32), -5.0, 5.0)
    return drawn.astype(jnp.bfloat16)


def draw_queries(key, part):
    key = jax.random.fold_in(key, 9)
    drawn = jnp.clip(jax.random.normal(key, (TOKENS, H * HD), jnp.float32), -4.0, 4.0)
    return drawn.astype(jnp.bfloat16)


def block_levels(rng, dims, cuts, smallest, high):
    def one(dim, shards_of):
        steps = jax.random.uniform(jax.random.fold_in(jax.random.fold_in(rng, 6), dim), (shards_of,), jnp.float32, smallest / len(cuts), high / len(cuts))
        return jnp.repeat(jnp.exp(steps), dims[dim] // shards_of).reshape((-1,) + (1,) * (len(dims) - dim - 1))

    gain = one(*cuts[0])
    for cut in cuts[1:]:
        gain = gain * one(*cut)
    return gain


def split_up(count, total, most, skew):
    loads = [(1 << 20) // math.isqrt(grade ** skew) + 1 for grade in range(2, count + 1)]
    spare, given = total - most - (count - 1), [1] * (count - 1)
    while spare > 0:
        candidates = [i for i in range(count - 1) if given[i] < most]
        pool, remaining = sum([loads[i] for i in candidates]), spare
        for i in candidates:
            extra = min(most - given[i], max(1, remaining * loads[i] // pool), spare)
            given[i] = given[i] + extra
            spare = spare - extra
    return np.array([most] + given)


def uneven_parts(stream_key, count, total, bound, skew):
    if count == 2:
        one = jax.random.randint(stream_key, (), max(1, total - bound), min(bound, total - 1) + 1)
        return jnp.stack([one, total - one])
    lengths = jnp.asarray(split_up(count, total, bound, skew), jnp.int32)
    twos = (count - 1) // 2
    source_of, receiver = lengths[1:1 + 2 * twos:2], lengths[2:2 + 2 * twos:2]
    room = jnp.minimum(source_of - 1, bound - receiver)
    moved = jax.random.randint(jax.random.fold_in(stream_key, 1), (twos,), 0, 1 << 20) % (room + 1)
    lengths = lengths.at[1:1 + 2 * twos:2].set(source_of - moved).at[2:2 + 2 * twos:2].set(receiver + moved)
    return lengths[jax.random.permutation(jax.random.fold_in(stream_key, 2), count)]


def gaussian(key, dims, deviation, most, pieces=(), kind=jnp.bfloat16):
    loudness = block_levels(key, dims, pieces, -0.22, 0.18) if pieces else 1.0
    values = jax.random.normal(key, dims, jnp.float32) * deviation * loudness
    return jnp.minimum(jnp.maximum(values, -most), most).astype(kind)


def setup_inputs(seed: int = 0) -> dict:
    arg_keys = jax.random.split(jax.random.key(seed), 6)
    return {
        "queries": draw_queries(jax.random.fold_in(arg_keys[5], 71), 0),
        "keys": draw_keys(jax.random.fold_in(arg_keys[5], 71), 0),
        "values": gaussian(arg_keys[2], (TOKENS, KVH * HD), 1.0, 6.0, ((0, 32),)),
        "out_grad": gaussian(arg_keys[3], (TOKENS, H * HD), 1.0, 6.0, ((0, 32), (1, 16))),
        "doc_lengths": uneven_parts(arg_keys[4], NDOC, TOKENS, MOST, 2).astype(jnp.int32),
    }


NEG = -1e+30

def doc_index(positions, ends):
    return lax.optimization_barrier(jnp.sum((positions[:, None] >= ends[None, :]).astype(jnp.int32), axis=1)).astype(jnp.int32)

def reference(queries, keys, values, out_grad, doc_lengths):
    group = H // KVH
    scale = 1.0 / math.sqrt(HD)
    ends = jnp.cumsum(doc_lengths).astype(jnp.int32)
    span = REACH * TOK_DEV
    width = span + TOK_DEV
    positions = jnp.arange(TOKENS, dtype=jnp.int32)
    docs = doc_index(positions, ends)
    key_pad = jnp.concatenate([jnp.zeros((span, KVH * HD), keys.dtype), keys], 0)
    val_pad = jnp.concatenate([jnp.zeros((span, KVH * HD), values.dtype), values], 0)
    kpos_pad = jnp.arange(-span, TOKENS, dtype=jnp.int32)
    kdoc_pad = jnp.concatenate([jnp.full((span,), -1, jnp.int32), docs], 0)
    zeros = jnp.zeros((span + TOKENS, KVH, HD), jnp.float32)

    def one_block(carry, index):
        key_acc, val_acc = carry
        start = (index * TOK_DEV).astype(jnp.int32)
        qrows = lax.dynamic_slice_in_dim(queries, start, TOK_DEV, 0).astype(jnp.float32).reshape(TOK_DEV, H, HD)
        grows = lax.dynamic_slice_in_dim(out_grad, start, TOK_DEV, 0).astype(jnp.float32).reshape(TOK_DEV, H, HD)
        qpos = lax.dynamic_slice_in_dim(positions, start, TOK_DEV, 0)
        qdoc = lax.dynamic_slice_in_dim(docs, start, TOK_DEV, 0)
        kwin = lax.dynamic_slice_in_dim(key_pad, start, width, 0).astype(jnp.float32).reshape(width, KVH, 1, HD)
        vwin = lax.dynamic_slice_in_dim(val_pad, start, width, 0).astype(jnp.float32).reshape(width, KVH, 1, HD)
        kwide = jnp.broadcast_to(kwin, (width, KVH, group, HD)).reshape(width, H, HD)
        vwide = jnp.broadcast_to(vwin, (width, KVH, group, HD)).reshape(width, H, HD)
        kpos = lax.dynamic_slice_in_dim(kpos_pad, start, width, 0)
        kdoc = lax.dynamic_slice_in_dim(kdoc_pad, start, width, 0)
        mask = (qdoc[:, None] == kdoc[None, :]) & (kpos[None, :] <= qpos[:, None]) & (kpos[None, :] >= 0)
        scores = jnp.einsum('qhd,khd->hqk', qrows, kwide) * scale
        top = lax.optimization_barrier(jnp.max(jnp.where(mask[None], scores, NEG), axis=2))
        lse = top + jnp.log(lax.optimization_barrier(jnp.sum(jnp.where(mask[None], jnp.exp(scores - top[:, :, None]), 0.0), axis=2)))
        probs = jnp.where(mask[None], jnp.exp(scores - lse[:, :, None]), 0.0)
        probs_b = lax.optimization_barrier(probs.astype(jnp.bfloat16)).astype(jnp.float32)
        attn = jnp.einsum('hqk,khd->qhd', probs_b, vwide).astype(jnp.bfloat16)
        delta = lax.optimization_barrier(jnp.sum(grows * attn.astype(jnp.float32), axis=2)).T
        dprob = jnp.einsum('qhd,khd->hqk', grows, vwide)
        dscore = lax.optimization_barrier((probs * (dprob - delta[:, :, None])).astype(jnp.bfloat16)).astype(jnp.float32)
        qgrad = (jnp.einsum('hqk,khd->qhd', dscore, kwide) * scale).astype(jnp.bfloat16)
        kgrad = (jnp.einsum('hqk,qhd->khd', dscore, qrows) * scale).reshape(width, KVH, group, HD).sum(axis=2)
        vgrad = jnp.einsum('hqk,qhd->khd', probs_b, grows).reshape(width, KVH, group, HD).sum(axis=2)
        key_acc = lax.dynamic_update_slice_in_dim(key_acc, lax.dynamic_slice_in_dim(key_acc, start, width, 0) + kgrad, start, 0)
        val_acc = lax.dynamic_update_slice_in_dim(val_acc, lax.dynamic_slice_in_dim(val_acc, start, width, 0) + vgrad, start, 0)
        return ((key_acc, val_acc), (attn.reshape(TOK_DEV, H * HD), qgrad.reshape(TOK_DEV, H * HD)))
    (key_acc, val_acc), (attns, qgrads) = lax.scan(one_block, (zeros, zeros), jnp.arange(TOKENS // TOK_DEV, dtype=jnp.int32))
    attn_out = attns.reshape(TOKENS, H * HD)
    query_grad = qgrads.reshape(TOKENS, H * HD)
    key_grad = key_acc[span:].reshape(TOKENS, KVH * HD).astype(jnp.bfloat16)
    value_grad = val_acc[span:].reshape(TOKENS, KVH * HD).astype(jnp.bfloat16)
    return (attn_out, query_grad, key_grad, value_grad)
```

```python
import functools
import math

import jax
import jax.numpy as jnp
from jax import lax
from jax.experimental import pallas as pl
from jax.experimental.pallas import tpu as pltpu
from jax.sharding import PartitionSpec as P

MESH = pl.DeviceIdType.MESH
HD = 128
KVH = 4
REACH = 4
BLK = 512
QN = 1024
CH = 256
QUART = 128
NSUB = 2
SUB = QUART // NSUB
STRAIGHT = (3, 4)
NEG = -1e30
FLOOR = -1e9
SCALE = 1.0 / math.sqrt(HD)
EXPC = SCALE * math.log2(math.e)
F32 = jnp.float32
BF = jnp.bfloat16


def nt(a, b):
    return lax.dot_general(a, b, (((1,), (1,)), ((), ())), preferred_element_type=F32)


def nn(a, b):
    return jnp.dot(a, b, preferred_element_type=F32)


def kernel(n_ctx, ndoc, q_hbm, k_hbm, v_hbm, g_hbm, len_ref, o_ref, dq_ref, dk_ref, dv_ref,
           q_in, g_in, kv, qt, gt, kvt, probs, dprob, acc, ot, dqt, gs, qs, ds,
           term, cbuf, dbuf, hold, xsend, xbuf, zbuf, zsend, lsem, ssem, rsem):
    c = lax.axis_index("ctx")
    t = lax.axis_index("tp")
    half_ctx = n_ctx // 2
    y, xlo, core = t // 4, (t // 2) % 2, t % 2
    xhi = c // half_ctx
    xl = xlo + xhi - 2 * xlo * xhi

    def place(ctx, yy, xx, cc):
        hi = ctx // half_ctx
        lo = xx + hi - 2 * xx * hi
        return (ctx, yy * 4 + lo * 2 + cc)

    z_next = place((c + 1) % n_ctx, y, xl, core)
    z_prev = place((c + n_ctx - 1) % n_ctx, y, xl, core)
    x_peer = place(c, y, 1 - xl, core)
    c_peer = place(c, y, xl, 1 - core)
    y_next = place(c, (y + 1) % 4, xl, core)
    y_prev = place(c, (y + 3) % 4, xl, core)
    x_diag = place(c, y, 1 - xl, 1 - core)
    y_next_o = place(c, (y + 1) % 4, xl, 1 - core)
    y_prev_o = place(c, (y + 3) % 4, xl, 1 - core)

    col = pl.ds(pl.multiple_of(y * HD, HD), HD)
    my_half = pl.multiple_of(core * 256, 256)
    my_rows = pl.ds(pl.multiple_of(core * 256 + xl * QUART, QUART), QUART)
    sub_rows = [pl.ds(pl.multiple_of(core * 256 + xl * QUART + k * SUB, SUB), SUB) for k in range(NSUB)]
    half_rows = pl.ds(my_half, 256)
    peer_half = pl.ds(pl.multiple_of((1 - core) * 256, 256), 256)

    loads = [
        pltpu.make_async_copy(q_hbm, q_in, lsem.at[0]),
        pltpu.make_async_copy(g_hbm, g_in, lsem.at[1]),
        pltpu.make_async_copy(k_hbm.at[:, col], kv.at[0, 0], lsem.at[2]),
        pltpu.make_async_copy(v_hbm.at[:, col], kv.at[0, 1], lsem.at[3]),
    ]
    for cp in loads:
        cp.start()

    barrier = pltpu.get_barrier_semaphore()
    peers = (z_next, z_prev, x_peer, c_peer, y_next, y_prev, x_diag, y_next_o, y_prev_o)
    for dev in peers:
        pl.semaphore_signal(barrier, inc=1, device_id=dev, device_id_type=MESH)
    pl.semaphore_wait(barrier, len(peers))

    sent = []

    def send(src, dst, dev):
        i = len(sent)
        cp = pltpu.make_async_remote_copy(src_ref=src, dst_ref=dst, send_sem=ssem.at[i], recv_sem=rsem.at[i],
                                          device_id=dev, device_id_type=MESH)
        cp.start()
        sent.append(cp)
        return cp

    zc, xc, cc, dc = {}, {}, {}, {}
    for j, src in ((0, k_hbm), (1, v_hbm)):
        for k in range(NSUB):
            zc[1, j, k] = send(src.at[sub_rows[k], col], kv.at[1, j, sub_rows[k]], z_next)

    lane = lax.broadcasted_iota(jnp.int32, (1, BLK), 1)
    pos = lane + c * BLK
    start = jnp.zeros((1, BLK), jnp.int32)
    end = jnp.int32(0)
    for d in range(ndoc):
        end = end + len_ref[d]
        start = jnp.where(pos >= end, end, start)
    krow = lax.broadcasted_iota(jnp.int32, (BLK, CH), 0)

    for cp in loads:
        cp.wait()
    for h in range(2):
        qt[:, h * BLK:(h + 1) * BLK] = q_in[:, h * HD:(h + 1) * HD].T
        gt[:, h * BLK:(h + 1) * BLK] = g_in[:, h * HD:(h + 1) * HD].T

    nch = QN // CH
    m_run = [jnp.full((1, CH), FLOOR, F32)] * nch
    l_run = [jnp.zeros((1, CH), F32)] * nch
    m_at = {}

    def forward(s):
        keys, vals = kv[s, 0], kv[s, 1]
        kvt[s, 0] = keys.T
        vt = vals.T
        for i in range(nch):
            lo = i * CH
            off = (i * CH) % BLK
            sc = nn(keys, qt[:, lo:lo + CH])
            first = start[:, off:off + CH] - (c - s) * BLK
            seen = krow >= first
            if s == 0:
                seen = seen & (krow <= lane[:, off:off + CH])
            sc = jnp.where(seen, sc, NEG)
            top = jnp.maximum(m_run[i], jnp.max(sc, axis=0, keepdims=True))
            p = jnp.exp2(sc * EXPC - top * EXPC)
            fade = jnp.exp2((m_run[i] - top) * EXPC)
            l_run[i] = l_run[i] * fade + jnp.sum(p, axis=0, keepdims=True)
            m_run[i] = top
            m_at[s, i] = top
            pb = p.astype(BF)
            probs[s, :, lo:lo + CH] = pb
            part = nn(vt, pb)
            if s == 0:
                acc[:, lo:lo + CH] = part
            else:
                acc[:, lo:lo + CH] = acc[:, lo:lo + CH] * fade + part
            dprob[s, :, lo:lo + CH] = nn(vals, gt[:, lo:lo + CH])

    def take_z(s):
        for j in range(2):
            for k in range(NSUB):
                zc[s, j, k].wait_recv()
                if s < REACH:
                    zc[s + 1, j, k] = send(kv.at[s, j, sub_rows[k]], kv.at[s + 1, j, sub_rows[k]], z_next)
            piece = kv.at[s, j, my_rows]
            xc[s, j] = send(piece, piece, x_peer)
            if s == REACH:
                dc[s, j] = send(piece, piece, x_diag)
                cc[s, j] = send(piece, piece, c_peer)

    def take_x(s):
        for j in range(2):
            xc[s, j].wait_recv()
            if s < REACH:
                cc[s, j] = send(kv.at[s, j, half_rows], kv.at[s, j, half_rows], c_peer)

    def take_c(s):
        for j in range(2):
            cc[s, j].wait_recv()
            if s == REACH:
                dc[s, j].wait_recv()

    take_z(1)
    for s in range(1, REACH + 1):
        if s < REACH:
            take_z(s + 1)
            take_x(s)
        if s > 1:
            take_c(s - 1)
        forward(s - 1)
    take_x(REACH)
    take_c(REACH)
    forward(REACH)

    inv, delta = [], []
    for i in range(nch):
        inv.append(1.0 / l_run[i])

    def finish():
        for i in range(nch):
            lo = i * CH
            out = (acc[:, lo:lo + CH] * inv[i]).astype(BF)
            ot[:, lo:lo + CH] = out
            delta.append(jnp.sum(gt[:, lo:lo + CH].astype(F32) * out.astype(F32), axis=0, keepdims=True))

    bc, bx, bz = {}, {}, {}
    far_x = pl.ds(pl.multiple_of(core * 256 + (1 - xl) * QUART, QUART), QUART)
    far_c = pl.ds(pl.multiple_of((1 - core) * 256 + xl * QUART, QUART), QUART)
    far_d = pl.ds(pl.multiple_of((1 - core) * 256 + (1 - xl) * QUART, QUART), QUART)

    def give(s, j):
        if s in STRAIGHT:
            bx[s, j] = [send(term.at[s, j, rows], dbuf.at[s - STRAIGHT[0], j, i], dev)
                        for i, (rows, dev) in enumerate(((far_x, x_peer), (far_d, x_diag), (far_c, c_peer)))]
        else:
            bc[s, j] = send(term.at[s, j, peer_half], cbuf.at[s, j], c_peer)

    def backward(s):
        b = s % 2
        fac = [jnp.exp2((m_at[s, i] - m_run[i]) * EXPC) * inv[i] for i in range(nch)]
        for i in range(nch):
            lo = i * CH
            gs[b, :, lo:lo + CH] = (gt[:, lo:lo + CH].astype(F32) * fac[i]).astype(BF)
            qs[b, :, lo:lo + CH] = (qt[:, lo:lo + CH].astype(F32) * (fac[i] * SCALE)).astype(BF)
        term[s, 1] = nt(probs[s], gs[b]).astype(BF)
        give(s, 1)
        if s == REACH:
            finish()
        for i in range(nch):
            lo = i * CH
            dsc = (probs[s, :, lo:lo + CH].astype(F32) * (dprob[s, :, lo:lo + CH] - delta[i])).astype(BF)
            ds[b, :, lo:lo + CH] = dsc
            part = nn(kvt[s, 0], dsc) * fac[i]
            if s == REACH:
                dqt[:, lo:lo + CH] = part
            else:
                dqt[:, lo:lo + CH] = dqt[:, lo:lo + CH] + part
        term[s, 0] = nt(ds[b], qs[b]).astype(BF)
        give(s, 0)

    mine = pl.ds(pl.multiple_of(xl * QUART, QUART), QUART)
    other = pl.ds(pl.multiple_of((1 - xl) * QUART, QUART), QUART)
    other_rows = pl.ds(pl.multiple_of(core * 256 + (1 - xl) * QUART, QUART), QUART)

    def fold_c(s):
        for j in (1, 0):
            bc[s, j].wait_recv()
            xsend[s, j] = (term[s, j, other_rows].astype(F32) + cbuf[s, j, other].astype(F32)).astype(BF)
            bx[s, j] = send(xsend.at[s, j], xbuf.at[s, j], x_peer)
            hold[s, j] = term[s, j, my_rows].astype(F32) + cbuf[s, j, mine].astype(F32)

    outs = (dk_ref, dv_ref)

    def fold_x(s):
        for j in (1, 0):
            if s in STRAIGHT:
                for cp in bx[s, j]:
                    cp.wait_recv()
            else:
                bx[s, j].wait_recv()
            for k in range(NSUB):
                rows = slice(k * SUB, (k + 1) * SUB)
                if s in STRAIGHT:
                    near = dbuf.at[s - STRAIGHT[0], j]
                    total = term[s, j, sub_rows[k]].astype(F32) + near[0, rows].astype(F32)
                    total = total + near[1, rows].astype(F32) + near[2, rows].astype(F32)
                else:
                    total = hold[s, j, rows] + xbuf[s, j, rows].astype(F32)
                if s < REACH:
                    bz[s + 1, j, k].wait_recv()
                    total = total + zbuf[s, j, rows].astype(F32)
                if s > 0:
                    zsend[s, j, rows] = total.astype(BF)
                    bz[s, j, k] = send(zsend.at[s, j, rows], zbuf.at[s - 1, j, rows], z_prev)
                else:
                    outs[j][sub_rows[k], col] = total.astype(BF)
            if s == 0:
                spread(j)

    ax, aup, adn, xup, xdn = {}, {}, {}, {}, {}

    def spread(j):
        piece = outs[j].at[my_rows, col]
        ax[j] = send(piece, piece, x_peer)
        aup[j] = send(piece, piece, y_next)
        adn[j] = send(piece, piece, y_prev)

    backward(4)
    backward(3)
    backward(2)
    fold_x(4)
    backward(1)
    fold_c(2)
    backward(0)
    fold_x(3)
    fold_c(1)
    fold_c(0)
    for h in range(2):
        o_ref[:, h * HD:(h + 1) * HD] = ot[:, h * BLK:(h + 1) * BLK].T
    fold_x(2)
    for h in range(2):
        dq_ref[:, h * HD:(h + 1) * HD] = (dqt[:, h * BLK:(h + 1) * BLK] * SCALE).astype(BF).T
    fold_x(1)
    fold_x(0)

    below = pl.ds(pl.multiple_of(((y + 3) % 4) * HD, HD), HD)
    above = pl.ds(pl.multiple_of(((y + 1) % 4) * HD, HD), HD)
    across = pl.ds(pl.multiple_of(((y + 2) % 4) * HD, HD), HD)

    def hrow(which, k):
        return pl.ds(pl.multiple_of(core * 256 + which * QUART + k * 64, 64), 64)

    fin = []

    def relay(j, which):
        up = outs[j].at[hrow(which, 0), below]
        dn = outs[j].at[hrow(which, 1), above]
        fin.append(send(up, up, y_next))
        fin.append(send(dn, dn, y_prev))
        fin.append(send(up, up, y_next_o))
        fin.append(send(dn, dn, y_prev_o))

    for j in (1, 0):
        ax[j].wait_recv()
        piece = outs[j].at[other_rows, col]
        xup[j] = send(piece, piece, y_next)
        xdn[j] = send(piece, piece, y_prev)
        piece = outs[j].at[half_rows, col]
        fin.append(send(piece, piece, c_peer))
    for j in (1, 0):
        aup[j].wait_recv()
        adn[j].wait_recv()
        relay(j, xl)
    for j in (1, 0):
        xup[j].wait_recv()
        xdn[j].wait_recv()
        relay(j, 1 - xl)
        for cols in (below, above):
            piece = outs[j].at[half_rows, cols]
            fin.append(send(piece, piece, c_peer))
    for cp in fin:
        cp.wait_recv()
    for cp in sent:
        cp.wait_send()
    assert len(sent) == N_SEND, len(sent)


def place_outputs(*refs):
    n = (len(refs) - 1) // 2
    sem = refs[-1]
    copies = [pltpu.make_async_copy(refs[i], refs[n + i], sem.at[i]) for i in range(n)]
    for cp in copies:
        cp.start()
    for cp in copies:
        cp.wait()


N_SEND = 106


def solution(mesh):
    n_ctx = mesh.shape["ctx"]

    def per_device(queries, keys, values, out_grad, doc_lengths):
        steps = REACH + 1
        vm = pl.BlockSpec(memory_space=pltpu.VMEM)
        hbm = pl.BlockSpec(memory_space=pl.ANY)
        shapes = tuple(jax.ShapeDtypeStruct(a.shape, BF) for a in (queries, queries, keys, values))
        raw = pl.pallas_call(
            functools.partial(kernel, n_ctx, doc_lengths.shape[0]),
            out_shape=shapes,
            in_specs=[hbm, hbm, hbm, hbm, pl.BlockSpec(memory_space=pltpu.SMEM)],
            out_specs=(vm, vm, vm, vm),
            scratch_shapes=[
                pltpu.VMEM((BLK, 256), BF),
                pltpu.VMEM((BLK, 256), BF),
                pltpu.VMEM((steps, 2, BLK, HD), BF),
                pltpu.VMEM((HD, QN), BF),
                pltpu.VMEM((HD, QN), BF),
                pltpu.VMEM((steps, 1, HD, BLK), BF),
                pltpu.VMEM((steps, BLK, QN), BF),
                pltpu.VMEM((steps, BLK, QN), F32),
                pltpu.VMEM((HD, QN), F32),
                pltpu.VMEM((HD, QN), BF),
                pltpu.VMEM((HD, QN), F32),
                pltpu.VMEM((2, HD, QN), BF),
                pltpu.VMEM((2, HD, QN), BF),
                pltpu.VMEM((2, BLK, QN), BF),
                pltpu.VMEM((steps, 2, BLK, HD), BF),
                pltpu.VMEM((steps, 2, 256, HD), BF),
                pltpu.VMEM((len(STRAIGHT), 2, 3, QUART, HD), BF),
                pltpu.VMEM((steps, 2, QUART, HD), F32),
                pltpu.VMEM((steps, 2, QUART, HD), BF),
                pltpu.VMEM((steps, 2, QUART, HD), BF),
                pltpu.VMEM((REACH, 2, QUART, HD), BF),
                pltpu.VMEM((steps, 2, QUART, HD), BF),
                pltpu.SemaphoreType.DMA((4,)),
                pltpu.SemaphoreType.DMA((N_SEND,)),
                pltpu.SemaphoreType.DMA((N_SEND,)),
            ],
            compiler_params=pltpu.CompilerParams(
                collective_id=0, has_side_effects=True, vmem_limit_bytes=40 * 1024 * 1024
            ),
        )(queries, keys, values, out_grad, doc_lengths)
        return pl.pallas_call(
            place_outputs,
            out_shape=shapes,
            in_specs=[vm] * 4,
            out_specs=(hbm,) * 4,
            scratch_shapes=[pltpu.SemaphoreType.DMA((4,))],
        )(*raw)

    return jax.shard_map(
        per_device,
        mesh=mesh,
        in_specs=(P("ctx", "tp"), P("ctx", None), P("ctx", None), P("ctx", "tp"), P()),
        out_specs=(P("ctx", "tp"), P("ctx", "tp"), P("ctx", None), P("ctx", None)),
        check_vma=False,
    )
```

```python
import functools
import math

import jax
import jax.numpy as jnp
from jax import lax
from jax.experimental import pallas as pl
from jax.experimental.pallas import tpu as pltpu
from jax.sharding import PartitionSpec as P

MESH = pl.DeviceIdType.MESH
HD = 128
KVH = 4
REACH = 4
BLK = 512
QN = 1024
CH = 256
QUART = 128
NSUB = 2
SUB = QUART // NSUB
STRAIGHT = (3, 4)
NEG = -1e30
FLOOR = -1e9
SCALE = 1.0 / math.sqrt(HD)
EXPC = SCALE * math.log2(math.e)
F32 = jnp.float32
BF = jnp.bfloat16


def nt(a, b):
    return lax.dot_general(a, b, (((1,), (1,)), ((), ())), preferred_element_type=F32)


def nn(a, b):
    return jnp.dot(a, b, preferred_element_type=F32)


def kernel(n_ctx, ndoc, q_hbm, k_hbm, v_hbm, g_hbm, len_ref, o_ref, dq_ref, kvg_ref,
           q_in, g_in, kv, qt, gt, kvt, vtr, probs, dprob, acc, ot, dqt, gs, qs, ds,
           term, cbuf, dbuf, hold, xsend, xbuf, zbuf, zsend, lsem, ssem, rsem):
    c = lax.axis_index("ctx")
    t = lax.axis_index("tp")
    half_ctx = n_ctx // 2
    y, xlo, core = t // 4, (t // 2) % 2, t % 2
    xhi = c // half_ctx
    xl = xlo + xhi - 2 * xlo * xhi

    def place(ctx, yy, xx, cc):
        hi = ctx // half_ctx
        lo = xx + hi - 2 * xx * hi
        return (ctx, yy * 4 + lo * 2 + cc)

    z_next = place((c + 1) % n_ctx, y, xl, core)
    z_prev = place((c + n_ctx - 1) % n_ctx, y, xl, core)
    x_peer = place(c, y, 1 - xl, core)
    c_peer = place(c, y, xl, 1 - core)
    y_next = place(c, (y + 1) % 4, xl, core)
    y_prev = place(c, (y + 3) % 4, xl, core)
    x_diag = place(c, y, 1 - xl, 1 - core)
    y_next_o = place(c, (y + 1) % 4, xl, 1 - core)
    y_prev_o = place(c, (y + 3) % 4, xl, 1 - core)

    col = pl.ds(pl.multiple_of(y * HD, HD), HD)
    my_half = pl.multiple_of(core * 256, 256)
    my_rows = pl.ds(pl.multiple_of(core * 256 + xl * QUART, QUART), QUART)
    sub_rows = [pl.ds(pl.multiple_of(core * 256 + xl * QUART + k * SUB, SUB), SUB) for k in range(NSUB)]
    half_rows = pl.ds(my_half, 256)
    peer_half = pl.ds(pl.multiple_of((1 - core) * 256, 256), 256)

    loads = [
        pltpu.make_async_copy(q_hbm, q_in, lsem.at[0]),
        pltpu.make_async_copy(g_hbm, g_in, lsem.at[1]),
        pltpu.make_async_copy(k_hbm.at[:, col], kv.at[0, 0], lsem.at[2]),
        pltpu.make_async_copy(v_hbm.at[:, col], kv.at[0, 1], lsem.at[3]),
    ]
    for cp in loads:
        cp.start()

    barrier = pltpu.get_barrier_semaphore()
    peers = (z_next, z_prev, x_peer, c_peer, y_next, y_prev, x_diag, y_next_o, y_prev_o)
    for dev in peers:
        pl.semaphore_signal(barrier, inc=1, device_id=dev, device_id_type=MESH)
    pl.semaphore_wait(barrier, len(peers))

    sent = []

    def send(src, dst, dev):
        i = len(sent)
        cp = pltpu.make_async_remote_copy(src_ref=src, dst_ref=dst, send_sem=ssem.at[i], recv_sem=rsem.at[i],
                                          device_id=dev, device_id_type=MESH)
        cp.start()
        sent.append(cp)
        return cp

    zc, xc, cc, dc = {}, {}, {}, {}
    for j, src in ((0, k_hbm), (1, v_hbm)):
        for k in range(NSUB):
            zc[1, j, k] = send(src.at[sub_rows[k], col], kv.at[1, j, sub_rows[k]], z_next)

    lane = lax.broadcasted_iota(jnp.int32, (1, BLK), 1)
    pos = lane + c * BLK
    start = jnp.zeros((1, BLK), jnp.int32)
    end = jnp.int32(0)
    for d in range(ndoc):
        end = end + len_ref[d]
        start = jnp.where(pos >= end, end, start)
    krow = lax.broadcasted_iota(jnp.int32, (BLK, CH), 0)

    for cp in loads:
        cp.wait()
    for h in range(2):
        qt[:, h * BLK:(h + 1) * BLK] = q_in[:, h * HD:(h + 1) * HD].T
        gt[:, h * BLK:(h + 1) * BLK] = g_in[:, h * HD:(h + 1) * HD].T

    nch = QN // CH
    m_run = [jnp.full((1, CH), FLOOR, F32)] * nch
    l_run = [jnp.zeros((1, CH), F32)] * nch
    m_at = {}

    def live_rows(s, off):
        if s == 0 and off + CH <= BLK // 2:
            return slice(0, BLK // 2)
        if s == REACH and off >= BLK // 2:
            return slice(BLK // 2, BLK)
        return slice(0, BLK)

    def blank(ref, rows, lo):
        if rows.stop - rows.start < BLK:
            skipped = slice(BLK // 2, BLK) if rows.start == 0 else slice(0, BLK // 2)
            ref[skipped, lo:lo + CH] = jnp.zeros((BLK // 2, CH), BF)

    def forward(s):
        kvt[s, 0] = kv[s, 0].T
        vtr[s % 2] = kv[s, 1].T
        for i in range(nch):
            lo = i * CH
            off = (i * CH) % BLK
            rows = live_rows(s, off)
            sc = nn(kv[s, 0, rows], qt[:, lo:lo + CH])
            first = start[:, off:off + CH] - (c - s) * BLK
            seen = krow[rows] >= first
            if s == 0:
                seen = seen & (krow[rows] <= lane[:, off:off + CH])
            sc = jnp.where(seen, sc, NEG)
            top = jnp.maximum(m_run[i], jnp.max(sc, axis=0, keepdims=True))
            p = jnp.exp2(sc * EXPC - top * EXPC)
            fade = jnp.exp2((m_run[i] - top) * EXPC)
            l_run[i] = l_run[i] * fade + jnp.sum(p, axis=0, keepdims=True)
            m_run[i] = top
            m_at[s, i] = top
            pb = p.astype(BF)
            probs[s, rows, lo:lo + CH] = pb
            blank(probs.at[s], rows, lo)
            part = nn(vtr[s % 2, :, rows], pb)
            if s == 0:
                acc[:, lo:lo + CH] = part
            else:
                acc[:, lo:lo + CH] = acc[:, lo:lo + CH] * fade + part
            dprob[s, rows, lo:lo + CH] = nn(kv[s, 1, rows], gt[:, lo:lo + CH])

    def take_z(s):
        for j in range(2):
            for k in range(NSUB):
                zc[s, j, k].wait_recv()
                if s < REACH:
                    zc[s + 1, j, k] = send(kv.at[s, j, sub_rows[k]], kv.at[s + 1, j, sub_rows[k]], z_next)
            piece = kv.at[s, j, my_rows]
            xc[s, j] = send(piece, piece, x_peer)
            if s == REACH:
                dc[s, j] = send(piece, piece, x_diag)
                cc[s, j] = send(piece, piece, c_peer)

    def take_x(s):
        for j in range(2):
            xc[s, j].wait_recv()
            if s < REACH:
                cc[s, j] = send(kv.at[s, j, half_rows], kv.at[s, j, half_rows], c_peer)

    def take_c(s):
        for j in range(2):
            cc[s, j].wait_recv()
            if s == REACH:
                dc[s, j].wait_recv()

    take_z(1)
    for s in range(1, REACH + 1):
        if s < REACH:
            take_z(s + 1)
            take_x(s)
        if s > 1:
            take_c(s - 1)
        forward(s - 1)
    take_x(REACH)
    take_c(REACH)
    forward(REACH)

    inv, delta = [], []
    for i in range(nch):
        inv.append(1.0 / l_run[i])

    def finish():
        for i in range(nch):
            lo = i * CH
            out = (acc[:, lo:lo + CH] * inv[i]).astype(BF)
            ot[:, lo:lo + CH] = out
            delta.append(jnp.sum(gt[:, lo:lo + CH].astype(F32) * out.astype(F32), axis=0, keepdims=True))

    bc, bx, bz = {}, {}, {}
    far_x = pl.ds(pl.multiple_of(core * 256 + (1 - xl) * QUART, QUART), QUART)
    far_c = pl.ds(pl.multiple_of((1 - core) * 256 + xl * QUART, QUART), QUART)
    far_d = pl.ds(pl.multiple_of((1 - core) * 256 + (1 - xl) * QUART, QUART), QUART)

    def give(s, j):
        if s in STRAIGHT:
            bx[s, j] = [send(term.at[s, j, rows], dbuf.at[s - STRAIGHT[0], j, i], dev)
                        for i, (rows, dev) in enumerate(((far_x, x_peer), (far_d, x_diag), (far_c, c_peer)))]
        else:
            bc[s, j] = send(term.at[s, j, peer_half], cbuf.at[s, j], c_peer)

    def backward(s):
        b = s % 2
        fac = [jnp.exp2((m_at[s, i] - m_run[i]) * EXPC) * inv[i] for i in range(nch)]
        for i in range(nch):
            lo = i * CH
            gs[b, :, lo:lo + CH] = (gt[:, lo:lo + CH].astype(F32) * fac[i]).astype(BF)
            qs[b, :, lo:lo + CH] = (qt[:, lo:lo + CH].astype(F32) * (fac[i] * SCALE)).astype(BF)
        term[s, 1] = nt(probs[s], gs[b]).astype(BF)
        give(s, 1)
        if s == REACH:
            finish()
        for i in range(nch):
            lo = i * CH
            rows = live_rows(s, lo % BLK)
            dsc = (probs[s, rows, lo:lo + CH].astype(F32) * (dprob[s, rows, lo:lo + CH] - delta[i])).astype(BF)
            ds[b, rows, lo:lo + CH] = dsc
            blank(ds.at[b], rows, lo)
            part = nn(kvt[s, 0, :, rows], dsc) * fac[i]
            if s == REACH:
                dqt[:, lo:lo + CH] = part
            else:
                dqt[:, lo:lo + CH] = dqt[:, lo:lo + CH] + part
        term[s, 0] = nt(ds[b], qs[b]).astype(BF)
        give(s, 0)

    mine = pl.ds(pl.multiple_of(xl * QUART, QUART), QUART)
    other = pl.ds(pl.multiple_of((1 - xl) * QUART, QUART), QUART)
    other_rows = pl.ds(pl.multiple_of(core * 256 + (1 - xl) * QUART, QUART), QUART)

    def fold_c(s):
        for j in (1, 0):
            bc[s, j].wait_recv()
            xsend[s, j] = (term[s, j, other_rows].astype(F32) + cbuf[s, j, other].astype(F32)).astype(BF)
            bx[s, j] = send(xsend.at[s, j], xbuf.at[s, j], x_peer)
            hold[s, j] = term[s, j, my_rows].astype(F32) + cbuf[s, j, mine].astype(F32)


    def fold_x(s):
        for j in (1, 0):
            if s in STRAIGHT:
                for cp in bx[s, j]:
                    cp.wait_recv()
            else:
                bx[s, j].wait_recv()
            for k in range(NSUB):
                rows = slice(k * SUB, (k + 1) * SUB)
                if s in STRAIGHT:
                    near = dbuf.at[s - STRAIGHT[0], j]
                    total = term[s, j, sub_rows[k]].astype(F32) + near[0, rows].astype(F32)
                    total = total + near[1, rows].astype(F32) + near[2, rows].astype(F32)
                else:
                    total = hold[s, j, rows] + xbuf[s, j, rows].astype(F32)
                if s < REACH:
                    bz[s + 1, j, k].wait_recv()
                    total = total + zbuf[s, j, rows].astype(F32)
                if s > 0:
                    zsend[s, j, rows] = total.astype(BF)
                    bz[s, j, k] = send(zsend.at[s, j, rows], zbuf.at[s - 1, j, rows], z_prev)
                else:
                    kvg_ref[j, y, sub_rows[k]] = total.astype(BF)
            if s == 0:
                spread(j)

    ax, aup, adn, xup, xdn = {}, {}, {}, {}, {}

    def spread(j):
        piece = kvg_ref.at[j, y, my_rows]
        ax[j] = send(piece, piece, x_peer)
        aup[j] = send(piece, piece, y_next)
        adn[j] = send(piece, piece, y_prev)

    backward(4)
    backward(3)
    backward(2)
    fold_x(4)
    backward(1)
    fold_c(2)
    backward(0)
    fold_x(3)
    fold_c(1)
    fold_c(0)
    for h in range(2):
        o_ref[:, h * HD:(h + 1) * HD] = ot[:, h * BLK:(h + 1) * BLK].T
    fold_x(2)
    for h in range(2):
        dq_ref[:, h * HD:(h + 1) * HD] = (dqt[:, h * BLK:(h + 1) * BLK] * SCALE).astype(BF).T
    fold_x(1)
    fold_x(0)

    below = (y + 3) % 4
    above = (y + 1) % 4

    def hrow(which, k):
        return pl.ds(pl.multiple_of(core * 256 + which * QUART + k * 64, 64), 64)

    fin = []

    def relay(j, which):
        up = kvg_ref.at[j, below, hrow(which, 0)]
        dn = kvg_ref.at[j, above, hrow(which, 1)]
        fin.append(send(up, up, y_next))
        fin.append(send(dn, dn, y_prev))
        fin.append(send(up, up, y_next_o))
        fin.append(send(dn, dn, y_prev_o))

    for j in (1, 0):
        ax[j].wait_recv()
        piece = kvg_ref.at[j, y, other_rows]
        xup[j] = send(piece, piece, y_next)
        xdn[j] = send(piece, piece, y_prev)
        piece = kvg_ref.at[j, y, half_rows]
        fin.append(send(piece, piece, c_peer))
    for j in (1, 0):
        aup[j].wait_recv()
        adn[j].wait_recv()
        relay(j, xl)
    for j in (1, 0):
        xup[j].wait_recv()
        xdn[j].wait_recv()
        relay(j, 1 - xl)
        for cols in (below, above):
            piece = kvg_ref.at[j, cols, half_rows]
            fin.append(send(piece, piece, c_peer))
    for cp in fin:
        cp.wait_recv()
    for cp in sent:
        cp.wait_send()
    assert len(sent) == N_SEND, len(sent)


def place_outputs(o_raw, dq_raw, kvg_raw, o_out, dq_out, dk_out, dv_out, o_v, dq_v, kvg_v, isem, osem):
    fetch = [pltpu.make_async_copy(o_raw, o_v, isem.at[0]), pltpu.make_async_copy(dq_raw, dq_v, isem.at[1])]
    store = [pltpu.make_async_copy(o_v, o_out, osem.at[0]), pltpu.make_async_copy(dq_v, dq_out, osem.at[1])]
    for j, out in enumerate((dk_out, dv_out)):
        for g in range(KVH):
            i = len(fetch)
            fetch.append(pltpu.make_async_copy(kvg_raw.at[j, g], kvg_v.at[j, g], isem.at[i]))
            store.append(pltpu.make_async_copy(kvg_v.at[j, g], out.at[:, g * HD:(g + 1) * HD], osem.at[i]))
    for cp in fetch:
        cp.start()
    for get, put in zip(fetch, store):
        get.wait()
        put.start()
    for cp in store:
        cp.wait()


N_SEND = 106


def solution(mesh):
    n_ctx = mesh.shape["ctx"]

    def per_device(queries, keys, values, out_grad, doc_lengths):
        steps = REACH + 1
        vm = pl.BlockSpec(memory_space=pltpu.VMEM)
        hbm = pl.BlockSpec(memory_space=pl.ANY)
        shapes = tuple(jax.ShapeDtypeStruct(a.shape, BF) for a in (queries, queries, keys, values))
        raw = pl.pallas_call(
            functools.partial(kernel, n_ctx, doc_lengths.shape[0]),
            out_shape=shapes[:2] + (jax.ShapeDtypeStruct((2, KVH, BLK, HD), BF),),
            in_specs=[hbm, hbm, hbm, hbm, pl.BlockSpec(memory_space=pltpu.SMEM)],
            out_specs=(vm, vm, vm),
            scratch_shapes=[
                pltpu.VMEM((BLK, 256), BF),
                pltpu.VMEM((BLK, 256), BF),
                pltpu.VMEM((steps, 2, BLK, HD), BF),
                pltpu.VMEM((HD, QN), BF),
                pltpu.VMEM((HD, QN), BF),
                pltpu.VMEM((steps, 1, HD, BLK), BF),
                pltpu.VMEM((2, HD, BLK), BF),
                pltpu.VMEM((steps, BLK, QN), BF),
                pltpu.VMEM((steps, BLK, QN), F32),
                pltpu.VMEM((HD, QN), F32),
                pltpu.VMEM((HD, QN), BF),
                pltpu.VMEM((HD, QN), F32),
                pltpu.VMEM((2, HD, QN), BF),
                pltpu.VMEM((2, HD, QN), BF),
                pltpu.VMEM((2, BLK, QN), BF),
                pltpu.VMEM((steps, 2, BLK, HD), BF),
                pltpu.VMEM((steps, 2, 256, HD), BF),
                pltpu.VMEM((len(STRAIGHT), 2, 3, QUART, HD), BF),
                pltpu.VMEM((steps, 2, QUART, HD), F32),
                pltpu.VMEM((steps, 2, QUART, HD), BF),
                pltpu.VMEM((steps, 2, QUART, HD), BF),
                pltpu.VMEM((REACH, 2, QUART, HD), BF),
                pltpu.VMEM((steps, 2, QUART, HD), BF),
                pltpu.SemaphoreType.DMA((4,)),
                pltpu.SemaphoreType.DMA((N_SEND,)),
                pltpu.SemaphoreType.DMA((N_SEND,)),
            ],
            compiler_params=pltpu.CompilerParams(
                collective_id=0, has_side_effects=True, vmem_limit_bytes=60 * 1024 * 1024
            ),
        )(queries, keys, values, out_grad, doc_lengths)
        return pl.pallas_call(
            place_outputs,
            out_shape=shapes,
            in_specs=[hbm] * 3,
            out_specs=(hbm,) * 4,
            scratch_shapes=[
                pltpu.VMEM((BLK, 256), BF),
                pltpu.VMEM((BLK, 256), BF),
                pltpu.VMEM((2, KVH, BLK, HD), BF),
                pltpu.SemaphoreType.DMA((10,)),
                pltpu.SemaphoreType.DMA((10,)),
            ],
            compiler_params=pltpu.CompilerParams(vmem_limit_bytes=62 * 1024 * 1024),
        )(*raw)

    return jax.shard_map(
        per_device,
        mesh=mesh,
        in_specs=(P("ctx", "tp"), P("ctx", None), P("ctx", None), P("ctx", "tp"), P()),
        out_specs=(P("ctx", "tp"), P("ctx", "tp"), P("ctx", None), P("ctx", None)),
        check_vma=False,
    )
```

```python
import functools
import math

import jax
import jax.numpy as jnp
from jax import lax
from jax.experimental import pallas as pl
from jax.experimental.pallas import tpu as pltpu
from jax.sharding import PartitionSpec as P

MESH = pl.DeviceIdType.MESH
HD = 128
KVH = 4
REACH = 4
BLK = 512
QN = 1024
CH = 256
RB = 128
QUART = 128
NSUB = 2
SUB = QUART // NSUB
STRAIGHT = (3, 4)
NEG = -1e30
FLOOR = -1e9
SCALE = 1.0 / math.sqrt(HD)
EXPC = SCALE * math.log2(math.e)
F32 = jnp.float32
BF = jnp.bfloat16


def nt(a, b):
    return lax.dot_general(a, b, (((1,), (1,)), ((), ())), preferred_element_type=F32)


def nn(a, b):
    return jnp.dot(a, b, preferred_element_type=F32)


def kernel(n_ctx, ndoc, q_hbm, k_hbm, v_hbm, g_hbm, len_ref, o_ref, dq_ref, kvg_ref,
           q_in, g_in, kv, qt, gt, kvt, vtr, kx, sbuf, probs, dprob, acc, ot, dqt, gs, qs, ds,
           term, cbuf, dbuf, hold, xsend, xbuf, zbuf, zsend, lsem, ssem, rsem):
    c = lax.axis_index("ctx")
    t = lax.axis_index("tp")
    half_ctx = n_ctx // 2
    y, xlo, core = t // 4, (t // 2) % 2, t % 2
    xhi = c // half_ctx
    xl = xlo + xhi - 2 * xlo * xhi

    def place(ctx, yy, xx, cc):
        hi = ctx // half_ctx
        lo = xx + hi - 2 * xx * hi
        return (ctx, yy * 4 + lo * 2 + cc)

    z_next = place((c + 1) % n_ctx, y, xl, core)
    z_prev = place((c + n_ctx - 1) % n_ctx, y, xl, core)
    x_peer = place(c, y, 1 - xl, core)
    c_peer = place(c, y, xl, 1 - core)
    y_next = place(c, (y + 1) % 4, xl, core)
    y_prev = place(c, (y + 3) % 4, xl, core)
    x_diag = place(c, y, 1 - xl, 1 - core)
    y_next_o = place(c, (y + 1) % 4, xl, 1 - core)
    y_prev_o = place(c, (y + 3) % 4, xl, 1 - core)

    col = pl.ds(pl.multiple_of(y * HD, HD), HD)
    my_half = pl.multiple_of(core * 256, 256)
    my_rows = pl.ds(pl.multiple_of(core * 256 + xl * QUART, QUART), QUART)
    sub_rows = [pl.ds(pl.multiple_of(core * 256 + xl * QUART + k * SUB, SUB), SUB) for k in range(NSUB)]
    half_rows = pl.ds(my_half, 256)
    peer_half = pl.ds(pl.multiple_of((1 - core) * 256, 256), 256)

    loads = [
        pltpu.make_async_copy(q_hbm, q_in, lsem.at[0]),
        pltpu.make_async_copy(g_hbm, g_in, lsem.at[1]),
        pltpu.make_async_copy(k_hbm.at[:, col], kv.at[0, 0], lsem.at[2]),
        pltpu.make_async_copy(v_hbm.at[:, col], kv.at[0, 1], lsem.at[3]),
    ]
    for cp in loads:
        cp.start()

    barrier = pltpu.get_barrier_semaphore()
    peers = (x_peer, c_peer, y_next, y_prev, x_diag, y_next_o, y_prev_o)
    for dev, ok in ((z_next, c < n_ctx - 1), (z_prev, c > 0)):
        @pl.when(ok)
        def _(dev=dev):
            pl.semaphore_signal(barrier, inc=1, device_id=dev, device_id_type=MESH)

    for dev in peers:
        pl.semaphore_signal(barrier, inc=1, device_id=dev, device_id_type=MESH)
    pl.semaphore_wait(barrier, len(peers) + jnp.minimum(c, 1) + jnp.minimum(n_ctx - 1 - c, 1))

    sent = []

    def only(ok, act):
        if ok is None:
            act()
        else:
            pl.when(ok)(act)

    def send(src, dst, dev, ok=None):
        i = len(sent)
        cp = pltpu.make_async_remote_copy(src_ref=src, dst_ref=dst, send_sem=ssem.at[i], recv_sem=rsem.at[i],
                                          device_id=dev, device_id_type=MESH)
        only(ok, lambda: cp.start())
        sent.append((cp, ok))
        return cp

    zc, xc, cc, dc = {}, {}, {}, {}
    for j, src in ((0, k_hbm), (1, v_hbm)):
        for k in range(NSUB):
            zc[1, j, k] = send(src.at[sub_rows[k], col], kv.at[1, j, sub_rows[k]], z_next, c < n_ctx - 1)

    lane = lax.broadcasted_iota(jnp.int32, (1, BLK), 1)
    dlane = lax.broadcasted_iota(jnp.int32, (1, HD), 1)
    drow = lax.broadcasted_iota(jnp.int32, (HD, 1), 0)
    lo_l, hi_l = jnp.zeros((1, HD), jnp.int32), jnp.zeros((1, HD), jnp.int32)
    lo_r, hi_r = jnp.zeros((HD, 1), jnp.int32), jnp.zeros((HD, 1), jnp.int32)
    end = jnp.int32(0)
    for d in range(ndoc):
        lo_l, lo_r = jnp.where(dlane == d, end, lo_l), jnp.where(drow == d, end, lo_r)
        end = end + len_ref[d]
        hi_l, hi_r = jnp.where(dlane == d, end, hi_l), jnp.where(drow == d, end, hi_r)
    lo_l = jnp.where(dlane == ndoc, -(1 << 30), lo_l)
    pos = lane + c * BLK
    block_doc = jnp.where((pos >= lo_r) & (pos < hi_r), 0.0, NEG).astype(BF)
    kpos0 = lax.broadcasted_iota(jnp.int32, (BLK, HD), 0) + c * BLK
    krow = lax.broadcasted_iota(jnp.int32, (RB, CH), 0)
    for b in range(2):
        vtr[b, HD:] = jnp.ones((8, BLK), BF)

    for cp in loads:
        cp.wait()
    for h in range(2):
        qt[:HD, h * BLK:(h + 1) * BLK] = q_in[:, h * HD:(h + 1) * HD].T
        qt[HD:, h * BLK:(h + 1) * BLK] = block_doc
        gt[:, h * BLK:(h + 1) * BLK] = g_in[:, h * HD:(h + 1) * HD].T

    nch = QN // CH
    m_run = [jnp.full((1, CH), FLOOR, F32)] * nch
    m_at = {}

    def live_rows(s, off):
        if s == 0 and off + CH <= BLK // 2:
            return slice(0, BLK // 2)
        if s == REACH and off >= BLK // 2:
            return slice(BLK // 2, BLK)
        return slice(0, BLK)

    def blank(ref, rows, lo):
        if rows.stop - rows.start < BLK:
            skipped = slice(BLK // 2, BLK) if rows.start == 0 else slice(0, BLK // 2)
            ref[skipped, lo:lo + CH] = jnp.zeros((BLK // 2, CH), BF)

    def forward(s):
        b = s % 2
        kvt[s, 0] = kv[s, 0].T
        vtr[b, :HD] = kv[s, 1].T
        kx[b, :, :HD] = kv[s, 0]
        kpos = kpos0 - s * BLK
        kx[b, :, HD:] = jnp.where((kpos >= lo_l) & (kpos < hi_l), 1.0, 0.0).astype(BF)
        for i in range(nch):
            lo = i * CH
            off = (i * CH) % BLK
            cols = slice(lo, lo + CH)
            rows = live_rows(s, off)
            pieces = [slice(r, r + RB) for r in range(rows.start, rows.stop, RB)]
            top = m_run[i]
            for piece in pieces:
                sc = nn(kx[b, piece], qt[:, cols])
                if s == 0 and piece.stop > off:
                    sc = jnp.where(krow + piece.start <= lane[:, off:off + CH], sc, NEG)
                sbuf[i % 2, piece] = sc
                top = jnp.maximum(top, jnp.max(sc, axis=0, keepdims=True))
            scaled = top * EXPC
            for piece in pieces:
                probs[s, piece, cols] = jnp.exp2(sbuf[i % 2, piece] * EXPC - scaled).astype(BF)
            fade = jnp.exp2((m_run[i] - top) * EXPC)
            m_run[i] = top
            m_at[s, i] = top
            blank(probs.at[s], rows, lo)
            part = nn(vtr[b, :, rows], probs[s, rows, cols])
            if s == 0:
                acc[:, cols] = part
            else:
                acc[:, cols] = acc[:, cols] * fade + part
            for piece in pieces:
                dprob[s, piece, cols] = nn(kv[s, 1, piece], gt[:, cols])

    def take_z(s):
        for j in range(2):
            for k in range(NSUB):
                @pl.when(c >= s)
                def _():
                    zc[s, j, k].wait_recv()

                @pl.when(c < s)
                def _():
                    kv[s, j, sub_rows[k]] = jnp.zeros((SUB, HD), BF)

                if s < REACH:
                    zc[s + 1, j, k] = send(kv.at[s, j, sub_rows[k]], kv.at[s + 1, j, sub_rows[k]], z_next,
                                           (c >= s) & (c < n_ctx - 1))
            piece = kv.at[s, j, my_rows]
            xc[s, j] = send(piece, piece, x_peer)
            if s == REACH:
                dc[s, j] = send(piece, piece, x_diag)
                cc[s, j] = send(piece, piece, c_peer)

    def take_x(s):
        for j in range(2):
            xc[s, j].wait_recv()
            if s < REACH:
                cc[s, j] = send(kv.at[s, j, half_rows], kv.at[s, j, half_rows], c_peer)

    def take_c(s):
        for j in range(2):
            cc[s, j].wait_recv()
            if s == REACH:
                dc[s, j].wait_recv()

    take_z(1)
    for s in range(1, REACH + 1):
        if s < REACH:
            take_z(s + 1)
            take_x(s)
        if s > 1:
            take_c(s - 1)
        forward(s - 1)
    take_x(REACH)
    take_c(REACH)
    forward(REACH)

    inv, delta = [], []
    for i in range(nch):
        inv.append(1.0 / acc[HD:HD + 1, i * CH:(i + 1) * CH])

    def finish():
        for i in range(nch):
            lo = i * CH
            out = (acc[:HD, lo:lo + CH] * inv[i]).astype(BF)
            ot[:, lo:lo + CH] = out
            delta.append(jnp.sum(gt[:, lo:lo + CH].astype(F32) * out.astype(F32), axis=0, keepdims=True))

    bc, bx, bz = {}, {}, {}
    far_x = pl.ds(pl.multiple_of(core * 256 + (1 - xl) * QUART, QUART), QUART)
    far_c = pl.ds(pl.multiple_of((1 - core) * 256 + xl * QUART, QUART), QUART)
    far_d = pl.ds(pl.multiple_of((1 - core) * 256 + (1 - xl) * QUART, QUART), QUART)

    def give(s, j):
        if s in STRAIGHT:
            bx[s, j] = [send(term.at[s, j, rows], dbuf.at[s - STRAIGHT[0], j, i], dev)
                        for i, (rows, dev) in enumerate(((far_x, x_peer), (far_d, x_diag), (far_c, c_peer)))]
        else:
            bc[s, j] = send(term.at[s, j, peer_half], cbuf.at[s, j], c_peer)

    def backward(s):
        b = s % 2
        fac = [jnp.exp2((m_at[s, i] - m_run[i]) * EXPC) * inv[i] for i in range(nch)]
        for i in range(nch):
            lo = i * CH
            gs[b, :, lo:lo + CH] = (gt[:, lo:lo + CH].astype(F32) * fac[i]).astype(BF)
            qs[b, :, lo:lo + CH] = (qt[:HD, lo:lo + CH].astype(F32) * (fac[i] * SCALE)).astype(BF)
        term[s, 1] = nt(probs[s], gs[b]).astype(BF)
        give(s, 1)
        if s == REACH:
            finish()
        for i in range(nch):
            lo = i * CH
            rows = live_rows(s, lo % BLK)
            cols = slice(lo, lo + CH)
            for r in range(rows.start, rows.stop, RB):
                piece = slice(r, r + RB)
                ds[b, piece, cols] = (probs[s, piece, cols].astype(F32) * (dprob[s, piece, cols] - delta[i])).astype(BF)
            blank(ds.at[b], rows, lo)
            part = nn(kvt[s, 0, :, rows], ds[b, rows, cols]) * fac[i]
            if s == REACH:
                dqt[:, lo:lo + CH] = part
            else:
                dqt[:, lo:lo + CH] = dqt[:, lo:lo + CH] + part
        term[s, 0] = nt(ds[b], qs[b]).astype(BF)
        give(s, 0)

    mine = pl.ds(pl.multiple_of(xl * QUART, QUART), QUART)
    other = pl.ds(pl.multiple_of((1 - xl) * QUART, QUART), QUART)
    other_rows = pl.ds(pl.multiple_of(core * 256 + (1 - xl) * QUART, QUART), QUART)

    def fold_c(s):
        for j in (1, 0):
            bc[s, j].wait_recv()
            xsend[s, j] = (term[s, j, other_rows].astype(F32) + cbuf[s, j, other].astype(F32)).astype(BF)
            bx[s, j] = send(xsend.at[s, j], xbuf.at[s, j], x_peer)
            hold[s, j] = term[s, j, my_rows].astype(F32) + cbuf[s, j, mine].astype(F32)


    def fold_x(s):
        for j in (1, 0):
            if s in STRAIGHT:
                for cp in bx[s, j]:
                    cp.wait_recv()
            else:
                bx[s, j].wait_recv()
            for k in range(NSUB):
                rows = slice(k * SUB, (k + 1) * SUB)
                if s in STRAIGHT:
                    near = dbuf.at[s - STRAIGHT[0], j]
                    total = term[s, j, sub_rows[k]].astype(F32) + near[0, rows].astype(F32)
                    total = total + near[1, rows].astype(F32) + near[2, rows].astype(F32)
                else:
                    total = hold[s, j, rows] + xbuf[s, j, rows].astype(F32)
                if s < REACH:
                    @pl.when((c >= s) & (c < n_ctx - 1))
                    def _():
                        bz[s + 1, j, k].wait_recv()

                    @pl.when((c < s) | (c == n_ctx - 1))
                    def _():
                        zbuf[s, j, rows] = jnp.zeros((SUB, HD), BF)

                    total = total + zbuf[s, j, rows].astype(F32)
                if s > 0:
                    zsend[s, j, rows] = total.astype(BF)
                    bz[s, j, k] = send(zsend.at[s, j, rows], zbuf.at[s - 1, j, rows], z_prev, c >= s)
                else:
                    kvg_ref[j, y, sub_rows[k]] = total.astype(BF)
            if s == 0:
                spread(j)

    ax, aup, adn, xup, xdn = {}, {}, {}, {}, {}

    def spread(j):
        piece = kvg_ref.at[j, y, my_rows]
        ax[j] = send(piece, piece, x_peer)
        aup[j] = send(piece, piece, y_next)
        adn[j] = send(piece, piece, y_prev)

    backward(4)
    backward(3)
    backward(2)
    fold_x(4)
    backward(1)
    fold_c(2)
    backward(0)
    fold_x(3)
    fold_c(1)
    fold_c(0)
    for h in range(2):
        o_ref[:, h * HD:(h + 1) * HD] = ot[:, h * BLK:(h + 1) * BLK].T
    fold_x(2)
    for h in range(2):
        dq_ref[:, h * HD:(h + 1) * HD] = (dqt[:, h * BLK:(h + 1) * BLK] * SCALE).astype(BF).T
    fold_x(1)
    fold_x(0)

    below = (y + 3) % 4
    above = (y + 1) % 4

    def hrow(which, k):
        return pl.ds(pl.multiple_of(core * 256 + which * QUART + k * 64, 64), 64)

    fin = []

    def relay(j, which):
        up = kvg_ref.at[j, below, hrow(which, 0)]
        dn = kvg_ref.at[j, above, hrow(which, 1)]
        fin.append(send(up, up, y_next))
        fin.append(send(dn, dn, y_prev))
        fin.append(send(up, up, y_next_o))
        fin.append(send(dn, dn, y_prev_o))

    for j in (1, 0):
        ax[j].wait_recv()
        piece = kvg_ref.at[j, y, other_rows]
        xup[j] = send(piece, piece, y_next)
        xdn[j] = send(piece, piece, y_prev)
        piece = kvg_ref.at[j, y, half_rows]
        fin.append(send(piece, piece, c_peer))
    for j in (1, 0):
        aup[j].wait_recv()
        adn[j].wait_recv()
        relay(j, xl)
    for j in (1, 0):
        xup[j].wait_recv()
        xdn[j].wait_recv()
        relay(j, 1 - xl)
        for cols in (below, above):
            piece = kvg_ref.at[j, cols, half_rows]
            fin.append(send(piece, piece, c_peer))
    for cp in fin:
        cp.wait_recv()
    for cp, ok in sent:
        only(ok, lambda: cp.wait_send())
    assert len(sent) == N_SEND, len(sent)


def place_outputs(o_raw, dq_raw, kvg_raw, o_out, dq_out, dk_out, dv_out, o_v, dq_v, kvg_v, isem, osem):
    fetch = [pltpu.make_async_copy(o_raw, o_v, isem.at[0]), pltpu.make_async_copy(dq_raw, dq_v, isem.at[1])]
    store = [pltpu.make_async_copy(o_v, o_out, osem.at[0]), pltpu.make_async_copy(dq_v, dq_out, osem.at[1])]
    for j, out in enumerate((dk_out, dv_out)):
        for g in range(KVH):
            i = len(fetch)
            fetch.append(pltpu.make_async_copy(kvg_raw.at[j, g], kvg_v.at[j, g], isem.at[i]))
            store.append(pltpu.make_async_copy(kvg_v.at[j, g], out.at[:, g * HD:(g + 1) * HD], osem.at[i]))
    for cp in fetch:
        cp.start()
    for get, put in zip(fetch, store):
        get.wait()
        put.start()
    for cp in store:
        cp.wait()


N_SEND = 106


def solution(mesh):
    n_ctx = mesh.shape["ctx"]

    def per_device(queries, keys, values, out_grad, doc_lengths):
        steps = REACH + 1
        vm = pl.BlockSpec(memory_space=pltpu.VMEM)
        hbm = pl.BlockSpec(memory_space=pl.ANY)
        shapes = tuple(jax.ShapeDtypeStruct(a.shape, BF) for a in (queries, queries, keys, values))
        raw = pl.pallas_call(
            functools.partial(kernel, n_ctx, doc_lengths.shape[0]),
            out_shape=shapes[:2] + (jax.ShapeDtypeStruct((2, KVH, BLK, HD), BF),),
            in_specs=[hbm, hbm, hbm, hbm, pl.BlockSpec(memory_space=pltpu.SMEM)],
            out_specs=(vm, vm, vm),
            scratch_shapes=[
                pltpu.VMEM((BLK, 256), BF),
                pltpu.VMEM((BLK, 256), BF),
                pltpu.VMEM((steps, 2, BLK, HD), BF),
                pltpu.VMEM((2 * HD, QN), BF),
                pltpu.VMEM((HD, QN), BF),
                pltpu.VMEM((steps, 1, HD, BLK), BF),
                pltpu.VMEM((2, HD + 8, BLK), BF),
                pltpu.VMEM((2, BLK, 2 * HD), BF),
                pltpu.VMEM((2, BLK, CH), F32),
                pltpu.VMEM((steps, BLK, QN), BF),
                pltpu.VMEM((steps, BLK, QN), F32),
                pltpu.VMEM((HD + 8, QN), F32),
                pltpu.VMEM((HD, QN), BF),
                pltpu.VMEM((HD, QN), F32),
                pltpu.VMEM((2, HD, QN), BF),
                pltpu.VMEM((2, HD, QN), BF),
                pltpu.VMEM((2, BLK, QN), BF),
                pltpu.VMEM((steps, 2, BLK, HD), BF),
                pltpu.VMEM((steps, 2, 256, HD), BF),
                pltpu.VMEM((len(STRAIGHT), 2, 3, QUART, HD), BF),
                pltpu.VMEM((steps, 2, QUART, HD), F32),
                pltpu.VMEM((steps, 2, QUART, HD), BF),
                pltpu.VMEM((steps, 2, QUART, HD), BF),
                pltpu.VMEM((REACH, 2, QUART, HD), BF),
                pltpu.VMEM((steps, 2, QUART, HD), BF),
                pltpu.SemaphoreType.DMA((4,)),
                pltpu.SemaphoreType.DMA((N_SEND,)),
                pltpu.SemaphoreType.DMA((N_SEND,)),
            ],
            compiler_params=pltpu.CompilerParams(
                collective_id=0, has_side_effects=True, vmem_limit_bytes=60 * 1024 * 1024
            ),
        )(queries, keys, values, out_grad, doc_lengths)
        return pl.pallas_call(
            place_outputs,
            out_shape=shapes,
            in_specs=[hbm] * 3,
            out_specs=(hbm,) * 4,
            scratch_shapes=[
                pltpu.VMEM((BLK, 256), BF),
                pltpu.VMEM((BLK, 256), BF),
                pltpu.VMEM((2, KVH, BLK, HD), BF),
                pltpu.SemaphoreType.DMA((10,)),
                pltpu.SemaphoreType.DMA((10,)),
            ],
            compiler_params=pltpu.CompilerParams(vmem_limit_bytes=62 * 1024 * 1024),
        )(*raw)

    return jax.shard_map(
        per_device,
        mesh=mesh,
        in_specs=(P("ctx", "tp"), P("ctx", None), P("ctx", None), P("ctx", "tp"), P()),
        out_specs=(P("ctx", "tp"), P("ctx", "tp"), P("ctx", None), P("ctx", None)),
        check_vma=False,
    )
```

```python
import functools
import math

import jax
import jax.numpy as jnp
from jax import lax
from jax.experimental import pallas as pl
from jax.experimental.pallas import tpu as pltpu
from jax.sharding import PartitionSpec as P

MESH = pl.DeviceIdType.MESH
HD = 128
KVH = 4
REACH = 4
BLK = 512
QN = 1024
CH = 256
RB = 128
QUART = 128
NSUB = 2
SUB = QUART // NSUB
STRAIGHT = (3, 4)
NEG = -1e30
FLOOR = -1e9
SCALE = 1.0 / math.sqrt(HD)
EXPC = SCALE * math.log2(math.e)
F32 = jnp.float32
BF = jnp.bfloat16


def nt(a, b):
    return lax.dot_general(a, b, (((1,), (1,)), ((), ())), preferred_element_type=F32)


def nn(a, b):
    return jnp.dot(a, b, preferred_element_type=F32)


def kernel(n_ctx, ndoc, q_hbm, k_hbm, v_hbm, g_hbm, len_ref, o_ref, dq_ref, kvg_ref,
           q_in, g_in, kv, qt, gt, kvt, vtr, kx, sbuf, probs, dprob, acc, ot, dqt, gs, qs, ds,
           term, cbuf, dbuf, hold, xsend, xbuf, zbuf, zsend, stage, o_v, dq_v, ksem, lsem, ssem, rsem):
    c = lax.axis_index("ctx")
    t = lax.axis_index("tp")
    half_ctx = n_ctx // 2
    y, xlo, core = t // 4, (t // 2) % 2, t % 2
    xhi = c // half_ctx
    xl = xlo + xhi - 2 * xlo * xhi

    def place(ctx, yy, xx, cc):
        hi = ctx // half_ctx
        lo = xx + hi - 2 * xx * hi
        return (ctx, yy * 4 + lo * 2 + cc)

    z_next = place((c + 1) % n_ctx, y, xl, core)
    z_prev = place((c + n_ctx - 1) % n_ctx, y, xl, core)
    x_peer = place(c, y, 1 - xl, core)
    c_peer = place(c, y, xl, 1 - core)
    y_next = place(c, (y + 1) % 4, xl, core)
    y_prev = place(c, (y + 3) % 4, xl, core)
    x_diag = place(c, y, 1 - xl, 1 - core)
    y_next_o = place(c, (y + 1) % 4, xl, 1 - core)
    y_prev_o = place(c, (y + 3) % 4, xl, 1 - core)

    col = pl.ds(pl.multiple_of(y * HD, HD), HD)
    my_half = pl.multiple_of(core * 256, 256)
    my_rows = pl.ds(pl.multiple_of(core * 256 + xl * QUART, QUART), QUART)
    sub_rows = [pl.ds(pl.multiple_of(core * 256 + xl * QUART + k * SUB, SUB), SUB) for k in range(NSUB)]
    half_rows = pl.ds(my_half, 256)
    peer_half = pl.ds(pl.multiple_of((1 - core) * 256, 256), 256)

    loads = [
        pltpu.make_async_copy(q_hbm, q_in, lsem.at[0]),
        pltpu.make_async_copy(g_hbm, g_in, lsem.at[1]),
        pltpu.make_async_copy(k_hbm.at[:, col], kv.at[0, 0], lsem.at[2]),
        pltpu.make_async_copy(v_hbm.at[:, col], kv.at[0, 1], lsem.at[3]),
    ]
    for cp in loads:
        cp.start()

    barrier = pltpu.get_barrier_semaphore()
    peers = (x_peer, c_peer, y_next, y_prev, x_diag, y_next_o, y_prev_o)
    for dev, ok in ((z_next, c < n_ctx - 1), (z_prev, c > 0)):
        @pl.when(ok)
        def _(dev=dev):
            pl.semaphore_signal(barrier, inc=1, device_id=dev, device_id_type=MESH)

    for dev in peers:
        pl.semaphore_signal(barrier, inc=1, device_id=dev, device_id_type=MESH)
    for cp in loads[2:]:
        cp.wait()
    pl.semaphore_wait(barrier, len(peers) + jnp.minimum(c, 1) + jnp.minimum(n_ctx - 1 - c, 1))

    sent = []

    def only(ok, act):
        if ok is None:
            act()
        else:
            pl.when(ok)(act)

    def send(src, dst, dev, ok=None):
        i = len(sent)
        cp = pltpu.make_async_remote_copy(src_ref=src, dst_ref=dst, send_sem=ssem.at[i], recv_sem=rsem.at[i],
                                          device_id=dev, device_id_type=MESH)
        only(ok, lambda: cp.start())
        sent.append((cp, ok))
        return cp

    settled = [0]

    def settle(upto):
        for cp, ok in sent[settled[0]:upto]:
            only(ok, lambda: cp.wait_send())
        settled[0] = upto

    zc, xc, cc, dc = {}, {}, {}, {}
    for j in range(2):
        for k in range(NSUB):
            zc[1, j, k] = send(kv.at[0, j, sub_rows[k]], kv.at[1, j, sub_rows[k]], z_next, c < n_ctx - 1)

    lane = lax.broadcasted_iota(jnp.int32, (1, BLK), 1)
    dlane = lax.broadcasted_iota(jnp.int32, (1, HD), 1)
    drow = lax.broadcasted_iota(jnp.int32, (HD, 1), 0)
    lo_l, hi_l = jnp.zeros((1, HD), jnp.int32), jnp.zeros((1, HD), jnp.int32)
    lo_r, hi_r = jnp.zeros((HD, 1), jnp.int32), jnp.zeros((HD, 1), jnp.int32)
    end = jnp.int32(0)
    for d in range(ndoc):
        lo_l, lo_r = jnp.where(dlane == d, end, lo_l), jnp.where(drow == d, end, lo_r)
        end = end + len_ref[d]
        hi_l, hi_r = jnp.where(dlane == d, end, hi_l), jnp.where(drow == d, end, hi_r)
    lo_l = jnp.where(dlane == ndoc, -(1 << 30), lo_l)
    pos = lane + c * BLK
    block_doc = jnp.where((pos >= lo_r) & (pos < hi_r), 0.0, NEG).astype(BF)
    kpos0 = lax.broadcasted_iota(jnp.int32, (BLK, HD), 0) + c * BLK
    krow = lax.broadcasted_iota(jnp.int32, (RB, CH), 0)
    for b in range(2):
        vtr[b, HD:] = jnp.ones((8, BLK), BF)

    for cp in loads[:2]:
        cp.wait()
    for h in range(2):
        qt[:HD, h * BLK:(h + 1) * BLK] = q_in[:, h * HD:(h + 1) * HD].T
        qt[HD:, h * BLK:(h + 1) * BLK] = block_doc
        gt[:, h * BLK:(h + 1) * BLK] = g_in[:, h * HD:(h + 1) * HD].T

    nch = QN // CH
    m_run = [jnp.full((1, CH), FLOOR, F32)] * nch
    m_at = {}

    def live_rows(s, off):
        if s == 0 and off + CH <= BLK // 2:
            return slice(0, BLK // 2)
        if s == REACH and off >= BLK // 2:
            return slice(BLK // 2, BLK)
        return slice(0, BLK)

    def blank(ref, rows, lo):
        if rows.stop - rows.start < BLK:
            skipped = slice(BLK // 2, BLK) if rows.start == 0 else slice(0, BLK // 2)
            ref[skipped, lo:lo + CH] = jnp.zeros((BLK // 2, CH), BF)

    def forward(s):
        b = s % 2
        kvt[s, 0] = kv[s, 0].T
        vtr[b, :HD] = kv[s, 1].T
        kx[b, :, :HD] = kv[s, 0]
        kpos = kpos0 - s * BLK
        kx[b, :, HD:] = jnp.where((kpos >= lo_l) & (kpos < hi_l), 1.0, 0.0).astype(BF)
        for i in range(nch):
            lo = i * CH
            off = (i * CH) % BLK
            cols = slice(lo, lo + CH)
            rows = live_rows(s, off)
            pieces = [slice(r, r + RB) for r in range(rows.start, rows.stop, RB)]
            top = m_run[i]
            for piece in pieces:
                sc = nn(kx[b, piece], qt[:, cols])
                if s == 0 and piece.stop > off:
                    sc = jnp.where(krow + piece.start <= lane[:, off:off + CH], sc, NEG)
                sbuf[i % 2, piece] = sc
                top = jnp.maximum(top, jnp.max(sc, axis=0, keepdims=True))
            scaled = top * EXPC
            for piece in pieces:
                probs[s, piece, cols] = jnp.exp2(sbuf[i % 2, piece] * EXPC - scaled).astype(BF)
            fade = jnp.exp2((m_run[i] - top) * EXPC)
            m_run[i] = top
            m_at[s, i] = top
            blank(probs.at[s], rows, lo)
            part = nn(vtr[b, :, rows], probs[s, rows, cols])
            if s == 0:
                acc[:, cols] = part
            else:
                acc[:, cols] = acc[:, cols] * fade + part
            for piece in pieces:
                dprob[s, piece, cols] = nn(kv[s, 1, piece], gt[:, cols])

    def take_z(s):
        for j in range(2):
            for k in range(NSUB):
                @pl.when(c >= s)
                def _():
                    zc[s, j, k].wait_recv()

                @pl.when(c < s)
                def _():
                    kv[s, j, sub_rows[k]] = jnp.zeros((SUB, HD), BF)

                if s < REACH:
                    zc[s + 1, j, k] = send(kv.at[s, j, sub_rows[k]], kv.at[s + 1, j, sub_rows[k]], z_next,
                                           (c >= s) & (c < n_ctx - 1))
            piece = kv.at[s, j, my_rows]
            xc[s, j] = send(piece, piece, x_peer)
            if s == REACH:
                dc[s, j] = send(piece, piece, x_diag)
                cc[s, j] = send(piece, piece, c_peer)

    def take_x(s):
        for j in range(2):
            xc[s, j].wait_recv()
            if s < REACH:
                cc[s, j] = send(kv.at[s, j, half_rows], kv.at[s, j, half_rows], c_peer)

    def take_c(s):
        for j in range(2):
            cc[s, j].wait_recv()
            if s == REACH:
                dc[s, j].wait_recv()

    take_z(1)
    for s in range(1, REACH + 1):
        if s < REACH:
            take_z(s + 1)
            take_x(s)
        if s > 1:
            take_c(s - 1)
        forward(s - 1)
    take_x(REACH)
    take_c(REACH)
    forward(REACH)

    inv, delta = [], []
    for i in range(nch):
        inv.append(1.0 / acc[HD:HD + 1, i * CH:(i + 1) * CH])

    def finish():
        for i in range(nch):
            lo = i * CH
            out = (acc[:HD, lo:lo + CH] * inv[i]).astype(BF)
            ot[:, lo:lo + CH] = out
            delta.append(jnp.sum(gt[:, lo:lo + CH].astype(F32) * out.astype(F32), axis=0, keepdims=True))

    bc, bx, bz = {}, {}, {}
    far_x = pl.ds(pl.multiple_of(core * 256 + (1 - xl) * QUART, QUART), QUART)
    far_c = pl.ds(pl.multiple_of((1 - core) * 256 + xl * QUART, QUART), QUART)
    far_d = pl.ds(pl.multiple_of((1 - core) * 256 + (1 - xl) * QUART, QUART), QUART)

    def give(s, j):
        if s in STRAIGHT:
            bx[s, j] = [send(term.at[s, j, rows], dbuf.at[s - STRAIGHT[0], j, i], dev)
                        for i, (rows, dev) in enumerate(((far_x, x_peer), (far_d, x_diag), (far_c, c_peer)))]
        else:
            bc[s, j] = send(term.at[s, j, peer_half], cbuf.at[s, j], c_peer)

    def backward(s):
        b = s % 2
        fac = [jnp.exp2((m_at[s, i] - m_run[i]) * EXPC) * inv[i] for i in range(nch)]
        for i in range(nch):
            lo = i * CH
            gs[b, :, lo:lo + CH] = (gt[:, lo:lo + CH].astype(F32) * fac[i]).astype(BF)
            qs[b, :, lo:lo + CH] = (qt[:HD, lo:lo + CH].astype(F32) * (fac[i] * SCALE)).astype(BF)
        term[s, 1] = nt(probs[s], gs[b]).astype(BF)
        give(s, 1)
        if s == REACH:
            finish()
        for i in range(nch):
            lo = i * CH
            rows = live_rows(s, lo % BLK)
            cols = slice(lo, lo + CH)
            for r in range(rows.start, rows.stop, RB):
                piece = slice(r, r + RB)
                ds[b, piece, cols] = (probs[s, piece, cols].astype(F32) * (dprob[s, piece, cols] - delta[i])).astype(BF)
            blank(ds.at[b], rows, lo)
            part = nn(kvt[s, 0, :, rows], ds[b, rows, cols]) * fac[i]
            if s == REACH:
                dqt[:, lo:lo + CH] = part
            else:
                dqt[:, lo:lo + CH] = dqt[:, lo:lo + CH] + part
        term[s, 0] = nt(ds[b], qs[b]).astype(BF)
        give(s, 0)

    mine = pl.ds(pl.multiple_of(xl * QUART, QUART), QUART)
    other = pl.ds(pl.multiple_of((1 - xl) * QUART, QUART), QUART)
    other_rows = pl.ds(pl.multiple_of(core * 256 + (1 - xl) * QUART, QUART), QUART)

    def fold_c(s):
        for j in (1, 0):
            bc[s, j].wait_recv()
            xsend[s, j] = (term[s, j, other_rows].astype(F32) + cbuf[s, j, other].astype(F32)).astype(BF)
            bx[s, j] = send(xsend.at[s, j], xbuf.at[s, j], x_peer)
            hold[s, j] = term[s, j, my_rows].astype(F32) + cbuf[s, j, mine].astype(F32)


    def fold_x(s):
        for j in (1, 0):
            if s in STRAIGHT:
                for cp in bx[s, j]:
                    cp.wait_recv()
            else:
                bx[s, j].wait_recv()
            for k in range(NSUB):
                rows = slice(k * SUB, (k + 1) * SUB)
                if s in STRAIGHT:
                    near = dbuf.at[s - STRAIGHT[0], j]
                    total = term[s, j, sub_rows[k]].astype(F32) + near[0, rows].astype(F32)
                    total = total + near[1, rows].astype(F32) + near[2, rows].astype(F32)
                else:
                    total = hold[s, j, rows] + xbuf[s, j, rows].astype(F32)
                if s < REACH:
                    @pl.when((c >= s) & (c < n_ctx - 1))
                    def _():
                        bz[s + 1, j, k].wait_recv()

                    @pl.when((c < s) | (c == n_ctx - 1))
                    def _():
                        zbuf[s, j, rows] = jnp.zeros((SUB, HD), BF)

                    total = total + zbuf[s, j, rows].astype(F32)
                if s > 0:
                    zsend[s, j, rows] = total.astype(BF)
                    bz[s, j, k] = send(zsend.at[s, j, rows], zbuf.at[s - 1, j, rows], z_prev, c >= s)
                else:
                    stage[j, y, sub_rows[k]] = total.astype(BF)
            if s == 0:
                spread(j)

    ax, aup, adn, xup, xdn = {}, {}, {}, {}, {}

    def spread(j):
        piece = stage.at[j, y, my_rows]
        ax[j] = send(piece, piece, x_peer)
        aup[j] = send(piece, piece, y_next)
        adn[j] = send(piece, piece, y_prev)

    kept = []

    def keep(src, dst):
        cp = pltpu.make_async_copy(src, dst, ksem.at[len(kept)])
        cp.start()
        kept.append(cp)

    first_part = len(sent)
    backward(4)
    backward(3)
    backward(2)
    settle(first_part)
    fold_x(4)
    backward(1)
    fold_c(2)
    backward(0)
    fold_x(3)
    fold_c(1)
    fold_c(0)
    for h in range(2):
        o_v[:, h * HD:(h + 1) * HD] = ot[:, h * BLK:(h + 1) * BLK].T
    keep(o_v, o_ref)
    fold_x(2)
    for h in range(2):
        dq_v[:, h * HD:(h + 1) * HD] = (dqt[:, h * BLK:(h + 1) * BLK] * SCALE).astype(BF).T
    keep(dq_v, dq_ref)
    second_part = len(sent)
    fold_x(1)
    settle(second_part)
    fold_x(0)

    below = (y + 3) % 4
    above = (y + 1) % 4

    def hrow(which, k):
        return pl.ds(pl.multiple_of(core * 256 + which * QUART + k * 64, 64), 64)

    fin = []

    def relay(j, which):
        up = stage.at[j, below, hrow(which, 0)]
        dn = stage.at[j, above, hrow(which, 1)]
        up_out = kvg_ref.at[j, below, hrow(which, 0)]
        dn_out = kvg_ref.at[j, above, hrow(which, 1)]
        fin.append(send(up, up_out, y_next))
        fin.append(send(dn, dn_out, y_prev))
        fin.append(send(up, up_out, y_next_o))
        fin.append(send(dn, dn_out, y_prev_o))

    def share(j, g):
        piece, out = stage.at[j, g, half_rows], kvg_ref.at[j, g, half_rows]
        fin.append(send(piece, out, c_peer))
        keep(piece, out)

    for j in (1, 0):
        ax[j].wait_recv()
        piece = stage.at[j, y, other_rows]
        xup[j] = send(piece, piece, y_next)
        xdn[j] = send(piece, piece, y_prev)
        share(j, y)
    for j in (1, 0):
        aup[j].wait_recv()
        adn[j].wait_recv()
        relay(j, xl)
    for j in (1, 0):
        xup[j].wait_recv()
        xdn[j].wait_recv()
        relay(j, 1 - xl)
        for cols in (below, above):
            share(j, cols)
    for cp in fin:
        cp.wait_recv()
    settle(len(sent))
    for cp in kept:
        cp.wait()
    assert len(sent) == N_SEND, len(sent)


def place_outputs(o_raw, dq_raw, kvg_raw, o_out, dq_out, dk_out, dv_out, o_v, dq_v, kvg_v, isem, osem):
    fetch = [pltpu.make_async_copy(o_raw, o_v, isem.at[0]), pltpu.make_async_copy(dq_raw, dq_v, isem.at[1])]
    store = [pltpu.make_async_copy(o_v, o_out, osem.at[0]), pltpu.make_async_copy(dq_v, dq_out, osem.at[1])]
    for j, out in enumerate((dk_out, dv_out)):
        for g in range(KVH):
            i = len(fetch)
            fetch.append(pltpu.make_async_copy(kvg_raw.at[j, g], kvg_v.at[j, g], isem.at[i]))
            store.append(pltpu.make_async_copy(kvg_v.at[j, g], out.at[:, g * HD:(g + 1) * HD], osem.at[i]))
    for cp in fetch:
        cp.start()
    for get, put in zip(fetch, store):
        get.wait()
        put.start()
    for cp in store:
        cp.wait()


N_SEND = 106


def solution(mesh):
    n_ctx = mesh.shape["ctx"]

    def per_device(queries, keys, values, out_grad, doc_lengths):
        steps = REACH + 1
        hbm = pl.BlockSpec(memory_space=pl.ANY)
        shapes = tuple(jax.ShapeDtypeStruct(a.shape, BF) for a in (queries, queries, keys, values))
        raw = pl.pallas_call(
            functools.partial(kernel, n_ctx, doc_lengths.shape[0]),
            out_shape=shapes[:2] + (jax.ShapeDtypeStruct((2, KVH, BLK, HD), BF),),
            in_specs=[hbm, hbm, hbm, hbm, pl.BlockSpec(memory_space=pltpu.SMEM)],
            out_specs=(hbm, hbm, hbm),
            scratch_shapes=[
                pltpu.VMEM((BLK, 256), BF),
                pltpu.VMEM((BLK, 256), BF),
                pltpu.VMEM((steps, 2, BLK, HD), BF),
                pltpu.VMEM((2 * HD, QN), BF),
                pltpu.VMEM((HD, QN), BF),
                pltpu.VMEM((steps, 1, HD, BLK), BF),
                pltpu.VMEM((2, HD + 8, BLK), BF),
                pltpu.VMEM((2, BLK, 2 * HD), BF),
                pltpu.VMEM((2, BLK, CH), F32),
                pltpu.VMEM((steps, BLK, QN), BF),
                pltpu.VMEM((steps, BLK, QN), F32),
                pltpu.VMEM((HD + 8, QN), F32),
                pltpu.VMEM((HD, QN), BF),
                pltpu.VMEM((HD, QN), F32),
                pltpu.VMEM((2, HD, QN), BF),
                pltpu.VMEM((2, HD, QN), BF),
                pltpu.VMEM((2, BLK, QN), BF),
                pltpu.VMEM((steps, 2, BLK, HD), BF),
                pltpu.VMEM((steps, 2, 256, HD), BF),
                pltpu.VMEM((len(STRAIGHT), 2, 3, QUART, HD), BF),
                pltpu.VMEM((steps, 2, QUART, HD), F32),
                pltpu.VMEM((steps, 2, QUART, HD), BF),
                pltpu.VMEM((steps, 2, QUART, HD), BF),
                pltpu.VMEM((REACH, 2, QUART, HD), BF),
                pltpu.VMEM((steps, 2, QUART, HD), BF),
                pltpu.VMEM((2, KVH, BLK, HD), BF),
                pltpu.VMEM((BLK, 256), BF),
                pltpu.VMEM((BLK, 256), BF),
                pltpu.SemaphoreType.DMA((8,)),
                pltpu.SemaphoreType.DMA((4,)),
                pltpu.SemaphoreType.DMA((N_SEND,)),
                pltpu.SemaphoreType.DMA((N_SEND,)),
            ],
            compiler_params=pltpu.CompilerParams(
                collective_id=0, has_side_effects=True, vmem_limit_bytes=60 * 1024 * 1024
            ),
        )(queries, keys, values, out_grad, doc_lengths)
        return pl.pallas_call(
            place_outputs,
            out_shape=shapes,
            in_specs=[hbm] * 3,
            out_specs=(hbm,) * 4,
            scratch_shapes=[
                pltpu.VMEM((BLK, 256), BF),
                pltpu.VMEM((BLK, 256), BF),
                pltpu.VMEM((2, KVH, BLK, HD), BF),
                pltpu.SemaphoreType.DMA((10,)),
                pltpu.SemaphoreType.DMA((10,)),
            ],
            compiler_params=pltpu.CompilerParams(vmem_limit_bytes=62 * 1024 * 1024),
        )(*raw)

    return jax.shard_map(
        per_device,
        mesh=mesh,
        in_specs=(P("ctx", "tp"), P("ctx", None), P("ctx", None), P("ctx", "tp"), P()),
        out_specs=(P("ctx", "tp"), P("ctx", "tp"), P("ctx", None), P("ctx", None)),
        check_vma=False,
    )
```

```python
import functools
import math

import jax
import jax.numpy as jnp
from jax import lax
from jax.experimental import pallas as pl
from jax.experimental.pallas import tpu as pltpu
from jax.sharding import PartitionSpec as P

MESH = pl.DeviceIdType.MESH
HD = 128
KVH = 4
REACH = 4
BLK = 512
QN = 1024
CH = 256
RB = 128
QUART = 128
NSUB = 1
SUB = QUART // NSUB
STRAIGHT = (3, 4)
NEG = -1e30
FLOOR = -1e9
SCALE = 1.0 / math.sqrt(HD)
EXPC = SCALE * math.log2(math.e)
F32 = jnp.float32
BF = jnp.bfloat16


def nt(a, b):
    return lax.dot_general(a, b, (((1,), (1,)), ((), ())), preferred_element_type=F32)


def nn(a, b):
    return jnp.dot(a, b, preferred_element_type=F32)


def kernel(n_ctx, ndoc, q_hbm, k_hbm, v_hbm, g_hbm, len_ref, o_ref, dq_ref, kvg_ref,
           q_in, g_in, kv, qt, gt, kvt, vtr, kx, sbuf, probs, dprob, acc, ot, dqt, gs, qs, ds,
           term, cbuf, dbuf, hold, xsend, xbuf, zbuf, zsend, stage, o_v, dq_v, ksem, lsem, ssem, rsem):
    c = lax.axis_index("ctx")
    t = lax.axis_index("tp")
    half_ctx = n_ctx // 2
    y, xlo, core = t // 4, (t // 2) % 2, t % 2
    xhi = c // half_ctx
    xl = xlo + xhi - 2 * xlo * xhi

    def place(ctx, yy, xx, cc):
        hi = ctx // half_ctx
        lo = xx + hi - 2 * xx * hi
        return (ctx, yy * 4 + lo * 2 + cc)

    z_next = place((c + 1) % n_ctx, y, xl, core)
    z_prev = place((c + n_ctx - 1) % n_ctx, y, xl, core)
    x_peer = place(c, y, 1 - xl, core)
    c_peer = place(c, y, xl, 1 - core)
    y_next = place(c, (y + 1) % 4, xl, core)
    y_prev = place(c, (y + 3) % 4, xl, core)
    x_diag = place(c, y, 1 - xl, 1 - core)
    y_next_o = place(c, (y + 1) % 4, xl, 1 - core)
    y_prev_o = place(c, (y + 3) % 4, xl, 1 - core)

    col = pl.ds(pl.multiple_of(y * HD, HD), HD)
    my_half = pl.multiple_of(core * 256, 256)
    my_rows = pl.ds(pl.multiple_of(core * 256 + xl * QUART, QUART), QUART)
    sub_rows = [pl.ds(pl.multiple_of(core * 256 + xl * QUART + k * SUB, SUB), SUB) for k in range(NSUB)]
    half_rows = pl.ds(my_half, 256)
    peer_half = pl.ds(pl.multiple_of((1 - core) * 256, 256), 256)

    loads = [
        pltpu.make_async_copy(q_hbm, q_in, lsem.at[0]),
        pltpu.make_async_copy(g_hbm, g_in, lsem.at[1]),
        pltpu.make_async_copy(k_hbm.at[:, col], kv.at[0, 0], lsem.at[2]),
        pltpu.make_async_copy(v_hbm.at[:, col], kv.at[0, 1], lsem.at[3]),
    ]
    for cp in loads:
        cp.start()

    barrier = pltpu.get_barrier_semaphore()
    peers = (x_peer, c_peer, y_next, y_prev, x_diag, y_next_o, y_prev_o)
    for dev, ok in ((z_next, c < n_ctx - 1), (z_prev, c > 0)):
        @pl.when(ok)
        def _(dev=dev):
            pl.semaphore_signal(barrier, inc=1, device_id=dev, device_id_type=MESH)

    for dev in peers:
        pl.semaphore_signal(barrier, inc=1, device_id=dev, device_id_type=MESH)
    for cp in loads[2:]:
        cp.wait()
    pl.semaphore_wait(barrier, len(peers) + jnp.minimum(c, 1) + jnp.minimum(n_ctx - 1 - c, 1))

    sent = []

    def only(ok, act):
        if ok is None:
            act()
        else:
            pl.when(ok)(act)

    def send(src, dst, dev, ok=None):
        i = len(sent)
        cp = pltpu.make_async_remote_copy(src_ref=src, dst_ref=dst, send_sem=ssem.at[i], recv_sem=rsem.at[i],
                                          device_id=dev, device_id_type=MESH)
        only(ok, lambda: cp.start())
        sent.append((cp, ok))
        return cp

    settled = [0]

    def settle(upto):
        for cp, ok in sent[settled[0]:upto]:
            only(ok, lambda: cp.wait_send())
        settled[0] = upto

    zc, xc, cc, dc = {}, {}, {}, {}
    for j in range(2):
        for k in range(NSUB):
            zc[1, j, k] = send(kv.at[0, j, sub_rows[k]], kv.at[1, j, sub_rows[k]], z_next, c < n_ctx - 1)

    lane = lax.broadcasted_iota(jnp.int32, (1, BLK), 1)
    dlane = lax.broadcasted_iota(jnp.int32, (1, HD), 1)
    drow = lax.broadcasted_iota(jnp.int32, (HD, 1), 0)
    lo_l, hi_l = jnp.zeros((1, HD), jnp.int32), jnp.zeros((1, HD), jnp.int32)
    lo_r, hi_r = jnp.zeros((HD, 1), jnp.int32), jnp.zeros((HD, 1), jnp.int32)
    end = jnp.int32(0)
    for d in range(ndoc):
        lo_l, lo_r = jnp.where(dlane == d, end, lo_l), jnp.where(drow == d, end, lo_r)
        end = end + len_ref[d]
        hi_l, hi_r = jnp.where(dlane == d, end, hi_l), jnp.where(drow == d, end, hi_r)
    lo_l = jnp.where(dlane == ndoc, -(1 << 30), lo_l)
    pos = lane + c * BLK
    block_doc = jnp.where((pos >= lo_r) & (pos < hi_r), 0.0, NEG).astype(BF)
    kpos0 = lax.broadcasted_iota(jnp.int32, (BLK, HD), 0) + c * BLK
    krow = lax.broadcasted_iota(jnp.int32, (RB, CH), 0)
    for b in range(2):
        vtr[b, HD:] = jnp.ones((8, BLK), BF)

    for cp in loads[:2]:
        cp.wait()
    for h in range(2):
        qt[:HD, h * BLK:(h + 1) * BLK] = q_in[:, h * HD:(h + 1) * HD].T
        qt[HD:, h * BLK:(h + 1) * BLK] = block_doc
        gt[:, h * BLK:(h + 1) * BLK] = g_in[:, h * HD:(h + 1) * HD].T

    nch = QN // CH
    m_run = [jnp.full((1, CH), FLOOR, F32)] * nch
    m_at = {}

    def live_rows(s, off):
        if s == 0 and off + CH <= BLK // 2:
            return slice(0, BLK // 2)
        if s == REACH and off >= BLK // 2:
            return slice(BLK // 2, BLK)
        return slice(0, BLK)

    def blank(ref, rows, lo):
        if rows.stop - rows.start < BLK:
            skipped = slice(BLK // 2, BLK) if rows.start == 0 else slice(0, BLK // 2)
            ref[skipped, lo:lo + CH] = jnp.zeros((BLK // 2, CH), BF)

    def forward(s):
        b = s % 2
        kvt[s, 0] = kv[s, 0].T
        vtr[b, :HD] = kv[s, 1].T
        kx[b, :, :HD] = kv[s, 0]
        kpos = kpos0 - s * BLK
        kx[b, :, HD:] = jnp.where((kpos >= lo_l) & (kpos < hi_l), 1.0, 0.0).astype(BF)
        for i in range(nch):
            lo = i * CH
            off = (i * CH) % BLK
            cols = slice(lo, lo + CH)
            rows = live_rows(s, off)
            pieces = [slice(r, r + RB) for r in range(rows.start, rows.stop, RB)]
            top = m_run[i]
            for piece in pieces:
                sc = nn(kx[b, piece], qt[:, cols])
                if s == 0 and piece.stop > off:
                    sc = jnp.where(krow + piece.start <= lane[:, off:off + CH], sc, NEG)
                sbuf[i % 2, piece] = sc
                top = jnp.maximum(top, jnp.max(sc, axis=0, keepdims=True))
            scaled = top * EXPC
            for piece in pieces:
                probs[s, piece, cols] = jnp.exp2(sbuf[i % 2, piece] * EXPC - scaled).astype(BF)
            fade = jnp.exp2((m_run[i] - top) * EXPC)
            m_run[i] = top
            m_at[s, i] = top
            blank(probs.at[s], rows, lo)
            part = nn(vtr[b, :, rows], probs[s, rows, cols])
            if s == 0:
                acc[:, cols] = part
            else:
                acc[:, cols] = acc[:, cols] * fade + part
            for piece in pieces:
                dprob[s, piece, cols] = nn(kv[s, 1, piece], gt[:, cols])

    def take_z(s):
        for j in range(2):
            for k in range(NSUB):
                @pl.when(c >= s)
                def _():
                    zc[s, j, k].wait_recv()

                @pl.when(c < s)
                def _():
                    kv[s, j, sub_rows[k]] = jnp.zeros((SUB, HD), BF)

                if s < REACH:
                    zc[s + 1, j, k] = send(kv.at[s, j, sub_rows[k]], kv.at[s + 1, j, sub_rows[k]], z_next,
                                           (c >= s) & (c < n_ctx - 1))
            piece = kv.at[s, j, my_rows]
            xc[s, j] = send(piece, piece, x_peer)
            if s == REACH:
                dc[s, j] = send(piece, piece, x_diag)
                cc[s, j] = send(piece, piece, c_peer)

    def take_x(s):
        for j in range(2):
            xc[s, j].wait_recv()
            if s < REACH:
                cc[s, j] = send(kv.at[s, j, half_rows], kv.at[s, j, half_rows], c_peer)

    def take_c(s):
        for j in range(2):
            cc[s, j].wait_recv()
            if s == REACH:
                dc[s, j].wait_recv()

    take_z(1)
    for s in range(1, REACH + 1):
        if s < REACH:
            take_z(s + 1)
            take_x(s)
        if s > 1:
            take_c(s - 1)
        forward(s - 1)
    take_x(REACH)
    take_c(REACH)
    forward(REACH)

    inv, delta = [], []
    for i in range(nch):
        inv.append(1.0 / acc[HD:HD + 1, i * CH:(i + 1) * CH])

    def finish():
        for i in range(nch):
            lo = i * CH
            out = (acc[:HD, lo:lo + CH] * inv[i]).astype(BF)
            ot[:, lo:lo + CH] = out
            delta.append(jnp.sum(gt[:, lo:lo + CH].astype(F32) * out.astype(F32), axis=0, keepdims=True))

    bc, bx, bz = {}, {}, {}
    far_x = pl.ds(pl.multiple_of(core * 256 + (1 - xl) * QUART, QUART), QUART)
    far_c = pl.ds(pl.multiple_of((1 - core) * 256 + xl * QUART, QUART), QUART)
    far_d = pl.ds(pl.multiple_of((1 - core) * 256 + (1 - xl) * QUART, QUART), QUART)

    def give(s, j):
        if s in STRAIGHT:
            bx[s, j] = [send(term.at[s, j, rows], dbuf.at[s - STRAIGHT[0], j, i], dev)
                        for i, (rows, dev) in enumerate(((far_x, x_peer), (far_d, x_diag), (far_c, c_peer)))]
        else:
            bc[s, j] = send(term.at[s, j, peer_half], cbuf.at[s, j], c_peer)

    def backward(s):
        b = s % 2
        fac = [jnp.exp2((m_at[s, i] - m_run[i]) * EXPC) * inv[i] for i in range(nch)]
        for i in range(nch):
            lo = i * CH
            gs[b, :, lo:lo + CH] = (gt[:, lo:lo + CH].astype(F32) * fac[i]).astype(BF)
            qs[b, :, lo:lo + CH] = (qt[:HD, lo:lo + CH].astype(F32) * (fac[i] * SCALE)).astype(BF)
        term[s, 1] = nt(probs[s], gs[b]).astype(BF)
        give(s, 1)
        if s == REACH:
            finish()
        for i in range(nch):
            lo = i * CH
            rows = live_rows(s, lo % BLK)
            cols = slice(lo, lo + CH)
            for r in range(rows.start, rows.stop, RB):
                piece = slice(r, r + RB)
                ds[b, piece, cols] = (probs[s, piece, cols].astype(F32) * (dprob[s, piece, cols] - delta[i])).astype(BF)
            blank(ds.at[b], rows, lo)
            part = nn(kvt[s, 0, :, rows], ds[b, rows, cols]) * fac[i]
            if s == REACH:
                dqt[:, lo:lo + CH] = part
            else:
                dqt[:, lo:lo + CH] = dqt[:, lo:lo + CH] + part
        term[s, 0] = nt(ds[b], qs[b]).astype(BF)
        give(s, 0)

    mine = pl.ds(pl.multiple_of(xl * QUART, QUART), QUART)
    other = pl.ds(pl.multiple_of((1 - xl) * QUART, QUART), QUART)
    other_rows = pl.ds(pl.multiple_of(core * 256 + (1 - xl) * QUART, QUART), QUART)

    def fold_c(s):
        for j in (1, 0):
            bc[s, j].wait_recv()
            xsend[s, j] = (term[s, j, other_rows].astype(F32) + cbuf[s, j, other].astype(F32)).astype(BF)
            bx[s, j] = send(xsend.at[s, j], xbuf.at[s, j], x_peer)
            hold[s, j] = term[s, j, my_rows].astype(F32) + cbuf[s, j, mine].astype(F32)


    def fold_x(s):
        for j in (1, 0):
            if s in STRAIGHT:
                for cp in bx[s, j]:
                    cp.wait_recv()
            else:
                bx[s, j].wait_recv()
            for k in range(NSUB):
                rows = slice(k * SUB, (k + 1) * SUB)
                if s in STRAIGHT:
                    near = dbuf.at[s - STRAIGHT[0], j]
                    total = term[s, j, sub_rows[k]].astype(F32) + near[0, rows].astype(F32)
                    total = total + near[1, rows].astype(F32) + near[2, rows].astype(F32)
                else:
                    total = hold[s, j, rows] + xbuf[s, j, rows].astype(F32)
                if s < REACH:
                    @pl.when((c >= s) & (c < n_ctx - 1))
                    def _():
                        bz[s + 1, j, k].wait_recv()

                    @pl.when((c < s) | (c == n_ctx - 1))
                    def _():
                        zbuf[s, j, rows] = jnp.zeros((SUB, HD), BF)

                    total = total + zbuf[s, j, rows].astype(F32)
                if s > 0:
                    zsend[s, j, rows] = total.astype(BF)
                    bz[s, j, k] = send(zsend.at[s, j, rows], zbuf.at[s - 1, j, rows], z_prev, c >= s)
                else:
                    stage[j, y, sub_rows[k]] = total.astype(BF)
            if s == 0:
                spread(j)

    ax, aup, adn, xup, xdn = {}, {}, {}, {}, {}

    def spread(j):
        piece = stage.at[j, y, my_rows]
        ax[j] = send(piece, piece, x_peer)
        aup[j] = send(piece, piece, y_next)
        adn[j] = send(piece, piece, y_prev)

    kept = []

    def keep(src, dst):
        cp = pltpu.make_async_copy(src, dst, ksem.at[len(kept)])
        cp.start()
        kept.append(cp)

    first_part = len(sent)
    backward(4)
    backward(3)
    backward(2)
    settle(first_part)
    fold_x(4)
    backward(1)
    fold_c(2)
    backward(0)
    fold_x(3)
    fold_c(1)
    fold_c(0)
    for h in range(2):
        o_v[:, h * HD:(h + 1) * HD] = ot[:, h * BLK:(h + 1) * BLK].T
    keep(o_v, o_ref)
    fold_x(2)
    for h in range(2):
        dq_v[:, h * HD:(h + 1) * HD] = (dqt[:, h * BLK:(h + 1) * BLK] * SCALE).astype(BF).T
    keep(dq_v, dq_ref)
    second_part = len(sent)
    fold_x(1)
    settle(second_part)
    fold_x(0)

    below = (y + 3) % 4
    above = (y + 1) % 4

    def hrow(which, k):
        return pl.ds(pl.multiple_of(core * 256 + which * QUART + k * 64, 64), 64)

    fin = []

    def relay(j, which):
        up = stage.at[j, below, hrow(which, 0)]
        dn = stage.at[j, above, hrow(which, 1)]
        up_out = kvg_ref.at[j, below, hrow(which, 0)]
        dn_out = kvg_ref.at[j, above, hrow(which, 1)]
        fin.append(send(up, up_out, y_next))
        fin.append(send(dn, dn_out, y_prev))
        fin.append(send(up, up_out, y_next_o))
        fin.append(send(dn, dn_out, y_prev_o))

    def share(j, g):
        piece, out = stage.at[j, g, half_rows], kvg_ref.at[j, g, half_rows]
        fin.append(send(piece, out, c_peer))
        keep(piece, out)

    for j in (1, 0):
        ax[j].wait_recv()
        piece = stage.at[j, y, other_rows]
        xup[j] = send(piece, piece, y_next)
        xdn[j] = send(piece, piece, y_prev)
        share(j, y)
    for j in (1, 0):
        aup[j].wait_recv()
        adn[j].wait_recv()
        relay(j, xl)
    for j in (1, 0):
        xup[j].wait_recv()
        xdn[j].wait_recv()
        relay(j, 1 - xl)
        for cols in (below, above):
            share(j, cols)
    for cp in fin:
        cp.wait_recv()
    settle(len(sent))
    for cp in kept:
        cp.wait()
    assert len(sent) == N_SEND, len(sent)


def place_outputs(o_raw, dq_raw, kvg_raw, o_out, dq_out, dk_out, dv_out, o_v, dq_v, kvg_v, isem, osem):
    fetch = [pltpu.make_async_copy(o_raw, o_v, isem.at[0]), pltpu.make_async_copy(dq_raw, dq_v, isem.at[1])]
    store = [pltpu.make_async_copy(o_v, o_out, osem.at[0]), pltpu.make_async_copy(dq_v, dq_out, osem.at[1])]
    for j, out in enumerate((dk_out, dv_out)):
        for g in range(KVH):
            i = len(fetch)
            fetch.append(pltpu.make_async_copy(kvg_raw.at[j, g], kvg_v.at[j, g], isem.at[i]))
            store.append(pltpu.make_async_copy(kvg_v.at[j, g], out.at[:, g * HD:(g + 1) * HD], osem.at[i]))
    for cp in fetch:
        cp.start()
    for get, put in zip(fetch, store):
        get.wait()
        put.start()
    for cp in store:
        cp.wait()


N_SEND = 90


def solution(mesh):
    n_ctx = mesh.shape["ctx"]

    def per_device(queries, keys, values, out_grad, doc_lengths):
        steps = REACH + 1
        hbm = pl.BlockSpec(memory_space=pl.ANY)
        shapes = tuple(jax.ShapeDtypeStruct(a.shape, BF) for a in (queries, queries, keys, values))
        raw = pl.pallas_call(
            functools.partial(kernel, n_ctx, doc_lengths.shape[0]),
            out_shape=shapes[:2] + (jax.ShapeDtypeStruct((2, KVH, BLK, HD), BF),),
            in_specs=[hbm, hbm, hbm, hbm, pl.BlockSpec(memory_space=pltpu.SMEM)],
            out_specs=(hbm, hbm, hbm),
            scratch_shapes=[
                pltpu.VMEM((BLK, 256), BF),
                pltpu.VMEM((BLK, 256), BF),
                pltpu.VMEM((steps, 2, BLK, HD), BF),
                pltpu.VMEM((2 * HD, QN), BF),
                pltpu.VMEM((HD, QN), BF),
                pltpu.VMEM((steps, 1, HD, BLK), BF),
                pltpu.VMEM((2, HD + 8, BLK), BF),
                pltpu.VMEM((2, BLK, 2 * HD), BF),
                pltpu.VMEM((2, BLK, CH), F32),
                pltpu.VMEM((steps, BLK, QN), BF),
                pltpu.VMEM((steps, BLK, QN), F32),
                pltpu.VMEM((HD + 8, QN), F32),
                pltpu.VMEM((HD, QN), BF),
                pltpu.VMEM((HD, QN), F32),
                pltpu.VMEM((2, HD, QN), BF),
                pltpu.VMEM((2, HD, QN), BF),
                pltpu.VMEM((2, BLK, QN), BF),
                pltpu.VMEM((steps, 2, BLK, HD), BF),
                pltpu.VMEM((steps, 2, 256, HD), BF),
                pltpu.VMEM((len(STRAIGHT), 2, 3, QUART, HD), BF),
                pltpu.VMEM((steps, 2, QUART, HD), F32),
                pltpu.VMEM((steps, 2, QUART, HD), BF),
                pltpu.VMEM((steps, 2, QUART, HD), BF),
                pltpu.VMEM((REACH, 2, QUART, HD), BF),
                pltpu.VMEM((steps, 2, QUART, HD), BF),
                pltpu.VMEM((2, KVH, BLK, HD), BF),
                pltpu.VMEM((BLK, 256), BF),
                pltpu.VMEM((BLK, 256), BF),
                pltpu.SemaphoreType.DMA((8,)),
                pltpu.SemaphoreType.DMA((4,)),
                pltpu.SemaphoreType.DMA((N_SEND,)),
                pltpu.SemaphoreType.DMA((N_SEND,)),
            ],
            compiler_params=pltpu.CompilerParams(
                collective_id=0, has_side_effects=True, vmem_limit_bytes=60 * 1024 * 1024
            ),
        )(queries, keys, values, out_grad, doc_lengths)
        return pl.pallas_call(
            place_outputs,
            out_shape=shapes,
            in_specs=[hbm] * 3,
            out_specs=(hbm,) * 4,
            scratch_shapes=[
                pltpu.VMEM((BLK, 256), BF),
                pltpu.VMEM((BLK, 256), BF),
                pltpu.VMEM((2, KVH, BLK, HD), BF),
                pltpu.SemaphoreType.DMA((10,)),
                pltpu.SemaphoreType.DMA((10,)),
            ],
            compiler_params=pltpu.CompilerParams(vmem_limit_bytes=62 * 1024 * 1024),
        )(*raw)

    return jax.shard_map(
        per_device,
        mesh=mesh,
        in_specs=(P("ctx", "tp"), P("ctx", None), P("ctx", None), P("ctx", "tp"), P()),
        out_specs=(P("ctx", "tp"), P("ctx", "tp"), P("ctx", None), P("ctx", None)),
        check_vma=False,
    )
```

```python
import functools
import math

import jax
import jax.numpy as jnp
from jax import lax
from jax.experimental import pallas as pl
from jax.experimental.pallas import tpu as pltpu
from jax.sharding import PartitionSpec as P

MESH = pl.DeviceIdType.MESH
HD = 128
KVH = 4
REACH = 4
BLK = 512
QN = 1024
CH = 256
RB = 128
QUART = 128
NSUB = 2
SUB = QUART // NSUB
STRAIGHT = (3, 4)
NEG = -1e30
FLOOR = -1e9
SCALE = 1.0 / math.sqrt(HD)
EXPC = SCALE * math.log2(math.e)
F32 = jnp.float32
BF = jnp.bfloat16


def nt(a, b):
    return lax.dot_general(a, b, (((1,), (1,)), ((), ())), preferred_element_type=F32)


def nn(a, b):
    return jnp.dot(a, b, preferred_element_type=F32)


def kernel(n_ctx, ndoc, q_hbm, k_hbm, v_hbm, g_hbm, len_ref, o_ref, dq_ref, kvg_ref,
           q_in, g_in, kv, qt, gt, kvt, vtr, kx, sbuf, probs, dprob, acc, ot, dqt, gs, qs, ds,
           term, cbuf, dbuf, hold, xsend, xbuf, zbuf, zsend, xs0, xr0, zdiag, stage, o_v, dq_v, ksem, lsem, ssem, rsem):
    c = lax.axis_index("ctx")
    t = lax.axis_index("tp")
    half_ctx = n_ctx // 2
    y, xlo, core = t // 4, (t // 2) % 2, t % 2
    xhi = c // half_ctx
    xl = xlo + xhi - 2 * xlo * xhi

    def place(ctx, yy, xx, cc):
        hi = ctx // half_ctx
        lo = xx + hi - 2 * xx * hi
        return (ctx, yy * 4 + lo * 2 + cc)

    z_next = place((c + 1) % n_ctx, y, xl, core)
    z_prev = place((c + n_ctx - 1) % n_ctx, y, xl, core)
    x_peer = place(c, y, 1 - xl, core)
    c_peer = place(c, y, xl, 1 - core)
    y_next = place(c, (y + 1) % 4, xl, core)
    y_prev = place(c, (y + 3) % 4, xl, core)
    x_diag = place(c, y, 1 - xl, 1 - core)
    z_next_x = place((c + 1) % n_ctx, y, 1 - xl, core)
    z_prev_x = place((c + n_ctx - 1) % n_ctx, y, 1 - xl, core)
    y_next_o = place(c, (y + 1) % 4, xl, 1 - core)
    y_prev_o = place(c, (y + 3) % 4, xl, 1 - core)

    col = pl.ds(pl.multiple_of(y * HD, HD), HD)
    my_half = pl.multiple_of(core * 256, 256)
    my_rows = pl.ds(pl.multiple_of(core * 256 + xl * QUART, QUART), QUART)
    sub_rows = [pl.ds(pl.multiple_of(core * 256 + xl * QUART + k * SUB, SUB), SUB) for k in range(NSUB)]
    half_rows = pl.ds(my_half, 256)
    peer_half = pl.ds(pl.multiple_of((1 - core) * 256, 256), 256)

    loads = [
        pltpu.make_async_copy(q_hbm, q_in, lsem.at[0]),
        pltpu.make_async_copy(g_hbm, g_in, lsem.at[1]),
        pltpu.make_async_copy(k_hbm.at[:, col], kv.at[0, 0], lsem.at[2]),
        pltpu.make_async_copy(v_hbm.at[:, col], kv.at[0, 1], lsem.at[3]),
    ]
    for cp in loads:
        cp.start()

    barrier = pltpu.get_barrier_semaphore()
    peers = (x_peer, c_peer, y_next, y_prev, x_diag, y_next_o, y_prev_o)
    for dev, ok in ((z_next, c < n_ctx - 1), (z_prev, c > 0), (z_next_x, c < n_ctx - 1), (z_prev_x, c > 0)):
        @pl.when(ok)
        def _(dev=dev):
            pl.semaphore_signal(barrier, inc=1, device_id=dev, device_id_type=MESH)

    for dev in peers:
        pl.semaphore_signal(barrier, inc=1, device_id=dev, device_id_type=MESH)
    for cp in loads[2:]:
        cp.wait()
    pl.semaphore_wait(barrier, len(peers) + 2 * jnp.minimum(c, 1) + 2 * jnp.minimum(n_ctx - 1 - c, 1))

    sent = []

    def only(ok, act):
        if ok is None:
            act()
        else:
            pl.when(ok)(act)

    def send(src, dst, dev, ok=None):
        i = len(sent)
        cp = pltpu.make_async_remote_copy(src_ref=src, dst_ref=dst, send_sem=ssem.at[i], recv_sem=rsem.at[i],
                                          device_id=dev, device_id_type=MESH)
        only(ok, lambda: cp.start())
        sent.append((cp, ok))
        return cp

    settled = [0]

    def settle(upto):
        for cp, ok in sent[settled[0]:upto]:
            only(ok, lambda: cp.wait_send())
        settled[0] = upto

    zc, xc, cc, dc = {}, {}, {}, {}
    for j in range(2):
        for k in range(NSUB):
            zc[1, j, k] = send(kv.at[0, j, sub_rows[k]], kv.at[1, j, sub_rows[k]], z_next, c < n_ctx - 1)

    lane = lax.broadcasted_iota(jnp.int32, (1, BLK), 1)
    dlane = lax.broadcasted_iota(jnp.int32, (1, HD), 1)
    drow = lax.broadcasted_iota(jnp.int32, (HD, 1), 0)
    lo_l, hi_l = jnp.zeros((1, HD), jnp.int32), jnp.zeros((1, HD), jnp.int32)
    lo_r, hi_r = jnp.zeros((HD, 1), jnp.int32), jnp.zeros((HD, 1), jnp.int32)
    end = jnp.int32(0)
    for d in range(ndoc):
        lo_l, lo_r = jnp.where(dlane == d, end, lo_l), jnp.where(drow == d, end, lo_r)
        end = end + len_ref[d]
        hi_l, hi_r = jnp.where(dlane == d, end, hi_l), jnp.where(drow == d, end, hi_r)
    lo_l = jnp.where(dlane == ndoc, -(1 << 30), lo_l)
    pos = lane + c * BLK
    block_doc = jnp.where((pos >= lo_r) & (pos < hi_r), 0.0, NEG).astype(BF)
    kpos0 = lax.broadcasted_iota(jnp.int32, (BLK, HD), 0) + c * BLK
    krow = lax.broadcasted_iota(jnp.int32, (RB, CH), 0)
    for b in range(2):
        vtr[b, HD:] = jnp.ones((8, BLK), BF)

    for cp in loads[:2]:
        cp.wait()
    for h in range(2):
        qt[:HD, h * BLK:(h + 1) * BLK] = q_in[:, h * HD:(h + 1) * HD].T
        qt[HD:, h * BLK:(h + 1) * BLK] = block_doc
        gt[:, h * BLK:(h + 1) * BLK] = g_in[:, h * HD:(h + 1) * HD].T

    nch = QN // CH
    m_run = [jnp.full((1, CH), FLOOR, F32)] * nch
    m_at = {}

    def live_rows(s, off):
        if s == 0 and off + CH <= BLK // 2:
            return slice(0, BLK // 2)
        if s == REACH and off >= BLK // 2:
            return slice(BLK // 2, BLK)
        return slice(0, BLK)

    def blank(ref, rows, lo):
        if rows.stop - rows.start < BLK:
            skipped = slice(BLK // 2, BLK) if rows.start == 0 else slice(0, BLK // 2)
            ref[skipped, lo:lo + CH] = jnp.zeros((BLK // 2, CH), BF)

    def forward(s):
        b = s % 2
        kvt[s, 0] = kv[s, 0].T
        vtr[b, :HD] = kv[s, 1].T
        kx[b, :, :HD] = kv[s, 0]
        kpos = kpos0 - s * BLK
        kx[b, :, HD:] = jnp.where((kpos >= lo_l) & (kpos < hi_l), 1.0, 0.0).astype(BF)
        for i in range(nch):
            lo = i * CH
            off = (i * CH) % BLK
            cols = slice(lo, lo + CH)
            rows = live_rows(s, off)
            pieces = [slice(r, r + RB) for r in range(rows.start, rows.stop, RB)]
            top = m_run[i]
            for piece in pieces:
                sc = nn(kx[b, piece], qt[:, cols])
                if s == 0 and piece.stop > off:
                    sc = jnp.where(krow + piece.start <= lane[:, off:off + CH], sc, NEG)
                sbuf[i % 2, piece] = sc
                top = jnp.maximum(top, jnp.max(sc, axis=0, keepdims=True))
            scaled = top * EXPC
            for piece in pieces:
                probs[s, piece, cols] = jnp.exp2(sbuf[i % 2, piece] * EXPC - scaled).astype(BF)
            fade = jnp.exp2((m_run[i] - top) * EXPC)
            m_run[i] = top
            m_at[s, i] = top
            blank(probs.at[s], rows, lo)
            part = nn(vtr[b, :, rows], probs[s, rows, cols])
            if s == 0:
                acc[:, cols] = part
            else:
                acc[:, cols] = acc[:, cols] * fade + part
            for piece in pieces:
                dprob[s, piece, cols] = nn(kv[s, 1, piece], gt[:, cols])

    def take_z(s):
        for j in range(2):
            for k in range(NSUB):
                @pl.when(c >= s)
                def _():
                    zc[s, j, k].wait_recv()

                @pl.when(c < s)
                def _():
                    kv[s, j, sub_rows[k]] = jnp.zeros((SUB, HD), BF)

                if s < REACH:
                    zc[s + 1, j, k] = send(kv.at[s, j, sub_rows[k]], kv.at[s + 1, j, sub_rows[k]], z_next,
                                           (c >= s) & (c < n_ctx - 1))
            piece = kv.at[s, j, my_rows]
            xc[s, j] = send(piece, piece, x_peer)
            if s == REACH:
                dc[s, j] = send(piece, piece, x_diag)
                cc[s, j] = send(piece, piece, c_peer)

    def take_x(s):
        for j in range(2):
            xc[s, j].wait_recv()
            if s < REACH:
                cc[s, j] = send(kv.at[s, j, half_rows], kv.at[s, j, half_rows], c_peer)

    def take_c(s):
        for j in range(2):
            cc[s, j].wait_recv()
            if s == REACH:
                dc[s, j].wait_recv()

    take_z(1)
    for s in range(1, REACH + 1):
        if s < REACH:
            take_z(s + 1)
            take_x(s)
        if s > 1:
            take_c(s - 1)
        forward(s - 1)
    take_x(REACH)
    take_c(REACH)
    forward(REACH)

    inv, delta = [], []
    for i in range(nch):
        inv.append(1.0 / acc[HD:HD + 1, i * CH:(i + 1) * CH])

    def finish():
        for i in range(nch):
            lo = i * CH
            out = (acc[:HD, lo:lo + CH] * inv[i]).astype(BF)
            ot[:, lo:lo + CH] = out
            delta.append(jnp.sum(gt[:, lo:lo + CH].astype(F32) * out.astype(F32), axis=0, keepdims=True))

    bc, bx, bz = {}, {}, {}
    far_x = pl.ds(pl.multiple_of(core * 256 + (1 - xl) * QUART, QUART), QUART)
    far_c = pl.ds(pl.multiple_of((1 - core) * 256 + xl * QUART, QUART), QUART)
    far_d = pl.ds(pl.multiple_of((1 - core) * 256 + (1 - xl) * QUART, QUART), QUART)

    def give(s, j):
        if s in STRAIGHT:
            bx[s, j] = [send(term.at[s, j, rows], dbuf.at[s - STRAIGHT[0], j, i], dev)
                        for i, (rows, dev) in enumerate(((far_x, x_peer), (far_d, x_diag), (far_c, c_peer)))]
        else:
            bc[s, j] = send(term.at[s, j, peer_half], cbuf.at[s, j], c_peer)

    def backward(s):
        b = s % 2
        fac = [jnp.exp2((m_at[s, i] - m_run[i]) * EXPC) * inv[i] for i in range(nch)]
        for i in range(nch):
            lo = i * CH
            gs[b, :, lo:lo + CH] = (gt[:, lo:lo + CH].astype(F32) * fac[i]).astype(BF)
            qs[b, :, lo:lo + CH] = (qt[:HD, lo:lo + CH].astype(F32) * (fac[i] * SCALE)).astype(BF)
        term[s, 1] = nt(probs[s], gs[b]).astype(BF)
        give(s, 1)
        if s == REACH:
            finish()
        for i in range(nch):
            lo = i * CH
            rows = live_rows(s, lo % BLK)
            cols = slice(lo, lo + CH)
            for r in range(rows.start, rows.stop, RB):
                piece = slice(r, r + RB)
                ds[b, piece, cols] = (probs[s, piece, cols].astype(F32) * (dprob[s, piece, cols] - delta[i])).astype(BF)
            blank(ds.at[b], rows, lo)
            part = nn(kvt[s, 0, :, rows], ds[b, rows, cols]) * fac[i]
            if s == REACH:
                dqt[:, lo:lo + CH] = part
            else:
                dqt[:, lo:lo + CH] = dqt[:, lo:lo + CH] + part
        term[s, 0] = nt(ds[b], qs[b]).astype(BF)
        give(s, 0)

    mine = pl.ds(pl.multiple_of(xl * QUART, QUART), QUART)
    other = pl.ds(pl.multiple_of((1 - xl) * QUART, QUART), QUART)
    other_rows = pl.ds(pl.multiple_of(core * 256 + (1 - xl) * QUART, QUART), QUART)

    def fold_c(s):
        for j in (1, 0):
            bc[s, j].wait_recv()
            xsend[s, j] = (term[s, j, other_rows].astype(F32) + cbuf[s, j, other].astype(F32)).astype(BF)
            bx[s, j] = send(xsend.at[s, j], xbuf.at[s, j], x_peer)
            hold[s, j] = term[s, j, my_rows].astype(F32) + cbuf[s, j, mine].astype(F32)


    def fold_c_last():
        for j in (1, 0):
            bc[0, j].wait_recv()
            xs0[j] = (term[0, j, half_rows].astype(F32) + cbuf[0, j].astype(F32)).astype(BF)
            bx[0, j] = send(xs0.at[j], xr0.at[j], x_peer)

    def settle_last(j, at, arrived, rows):
        total = xs0[j, at].astype(F32) + xr0[j, at].astype(F32) + arrived.astype(F32)
        stage[j, y, rows] = total.astype(BF)

    def finish_last():
        coming = c < n_ctx - 1
        for j in (1, 0):
            bx[0, j].wait_recv()
            for k in range(NSUB):
                rows = slice(k * SUB, (k + 1) * SUB)

                @pl.when(coming)
                def _():
                    bz[1, j, k].wait_recv()

                @pl.when(c == n_ctx - 1)
                def _():
                    zbuf[0, j, rows] = jnp.zeros((SUB, HD), BF)

                at = pl.ds(pl.multiple_of(xl * QUART + k * SUB, SUB), SUB)
                settle_last(j, at, zbuf[0, j, rows], sub_rows[k])
            piece = stage.at[j, y, my_rows]
            aup[j] = send(piece, piece, y_next)
            adn[j] = send(piece, piece, y_prev)
        for j in (1, 0):
            @pl.when(coming)
            def _():
                bd[j].wait_recv()

            @pl.when(c == n_ctx - 1)
            def _():
                zdiag[j] = jnp.zeros((QUART, HD), BF)

            settle_last(j, other, zdiag[j], other_rows)
            piece = stage.at[j, y, other_rows]
            xup[j] = send(piece, piece, y_next)
            xdn[j] = send(piece, piece, y_prev)

    def fold_x(s):
        for j in (1, 0):
            if s in STRAIGHT:
                for cp in bx[s, j]:
                    cp.wait_recv()
            else:
                bx[s, j].wait_recv()
            for k in range(NSUB):
                rows = slice(k * SUB, (k + 1) * SUB)
                if s in STRAIGHT:
                    near = dbuf.at[s - STRAIGHT[0], j]
                    total = term[s, j, sub_rows[k]].astype(F32) + near[0, rows].astype(F32)
                    total = total + near[1, rows].astype(F32) + near[2, rows].astype(F32)
                else:
                    total = hold[s, j, rows] + xbuf[s, j, rows].astype(F32)
                if s < REACH:
                    @pl.when((c >= s) & (c < n_ctx - 1))
                    def _():
                        bz[s + 1, j, k].wait_recv()

                    @pl.when((c < s) | (c == n_ctx - 1))
                    def _():
                        zbuf[s, j, rows] = jnp.zeros((SUB, HD), BF)

                    total = total + zbuf[s, j, rows].astype(F32)
                zsend[s, j, rows] = total.astype(BF)
                bz[s, j, k] = send(zsend.at[s, j, rows], zbuf.at[s - 1, j, rows], z_prev, c >= s)
        if s == 1:
            for j in (1, 0):
                bd[j] = send(zsend.at[1, j], zdiag.at[j], z_prev_x, c >= 1)

    aup, adn, xup, xdn, bd = {}, {}, {}, {}, {}

    kept = []

    def keep(src, dst):
        cp = pltpu.make_async_copy(src, dst, ksem.at[len(kept)])
        cp.start()
        kept.append(cp)

    first_part = len(sent)
    backward(4)
    backward(3)
    backward(2)
    settle(first_part)
    fold_x(4)
    backward(1)
    fold_c(2)
    backward(0)
    fold_x(3)
    fold_c(1)
    fold_c_last()
    for h in range(2):
        o_v[:, h * HD:(h + 1) * HD] = ot[:, h * BLK:(h + 1) * BLK].T
    keep(o_v, o_ref)
    fold_x(2)
    for h in range(2):
        dq_v[:, h * HD:(h + 1) * HD] = (dqt[:, h * BLK:(h + 1) * BLK] * SCALE).astype(BF).T
    keep(dq_v, dq_ref)
    second_part = len(sent)
    fold_x(1)
    settle(second_part)
    finish_last()

    below = (y + 3) % 4
    above = (y + 1) % 4

    def hrow(which, k):
        return pl.ds(pl.multiple_of(core * 256 + which * QUART + k * 64, 64), 64)

    fin = []

    def relay(j, which):
        up = stage.at[j, below, hrow(which, 0)]
        dn = stage.at[j, above, hrow(which, 1)]
        up_out = kvg_ref.at[j, below, hrow(which, 0)]
        dn_out = kvg_ref.at[j, above, hrow(which, 1)]
        fin.append(send(up, up_out, y_next))
        fin.append(send(dn, dn_out, y_prev))
        fin.append(send(up, up_out, y_next_o))
        fin.append(send(dn, dn_out, y_prev_o))

    def share(j, g):
        piece, out = stage.at[j, g, half_rows], kvg_ref.at[j, g, half_rows]
        fin.append(send(piece, out, c_peer))
        keep(piece, out)

    for j in (1, 0):
        share(j, y)
    for j in (1, 0):
        aup[j].wait_recv()
        adn[j].wait_recv()
        relay(j, xl)
    for j in (1, 0):
        xup[j].wait_recv()
        xdn[j].wait_recv()
        relay(j, 1 - xl)
        for cols in (below, above):
            share(j, cols)
    for cp in fin:
        cp.wait_recv()
    settle(len(sent))
    for cp in kept:
        cp.wait()
    assert len(sent) == N_SEND, len(sent)


def place_outputs(o_raw, dq_raw, kvg_raw, o_out, dq_out, dk_out, dv_out, o_v, dq_v, kvg_v, isem, osem):
    fetch = [pltpu.make_async_copy(o_raw, o_v, isem.at[0]), pltpu.make_async_copy(dq_raw, dq_v, isem.at[1])]
    store = [pltpu.make_async_copy(o_v, o_out, osem.at[0]), pltpu.make_async_copy(dq_v, dq_out, osem.at[1])]
    for j, out in enumerate((dk_out, dv_out)):
        for g in range(KVH):
            i = len(fetch)
            fetch.append(pltpu.make_async_copy(kvg_raw.at[j, g], kvg_v.at[j, g], isem.at[i]))
            store.append(pltpu.make_async_copy(kvg_v.at[j, g], out.at[:, g * HD:(g + 1) * HD], osem.at[i]))
    for cp in fetch:
        cp.start()
    for get, put in zip(fetch, store):
        get.wait()
        put.start()
    for cp in store:
        cp.wait()


N_SEND = 106


def solution(mesh):
    n_ctx = mesh.shape["ctx"]

    def per_device(queries, keys, values, out_grad, doc_lengths):
        steps = REACH + 1
        hbm = pl.BlockSpec(memory_space=pl.ANY)
        shapes = tuple(jax.ShapeDtypeStruct(a.shape, BF) for a in (queries, queries, keys, values))
        raw = pl.pallas_call(
            functools.partial(kernel, n_ctx, doc_lengths.shape[0]),
            out_shape=shapes[:2] + (jax.ShapeDtypeStruct((2, KVH, BLK, HD), BF),),
            in_specs=[hbm, hbm, hbm, hbm, pl.BlockSpec(memory_space=pltpu.SMEM)],
            out_specs=(hbm, hbm, hbm),
            scratch_shapes=[
                pltpu.VMEM((BLK, 256), BF),
                pltpu.VMEM((BLK, 256), BF),
                pltpu.VMEM((steps, 2, BLK, HD), BF),
                pltpu.VMEM((2 * HD, QN), BF),
                pltpu.VMEM((HD, QN), BF),
                pltpu.VMEM((steps, 1, HD, BLK), BF),
                pltpu.VMEM((2, HD + 8, BLK), BF),
                pltpu.VMEM((2, BLK, 2 * HD), BF),
                pltpu.VMEM((2, BLK, CH), F32),
                pltpu.VMEM((steps, BLK, QN), BF),
                pltpu.VMEM((steps, BLK, QN), F32),
                pltpu.VMEM((HD + 8, QN), F32),
                pltpu.VMEM((HD, QN), BF),
                pltpu.VMEM((HD, QN), F32),
                pltpu.VMEM((2, HD, QN), BF),
                pltpu.VMEM((2, HD, QN), BF),
                pltpu.VMEM((2, BLK, QN), BF),
                pltpu.VMEM((steps, 2, BLK, HD), BF),
                pltpu.VMEM((steps, 2, 256, HD), BF),
                pltpu.VMEM((len(STRAIGHT), 2, 3, QUART, HD), BF),
                pltpu.VMEM((steps, 2, QUART, HD), F32),
                pltpu.VMEM((steps, 2, QUART, HD), BF),
                pltpu.VMEM((steps, 2, QUART, HD), BF),
                pltpu.VMEM((REACH, 2, QUART, HD), BF),
                pltpu.VMEM((steps, 2, QUART, HD), BF),
                pltpu.VMEM((2, 256, HD), BF),
                pltpu.VMEM((2, 256, HD), BF),
                pltpu.VMEM((2, QUART, HD), BF),
                pltpu.VMEM((2, KVH, BLK, HD), BF),
                pltpu.VMEM((BLK, 256), BF),
                pltpu.VMEM((BLK, 256), BF),
                pltpu.SemaphoreType.DMA((8,)),
                pltpu.SemaphoreType.DMA((4,)),
                pltpu.SemaphoreType.DMA((N_SEND,)),
                pltpu.SemaphoreType.DMA((N_SEND,)),
            ],
            compiler_params=pltpu.CompilerParams(
                collective_id=0, has_side_effects=True, vmem_limit_bytes=60 * 1024 * 1024
            ),
        )(queries, keys, values, out_grad, doc_lengths)
        return pl.pallas_call(
            place_outputs,
            out_shape=shapes,
            in_specs=[hbm] * 3,
            out_specs=(hbm,) * 4,
            scratch_shapes=[
                pltpu.VMEM((BLK, 256), BF),
                pltpu.VMEM((BLK, 256), BF),
                pltpu.VMEM((2, KVH, BLK, HD), BF),
                pltpu.SemaphoreType.DMA((10,)),
                pltpu.SemaphoreType.DMA((10,)),
            ],
            compiler_params=pltpu.CompilerParams(vmem_limit_bytes=62 * 1024 * 1024),
        )(*raw)

    return jax.shard_map(
        per_device,
        mesh=mesh,
        in_specs=(P("ctx", "tp"), P("ctx", None), P("ctx", None), P("ctx", "tp"), P()),
        out_specs=(P("ctx", "tp"), P("ctx", "tp"), P("ctx", None), P("ctx", None)),
        check_vma=False,
    )
```

```python
import functools
import math

import jax
import jax.numpy as jnp
from jax import lax
from jax.experimental import pallas as pl
from jax.experimental.pallas import tpu as pltpu
from jax.sharding import PartitionSpec as P

MESH = pl.DeviceIdType.MESH
HD = 128
KVH = 4
REACH = 4
BLK = 512
QN = 1024
CH = 256
RB = 128
QUART = 128
NSUB = 2
SUB = QUART // NSUB
STRAIGHT = (3, 4)
NEG = -1e30
FLOOR = -1e9
SCALE = 1.0 / math.sqrt(HD)
EXPC = SCALE * math.log2(math.e)
F32 = jnp.float32
BF = jnp.bfloat16


def nt(a, b):
    return lax.dot_general(a, b, (((1,), (1,)), ((), ())), preferred_element_type=F32)


def nn(a, b):
    return jnp.dot(a, b, preferred_element_type=F32)


def kernel(n_ctx, ndoc, q_hbm, k_hbm, v_hbm, g_hbm, len_ref, o_ref, dq_ref, kvg_ref,
           q_in, g_in, kv, qt, gt, kvt, vtr, kx, sbuf, probs, dprob, acc, ot, dqt, gs, qs, ds,
           term, cbuf, dbuf, hold, xsend, xbuf, zbuf, zsend, xs0, xr0, zdiag, stage, o_v, dq_v, ksem, lsem, ssem, rsem):
    c = lax.axis_index("ctx")
    t = lax.axis_index("tp")
    half_ctx = n_ctx // 2
    y, xlo, core = t // 4, (t // 2) % 2, t % 2
    xhi = c // half_ctx
    xl = xlo + xhi - 2 * xlo * xhi

    def place(ctx, yy, xx, cc):
        hi = ctx // half_ctx
        lo = xx + hi - 2 * xx * hi
        return (ctx, yy * 4 + lo * 2 + cc)

    z_next = place((c + 1) % n_ctx, y, xl, core)
    z_prev = place((c + n_ctx - 1) % n_ctx, y, xl, core)
    x_peer = place(c, y, 1 - xl, core)
    c_peer = place(c, y, xl, 1 - core)
    y_next = place(c, (y + 1) % 4, xl, core)
    y_prev = place(c, (y + 3) % 4, xl, core)
    x_diag = place(c, y, 1 - xl, 1 - core)
    z_next_x = place((c + 1) % n_ctx, y, 1 - xl, core)
    z_prev_x = place((c + n_ctx - 1) % n_ctx, y, 1 - xl, core)
    y_next_o = place(c, (y + 1) % 4, xl, 1 - core)
    y_prev_o = place(c, (y + 3) % 4, xl, 1 - core)

    col = pl.ds(pl.multiple_of(y * HD, HD), HD)
    my_half = pl.multiple_of(core * 256, 256)
    my_rows = pl.ds(pl.multiple_of(core * 256 + xl * QUART, QUART), QUART)
    sub_rows = [pl.ds(pl.multiple_of(core * 256 + xl * QUART + k * SUB, SUB), SUB) for k in range(NSUB)]
    other_rows = pl.ds(pl.multiple_of(core * 256 + (1 - xl) * QUART, QUART), QUART)
    half_rows = pl.ds(my_half, 256)
    peer_half = pl.ds(pl.multiple_of((1 - core) * 256, 256), 256)

    loads = [
        pltpu.make_async_copy(q_hbm, q_in, lsem.at[0]),
        pltpu.make_async_copy(g_hbm, g_in, lsem.at[1]),
        pltpu.make_async_copy(k_hbm.at[:, col], kv.at[0, 0], lsem.at[2]),
        pltpu.make_async_copy(v_hbm.at[:, col], kv.at[0, 1], lsem.at[3]),
    ]
    for cp in loads:
        cp.start()

    barrier = pltpu.get_barrier_semaphore()
    peers = (x_peer, c_peer, y_next, y_prev, x_diag, y_next_o, y_prev_o)
    for dev, ok in ((z_next, c < n_ctx - 1), (z_prev, c > 0), (z_next_x, c < n_ctx - 1), (z_prev_x, c > 0)):
        @pl.when(ok)
        def _(dev=dev):
            pl.semaphore_signal(barrier, inc=1, device_id=dev, device_id_type=MESH)

    for dev in peers:
        pl.semaphore_signal(barrier, inc=1, device_id=dev, device_id_type=MESH)
    for cp in loads[2:]:
        cp.wait()
    pl.semaphore_wait(barrier, len(peers) + 2 * jnp.minimum(c, 1) + 2 * jnp.minimum(n_ctx - 1 - c, 1))

    sent = []

    def only(ok, act):
        if ok is None:
            act()
        else:
            pl.when(ok)(act)

    def send(src, dst, dev, ok=None):
        i = len(sent)
        cp = pltpu.make_async_remote_copy(src_ref=src, dst_ref=dst, send_sem=ssem.at[i], recv_sem=rsem.at[i],
                                          device_id=dev, device_id_type=MESH)
        only(ok, lambda: cp.start())
        sent.append((cp, ok))
        return cp

    settled = [0]

    def settle(upto):
        for cp, ok in sent[settled[0]:upto]:
            only(ok, lambda: cp.wait_send())
        settled[0] = upto

    zc, xc, cc, dc = {}, {}, {}, {}
    for j in range(2):
        for k in range(NSUB):
            zc[1, j, k] = send(kv.at[0, j, sub_rows[k]], kv.at[1, j, sub_rows[k]], z_next, c < n_ctx - 1)

    lane = lax.broadcasted_iota(jnp.int32, (1, BLK), 1)
    dlane = lax.broadcasted_iota(jnp.int32, (1, HD), 1)
    drow = lax.broadcasted_iota(jnp.int32, (HD, 1), 0)
    lo_l, hi_l = jnp.zeros((1, HD), jnp.int32), jnp.zeros((1, HD), jnp.int32)
    lo_r, hi_r = jnp.zeros((HD, 1), jnp.int32), jnp.zeros((HD, 1), jnp.int32)
    end = jnp.int32(0)
    for d in range(ndoc):
        lo_l, lo_r = jnp.where(dlane == d, end, lo_l), jnp.where(drow == d, end, lo_r)
        end = end + len_ref[d]
        hi_l, hi_r = jnp.where(dlane == d, end, hi_l), jnp.where(drow == d, end, hi_r)
    lo_l = jnp.where(dlane == ndoc, -(1 << 30), lo_l)
    pos = lane + c * BLK
    block_doc = jnp.where((pos >= lo_r) & (pos < hi_r), 0.0, NEG).astype(BF)
    kpos0 = lax.broadcasted_iota(jnp.int32, (BLK, HD), 0) + c * BLK
    krow = lax.broadcasted_iota(jnp.int32, (RB, CH), 0)
    for b in range(2):
        vtr[b, HD:] = jnp.ones((8, BLK), BF)

    for cp in loads[:2]:
        cp.wait()
    for h in range(2):
        qt[:HD, h * BLK:(h + 1) * BLK] = q_in[:, h * HD:(h + 1) * HD].T
        qt[HD:, h * BLK:(h + 1) * BLK] = block_doc
        gt[:, h * BLK:(h + 1) * BLK] = g_in[:, h * HD:(h + 1) * HD].T

    nch = QN // CH
    m_run = [jnp.full((1, CH), FLOOR, F32)] * nch
    m_at = {}

    def live_rows(s, off):
        if s == 0 and off + CH <= BLK // 2:
            return slice(0, BLK // 2)
        if s == REACH and off >= BLK // 2:
            return slice(BLK // 2, BLK)
        return slice(0, BLK)

    def blank(ref, rows, lo):
        if rows.stop - rows.start < BLK:
            skipped = slice(BLK // 2, BLK) if rows.start == 0 else slice(0, BLK // 2)
            ref[skipped, lo:lo + CH] = jnp.zeros((BLK // 2, CH), BF)

    def forward(s):
        b = s % 2
        kvt[s, 0] = kv[s, 0].T
        vtr[b, :HD] = kv[s, 1].T
        kx[b, :, :HD] = kv[s, 0]
        kpos = kpos0 - s * BLK
        kx[b, :, HD:] = jnp.where((kpos >= lo_l) & (kpos < hi_l), 1.0, 0.0).astype(BF)
        for i in range(nch):
            lo = i * CH
            off = (i * CH) % BLK
            cols = slice(lo, lo + CH)
            rows = live_rows(s, off)
            pieces = [slice(r, r + RB) for r in range(rows.start, rows.stop, RB)]
            top = m_run[i]
            for piece in pieces:
                sc = nn(kx[b, piece], qt[:, cols])
                if s == 0 and piece.stop > off:
                    sc = jnp.where(krow + piece.start <= lane[:, off:off + CH], sc, NEG)
                sbuf[i % 2, piece] = sc
                top = jnp.maximum(top, jnp.max(sc, axis=0, keepdims=True))
            scaled = top * EXPC
            for piece in pieces:
                probs[s, piece, cols] = jnp.exp2(sbuf[i % 2, piece] * EXPC - scaled).astype(BF)
            fade = jnp.exp2((m_run[i] - top) * EXPC)
            m_run[i] = top
            m_at[s, i] = top
            blank(probs.at[s], rows, lo)
            part = nn(vtr[b, :, rows], probs[s, rows, cols])
            if s == 0:
                acc[:, cols] = part
            else:
                acc[:, cols] = acc[:, cols] * fade + part
            for piece in pieces:
                dprob[s, piece, cols] = nn(kv[s, 1, piece], gt[:, cols])

    def take_z(s):
        for j in range(2):
            for k in range(NSUB):
                @pl.when(c >= s)
                def _():
                    zc[s, j, k].wait_recv()

                @pl.when(c < s)
                def _():
                    kv[s, j, sub_rows[k]] = jnp.zeros((SUB, HD), BF)

                if s < REACH:
                    zc[s + 1, j, k] = send(kv.at[s, j, sub_rows[k]], kv.at[s + 1, j, sub_rows[k]], z_next,
                                           (c >= s) & (c < n_ctx - 1))
            if s < REACH:
                piece = kv.at[s, j, my_rows]
                xc[s, j] = send(piece, piece, x_peer)
            else:
                @pl.when(c >= s)
                def _():
                    dc[s, j].wait_recv()

                @pl.when(c < s)
                def _():
                    kv[s, j, other_rows] = jnp.zeros((QUART, HD), BF)

                cc[s, j] = send(kv.at[s, j, half_rows], kv.at[s, j, half_rows], c_peer)
        if s == REACH - 1:
            for j in range(2):
                dc[s + 1, j] = send(kv.at[s, j, my_rows], kv.at[s + 1, j, my_rows], z_next_x,
                                    (c >= s) & (c < n_ctx - 1))

    def take_x(s):
        for j in range(2):
            xc[s, j].wait_recv()
            cc[s, j] = send(kv.at[s, j, half_rows], kv.at[s, j, half_rows], c_peer)

    def take_c(s):
        for j in range(2):
            cc[s, j].wait_recv()

    forward(0)
    take_z(1)
    take_z(2)
    take_x(1)
    take_z(3)
    take_x(2)
    take_c(1)
    forward(1)
    take_x(3)
    take_c(2)
    forward(2)
    take_z(4)
    take_c(3)
    forward(3)
    take_c(4)
    forward(4)

    inv, delta = [], []
    for i in range(nch):
        inv.append(1.0 / acc[HD:HD + 1, i * CH:(i + 1) * CH])

    def finish():
        for i in range(nch):
            lo = i * CH
            out = (acc[:HD, lo:lo + CH] * inv[i]).astype(BF)
            ot[:, lo:lo + CH] = out
            delta.append(jnp.sum(gt[:, lo:lo + CH].astype(F32) * out.astype(F32), axis=0, keepdims=True))

    bc, bx, bz = {}, {}, {}
    far_x = pl.ds(pl.multiple_of(core * 256 + (1 - xl) * QUART, QUART), QUART)
    far_c = pl.ds(pl.multiple_of((1 - core) * 256 + xl * QUART, QUART), QUART)
    far_d = pl.ds(pl.multiple_of((1 - core) * 256 + (1 - xl) * QUART, QUART), QUART)

    def give(s, j):
        if s in STRAIGHT:
            bx[s, j] = [send(term.at[s, j, rows], dbuf.at[s - STRAIGHT[0], j, i], dev)
                        for i, (rows, dev) in enumerate(((far_x, x_peer), (far_d, x_diag), (far_c, c_peer)))]
        else:
            bc[s, j] = send(term.at[s, j, peer_half], cbuf.at[s, j], c_peer)

    def backward(s):
        b = s % 2
        fac = [jnp.exp2((m_at[s, i] - m_run[i]) * EXPC) * inv[i] for i in range(nch)]
        for i in range(nch):
            lo = i * CH
            gs[b, :, lo:lo + CH] = (gt[:, lo:lo + CH].astype(F32) * fac[i]).astype(BF)
            qs[b, :, lo:lo + CH] = (qt[:HD, lo:lo + CH].astype(F32) * (fac[i] * SCALE)).astype(BF)
        term[s, 1] = nt(probs[s], gs[b]).astype(BF)
        give(s, 1)
        if s == REACH:
            finish()
        for i in range(nch):
            lo = i * CH
            rows = live_rows(s, lo % BLK)
            cols = slice(lo, lo + CH)
            for r in range(rows.start, rows.stop, RB):
                piece = slice(r, r + RB)
                ds[b, piece, cols] = (probs[s, piece, cols].astype(F32) * (dprob[s, piece, cols] - delta[i])).astype(BF)
            blank(ds.at[b], rows, lo)
            part = nn(kvt[s, 0, :, rows], ds[b, rows, cols]) * fac[i]
            if s == REACH:
                dqt[:, lo:lo + CH] = part
            else:
                dqt[:, lo:lo + CH] = dqt[:, lo:lo + CH] + part
        term[s, 0] = nt(ds[b], qs[b]).astype(BF)
        give(s, 0)

    mine = pl.ds(pl.multiple_of(xl * QUART, QUART), QUART)
    other = pl.ds(pl.multiple_of((1 - xl) * QUART, QUART), QUART)
    other_rows = pl.ds(pl.multiple_of(core * 256 + (1 - xl) * QUART, QUART), QUART)

    def fold_c(s):
        for j in (1, 0):
            bc[s, j].wait_recv()
            xsend[s, j] = (term[s, j, other_rows].astype(F32) + cbuf[s, j, other].astype(F32)).astype(BF)
            bx[s, j] = send(xsend.at[s, j], xbuf.at[s, j], x_peer)
            hold[s, j] = term[s, j, my_rows].astype(F32) + cbuf[s, j, mine].astype(F32)


    def fold_c_last():
        for j in (1, 0):
            bc[0, j].wait_recv()
            xs0[j] = (term[0, j, half_rows].astype(F32) + cbuf[0, j].astype(F32)).astype(BF)
            bx[0, j] = send(xs0.at[j], xr0.at[j], x_peer)

    def settle_last(j, at, arrived, rows):
        total = xs0[j, at].astype(F32) + xr0[j, at].astype(F32) + arrived.astype(F32)
        stage[j, y, rows] = total.astype(BF)

    def finish_last():
        coming = c < n_ctx - 1
        for j in (1, 0):
            bx[0, j].wait_recv()
            for k in range(NSUB):
                rows = slice(k * SUB, (k + 1) * SUB)

                @pl.when(coming)
                def _():
                    bz[1, j, k].wait_recv()

                @pl.when(c == n_ctx - 1)
                def _():
                    zbuf[0, j, rows] = jnp.zeros((SUB, HD), BF)

                at = pl.ds(pl.multiple_of(xl * QUART + k * SUB, SUB), SUB)
                settle_last(j, at, zbuf[0, j, rows], sub_rows[k])
            piece = stage.at[j, y, my_rows]
            aup[j] = send(piece, piece, y_next)
            adn[j] = send(piece, piece, y_prev)
        for j in (1, 0):
            @pl.when(coming)
            def _():
                bd[j].wait_recv()

            @pl.when(c == n_ctx - 1)
            def _():
                zdiag[j] = jnp.zeros((QUART, HD), BF)

            settle_last(j, other, zdiag[j], other_rows)
            piece = stage.at[j, y, other_rows]
            xup[j] = send(piece, piece, y_next)
            xdn[j] = send(piece, piece, y_prev)

    def fold_x(s):
        for j in (1, 0):
            if s in STRAIGHT:
                for cp in bx[s, j]:
                    cp.wait_recv()
            else:
                bx[s, j].wait_recv()
            for k in range(NSUB):
                rows = slice(k * SUB, (k + 1) * SUB)
                if s in STRAIGHT:
                    near = dbuf.at[s - STRAIGHT[0], j]
                    total = term[s, j, sub_rows[k]].astype(F32) + near[0, rows].astype(F32)
                    total = total + near[1, rows].astype(F32) + near[2, rows].astype(F32)
                else:
                    total = hold[s, j, rows] + xbuf[s, j, rows].astype(F32)
                if s < REACH:
                    @pl.when((c >= s) & (c < n_ctx - 1))
                    def _():
                        bz[s + 1, j, k].wait_recv()

                    @pl.when((c < s) | (c == n_ctx - 1))
                    def _():
                        zbuf[s, j, rows] = jnp.zeros((SUB, HD), BF)

                    total = total + zbuf[s, j, rows].astype(F32)
                zsend[s, j, rows] = total.astype(BF)
                bz[s, j, k] = send(zsend.at[s, j, rows], zbuf.at[s - 1, j, rows], z_prev, c >= s)
        if s == 1:
            for j in (1, 0):
                bd[j] = send(zsend.at[1, j], zdiag.at[j], z_prev_x, c >= 1)

    aup, adn, xup, xdn, bd = {}, {}, {}, {}, {}

    kept = []

    def keep(src, dst):
        cp = pltpu.make_async_copy(src, dst, ksem.at[len(kept)])
        cp.start()
        kept.append(cp)

    first_part = len(sent)
    backward(4)
    backward(3)
    backward(2)
    settle(first_part)
    fold_x(4)
    backward(1)
    fold_c(2)
    backward(0)
    fold_x(3)
    fold_c(1)
    fold_c_last()
    for h in range(2):
        o_v[:, h * HD:(h + 1) * HD] = ot[:, h * BLK:(h + 1) * BLK].T
    keep(o_v, o_ref)
    fold_x(2)
    for h in range(2):
        dq_v[:, h * HD:(h + 1) * HD] = (dqt[:, h * BLK:(h + 1) * BLK] * SCALE).astype(BF).T
    keep(dq_v, dq_ref)
    second_part = len(sent)
    fold_x(1)
    settle(second_part)
    finish_last()

    below = (y + 3) % 4
    above = (y + 1) % 4

    def hrow(which, k):
        return pl.ds(pl.multiple_of(core * 256 + which * QUART + k * 64, 64), 64)

    fin = []

    def relay(j, which):
        up = stage.at[j, below, hrow(which, 0)]
        dn = stage.at[j, above, hrow(which, 1)]
        up_out = kvg_ref.at[j, below, hrow(which, 0)]
        dn_out = kvg_ref.at[j, above, hrow(which, 1)]
        fin.append(send(up, up_out, y_next))
        fin.append(send(dn, dn_out, y_prev))
        fin.append(send(up, up_out, y_next_o))
        fin.append(send(dn, dn_out, y_prev_o))

    def share(j, g):
        piece, out = stage.at[j, g, half_rows], kvg_ref.at[j, g, half_rows]
        fin.append(send(piece, out, c_peer))
        keep(piece, out)

    for j in (1, 0):
        share(j, y)
    for j in (1, 0):
        aup[j].wait_recv()
        adn[j].wait_recv()
        relay(j, xl)
    for j in (1, 0):
        xup[j].wait_recv()
        xdn[j].wait_recv()
        relay(j, 1 - xl)
        for cols in (below, above):
            share(j, cols)
    for cp in fin:
        cp.wait_recv()
    settle(len(sent))
    for cp in kept:
        cp.wait()
    assert len(sent) == N_SEND, len(sent)


def place_outputs(o_raw, dq_raw, kvg_raw, o_out, dq_out, dk_out, dv_out, o_v, dq_v, kvg_v, isem, osem):
    fetch = [pltpu.make_async_copy(o_raw, o_v, isem.at[0]), pltpu.make_async_copy(dq_raw, dq_v, isem.at[1])]
    store = [pltpu.make_async_copy(o_v, o_out, osem.at[0]), pltpu.make_async_copy(dq_v, dq_out, osem.at[1])]
    for j, out in enumerate((dk_out, dv_out)):
        for g in range(KVH):
            i = len(fetch)
            fetch.append(pltpu.make_async_copy(kvg_raw.at[j, g], kvg_v.at[j, g], isem.at[i]))
            store.append(pltpu.make_async_copy(kvg_v.at[j, g], out.at[:, g * HD:(g + 1) * HD], osem.at[i]))
    for cp in fetch:
        cp.start()
    for get, put in zip(fetch, store):
        get.wait()
        put.start()
    for cp in store:
        cp.wait()


N_SEND = 104


def solution(mesh):
    n_ctx = mesh.shape["ctx"]

    def per_device(queries, keys, values, out_grad, doc_lengths):
        steps = REACH + 1
        hbm = pl.BlockSpec(memory_space=pl.ANY)
        shapes = tuple(jax.ShapeDtypeStruct(a.shape, BF) for a in (queries, queries, keys, values))
        raw = pl.pallas_call(
            functools.partial(kernel, n_ctx, doc_lengths.shape[0]),
            out_shape=shapes[:2] + (jax.ShapeDtypeStruct((2, KVH, BLK, HD), BF),),
            in_specs=[hbm, hbm, hbm, hbm, pl.BlockSpec(memory_space=pltpu.SMEM)],
            out_specs=(hbm, hbm, hbm),
            scratch_shapes=[
                pltpu.VMEM((BLK, 256), BF),
                pltpu.VMEM((BLK, 256), BF),
                pltpu.VMEM((steps, 2, BLK, HD), BF),
                pltpu.VMEM((2 * HD, QN), BF),
                pltpu.VMEM((HD, QN), BF),
                pltpu.VMEM((steps, 1, HD, BLK), BF),
                pltpu.VMEM((2, HD + 8, BLK), BF),
                pltpu.VMEM((2, BLK, 2 * HD), BF),
                pltpu.VMEM((2, BLK, CH), F32),
                pltpu.VMEM((steps, BLK, QN), BF),
                pltpu.VMEM((steps, BLK, QN), F32),
                pltpu.VMEM((HD + 8, QN), F32),
                pltpu.VMEM((HD, QN), BF),
                pltpu.VMEM((HD, QN), F32),
                pltpu.VMEM((2, HD, QN), BF),
                pltpu.VMEM((2, HD, QN), BF),
                pltpu.VMEM((2, BLK, QN), BF),
                pltpu.VMEM((steps, 2, BLK, HD), BF),
                pltpu.VMEM((steps, 2, 256, HD), BF),
                pltpu.VMEM((len(STRAIGHT), 2, 3, QUART, HD), BF),
                pltpu.VMEM((steps, 2, QUART, HD), F32),
                pltpu.VMEM((steps, 2, QUART, HD), BF),
                pltpu.VMEM((steps, 2, QUART, HD), BF),
                pltpu.VMEM((REACH, 2, QUART, HD), BF),
                pltpu.VMEM((steps, 2, QUART, HD), BF),
                pltpu.VMEM((2, 256, HD), BF),
                pltpu.VMEM((2, 256, HD), BF),
                pltpu.VMEM((2, QUART, HD), BF),
                pltpu.VMEM((2, KVH, BLK, HD), BF),
                pltpu.VMEM((BLK, 256), BF),
                pltpu.VMEM((BLK, 256), BF),
                pltpu.SemaphoreType.DMA((8,)),
                pltpu.SemaphoreType.DMA((4,)),
                pltpu.SemaphoreType.DMA((N_SEND,)),
                pltpu.SemaphoreType.DMA((N_SEND,)),
            ],
            compiler_params=pltpu.CompilerParams(
                collective_id=0, has_side_effects=True, vmem_limit_bytes=60 * 1024 * 1024
            ),
        )(queries, keys, values, out_grad, doc_lengths)
        return pl.pallas_call(
            place_outputs,
            out_shape=shapes,
            in_specs=[hbm] * 3,
            out_specs=(hbm,) * 4,
            scratch_shapes=[
                pltpu.VMEM((BLK, 256), BF),
                pltpu.VMEM((BLK, 256), BF),
                pltpu.VMEM((2, KVH, BLK, HD), BF),
                pltpu.SemaphoreType.DMA((10,)),
                pltpu.SemaphoreType.DMA((10,)),
            ],
            compiler_params=pltpu.CompilerParams(vmem_limit_bytes=62 * 1024 * 1024),
        )(*raw)

    return jax.shard_map(
        per_device,
        mesh=mesh,
        in_specs=(P("ctx", "tp"), P("ctx", None), P("ctx", None), P("ctx", "tp"), P()),
        out_specs=(P("ctx", "tp"), P("ctx", "tp"), P("ctx", None), P("ctx", None)),
        check_vma=False,
    )
```

```python
import functools
import math

import jax
import jax.numpy as jnp
from jax import lax
from jax.experimental import pallas as pl
from jax.experimental.pallas import tpu as pltpu
from jax.sharding import PartitionSpec as P

MESH = pl.DeviceIdType.MESH
HD = 128
KVH = 4
REACH = 4
BLK = 512
QN = 1024
CH = 256
RB = 128
QUART = 128
NSUB = 4
SUB = QUART // NSUB
STRAIGHT = (3, 4)
NEG = -1e30
FLOOR = -1e9
SCALE = 1.0 / math.sqrt(HD)
EXPC = SCALE * math.log2(math.e)
F32 = jnp.float32
BF = jnp.bfloat16


def nt(a, b):
    return lax.dot_general(a, b, (((1,), (1,)), ((), ())), preferred_element_type=F32)


def nn(a, b):
    return jnp.dot(a, b, preferred_element_type=F32)


def kernel(n_ctx, ndoc, q_hbm, k_hbm, v_hbm, g_hbm, len_ref, o_ref, dq_ref, kvg_ref,
           q_in, g_in, kv, qt, gt, kvt, vtr, kx, sbuf, probs, dprob, acc, ot, dqt, gs, qs, ds,
           term, cbuf, dbuf, hold, xsend, xbuf, zbuf, zsend, xs0, xr0, zdiag, stage, o_v, dq_v, ksem, lsem, ssem, rsem):
    c = lax.axis_index("ctx")
    t = lax.axis_index("tp")
    half_ctx = n_ctx // 2
    y, xlo, core = t // 4, (t // 2) % 2, t % 2
    xhi = c // half_ctx
    xl = xlo + xhi - 2 * xlo * xhi

    def place(ctx, yy, xx, cc):
        hi = ctx // half_ctx
        lo = xx + hi - 2 * xx * hi
        return (ctx, yy * 4 + lo * 2 + cc)

    z_next = place((c + 1) % n_ctx, y, xl, core)
    z_prev = place((c + n_ctx - 1) % n_ctx, y, xl, core)
    x_peer = place(c, y, 1 - xl, core)
    c_peer = place(c, y, xl, 1 - core)
    y_next = place(c, (y + 1) % 4, xl, core)
    y_prev = place(c, (y + 3) % 4, xl, core)
    x_diag = place(c, y, 1 - xl, 1 - core)
    z_next_x = place((c + 1) % n_ctx, y, 1 - xl, core)
    z_prev_x = place((c + n_ctx - 1) % n_ctx, y, 1 - xl, core)
    y_next_o = place(c, (y + 1) % 4, xl, 1 - core)
    y_prev_o = place(c, (y + 3) % 4, xl, 1 - core)

    col = pl.ds(pl.multiple_of(y * HD, HD), HD)
    my_half = pl.multiple_of(core * 256, 256)
    my_rows = pl.ds(pl.multiple_of(core * 256 + xl * QUART, QUART), QUART)
    sub_rows = [pl.ds(pl.multiple_of(core * 256 + xl * QUART + k * SUB, SUB), SUB) for k in range(NSUB)]
    other_rows = pl.ds(pl.multiple_of(core * 256 + (1 - xl) * QUART, QUART), QUART)
    half_rows = pl.ds(my_half, 256)
    peer_half = pl.ds(pl.multiple_of((1 - core) * 256, 256), 256)

    loads = [
        pltpu.make_async_copy(q_hbm, q_in, lsem.at[0]),
        pltpu.make_async_copy(g_hbm, g_in, lsem.at[1]),
        pltpu.make_async_copy(k_hbm.at[:, col], kv.at[0, 0], lsem.at[2]),
        pltpu.make_async_copy(v_hbm.at[:, col], kv.at[0, 1], lsem.at[3]),
    ]
    for cp in loads:
        cp.start()

    barrier = pltpu.get_barrier_semaphore()
    peers = (x_peer, c_peer, y_next, y_prev, x_diag, y_next_o, y_prev_o)
    for dev, ok in ((z_next, c < n_ctx - 1), (z_prev, c > 0), (z_next_x, c < n_ctx - 1), (z_prev_x, c > 0)):
        @pl.when(ok)
        def _(dev=dev):
            pl.semaphore_signal(barrier, inc=1, device_id=dev, device_id_type=MESH)

    for dev in peers:
        pl.semaphore_signal(barrier, inc=1, device_id=dev, device_id_type=MESH)
    for cp in loads[2:]:
        cp.wait()
    pl.semaphore_wait(barrier, len(peers) + 2 * jnp.minimum(c, 1) + 2 * jnp.minimum(n_ctx - 1 - c, 1))

    sent = []

    def only(ok, act):
        if ok is None:
            act()
        else:
            pl.when(ok)(act)

    def send(src, dst, dev, ok=None):
        i = len(sent)
        cp = pltpu.make_async_remote_copy(src_ref=src, dst_ref=dst, send_sem=ssem.at[i], recv_sem=rsem.at[i],
                                          device_id=dev, device_id_type=MESH)
        only(ok, lambda: cp.start())
        sent.append((cp, ok))
        return cp

    settled = [0]

    def settle(upto):
        for cp, ok in sent[settled[0]:upto]:
            only(ok, lambda: cp.wait_send())
        settled[0] = upto

    zc, xc, cc, dc = {}, {}, {}, {}
    for j in range(2):
        for k in range(NSUB):
            zc[1, j, k] = send(kv.at[0, j, sub_rows[k]], kv.at[1, j, sub_rows[k]], z_next, c < n_ctx - 1)

    lane = lax.broadcasted_iota(jnp.int32, (1, BLK), 1)
    dlane = lax.broadcasted_iota(jnp.int32, (1, HD), 1)
    drow = lax.broadcasted_iota(jnp.int32, (HD, 1), 0)
    lo_l, hi_l = jnp.zeros((1, HD), jnp.int32), jnp.zeros((1, HD), jnp.int32)
    lo_r, hi_r = jnp.zeros((HD, 1), jnp.int32), jnp.zeros((HD, 1), jnp.int32)
    end = jnp.int32(0)
    for d in range(ndoc):
        lo_l, lo_r = jnp.where(dlane == d, end, lo_l), jnp.where(drow == d, end, lo_r)
        end = end + len_ref[d]
        hi_l, hi_r = jnp.where(dlane == d, end, hi_l), jnp.where(drow == d, end, hi_r)
    lo_l = jnp.where(dlane == ndoc, -(1 << 30), lo_l)
    pos = lane + c * BLK
    block_doc = jnp.where((pos >= lo_r) & (pos < hi_r), 0.0, NEG).astype(BF)
    kpos0 = lax.broadcasted_iota(jnp.int32, (BLK, HD), 0) + c * BLK
    krow = lax.broadcasted_iota(jnp.int32, (RB, CH), 0)
    for b in range(2):
        vtr[b, HD:] = jnp.ones((8, BLK), BF)

    for cp in loads[:2]:
        cp.wait()
    for h in range(2):
        qt[:HD, h * BLK:(h + 1) * BLK] = q_in[:, h * HD:(h + 1) * HD].T
        qt[HD:, h * BLK:(h + 1) * BLK] = block_doc
        gt[:, h * BLK:(h + 1) * BLK] = g_in[:, h * HD:(h + 1) * HD].T

    nch = QN // CH
    m_run = [jnp.full((1, CH), FLOOR, F32)] * nch
    m_at = {}

    def live_rows(s, off):
        if s == 0 and off + CH <= BLK // 2:
            return slice(0, BLK // 2)
        if s == REACH and off >= BLK // 2:
            return slice(BLK // 2, BLK)
        return slice(0, BLK)

    def blank(ref, rows, lo):
        if rows.stop - rows.start < BLK:
            skipped = slice(BLK // 2, BLK) if rows.start == 0 else slice(0, BLK // 2)
            ref[skipped, lo:lo + CH] = jnp.zeros((BLK // 2, CH), BF)

    def forward(s):
        b = s % 2
        kvt[s, 0] = kv[s, 0].T
        vtr[b, :HD] = kv[s, 1].T
        kx[b, :, :HD] = kv[s, 0]
        kpos = kpos0 - s * BLK
        kx[b, :, HD:] = jnp.where((kpos >= lo_l) & (kpos < hi_l), 1.0, 0.0).astype(BF)
        for i in range(nch):
            lo = i * CH
            off = (i * CH) % BLK
            cols = slice(lo, lo + CH)
            rows = live_rows(s, off)
            pieces = [slice(r, r + RB) for r in range(rows.start, rows.stop, RB)]
            top = m_run[i]
            for piece in pieces:
                sc = nn(kx[b, piece], qt[:, cols])
                if s == 0 and piece.stop > off:
                    sc = jnp.where(krow + piece.start <= lane[:, off:off + CH], sc, NEG)
                sbuf[i % 2, piece] = sc
                top = jnp.maximum(top, jnp.max(sc, axis=0, keepdims=True))
            scaled = top * EXPC
            for piece in pieces:
                probs[s, piece, cols] = jnp.exp2(sbuf[i % 2, piece] * EXPC - scaled).astype(BF)
            fade = jnp.exp2((m_run[i] - top) * EXPC)
            m_run[i] = top
            m_at[s, i] = top
            blank(probs.at[s], rows, lo)
            part = nn(vtr[b, :, rows], probs[s, rows, cols])
            if s == 0:
                acc[:, cols] = part
            else:
                acc[:, cols] = acc[:, cols] * fade + part
            for piece in pieces:
                dprob[s, piece, cols] = nn(kv[s, 1, piece], gt[:, cols])

    def take_z(s):
        for j in range(2):
            for k in range(NSUB):
                @pl.when(c >= s)
                def _():
                    zc[s, j, k].wait_recv()

                @pl.when(c < s)
                def _():
                    kv[s, j, sub_rows[k]] = jnp.zeros((SUB, HD), BF)

                if s < REACH:
                    zc[s + 1, j, k] = send(kv.at[s, j, sub_rows[k]], kv.at[s + 1, j, sub_rows[k]], z_next,
                                           (c >= s) & (c < n_ctx - 1))
            if s < REACH:
                piece = kv.at[s, j, my_rows]
                xc[s, j] = send(piece, piece, x_peer)
            else:
                @pl.when(c >= s)
                def _():
                    dc[s, j].wait_recv()

                @pl.when(c < s)
                def _():
                    kv[s, j, other_rows] = jnp.zeros((QUART, HD), BF)

                cc[s, j] = send(kv.at[s, j, half_rows], kv.at[s, j, half_rows], c_peer)
        if s == REACH - 1:
            for j in range(2):
                dc[s + 1, j] = send(kv.at[s, j, my_rows], kv.at[s + 1, j, my_rows], z_next_x,
                                    (c >= s) & (c < n_ctx - 1))

    def take_x(s):
        for j in range(2):
            xc[s, j].wait_recv()
            cc[s, j] = send(kv.at[s, j, half_rows], kv.at[s, j, half_rows], c_peer)

    def take_c(s):
        for j in range(2):
            cc[s, j].wait_recv()

    forward(0)
    take_z(1)
    take_z(2)
    take_x(1)
    take_z(3)
    take_x(2)
    take_c(1)
    forward(1)
    take_x(3)
    take_c(2)
    forward(2)
    take_z(4)
    take_c(3)
    forward(3)
    take_c(4)
    forward(4)

    inv, delta = [], []
    for i in range(nch):
        inv.append(1.0 / acc[HD:HD + 1, i * CH:(i + 1) * CH])

    def finish():
        for i in range(nch):
            lo = i * CH
            out = (acc[:HD, lo:lo + CH] * inv[i]).astype(BF)
            ot[:, lo:lo + CH] = out
            delta.append(jnp.sum(gt[:, lo:lo + CH].astype(F32) * out.astype(F32), axis=0, keepdims=True))

    bc, bx, bz = {}, {}, {}
    far_x = pl.ds(pl.multiple_of(core * 256 + (1 - xl) * QUART, QUART), QUART)
    far_c = pl.ds(pl.multiple_of((1 - core) * 256 + xl * QUART, QUART), QUART)
    far_d = pl.ds(pl.multiple_of((1 - core) * 256 + (1 - xl) * QUART, QUART), QUART)

    def give(s, j):
        if s in STRAIGHT:
            bx[s, j] = [send(term.at[s, j, rows], dbuf.at[s - STRAIGHT[0], j, i], dev)
                        for i, (rows, dev) in enumerate(((far_x, x_peer), (far_d, x_diag), (far_c, c_peer)))]
        else:
            bc[s, j] = send(term.at[s, j, peer_half], cbuf.at[s, j], c_peer)

    def backward(s):
        b = s % 2
        fac = [jnp.exp2((m_at[s, i] - m_run[i]) * EXPC) * inv[i] for i in range(nch)]
        for i in range(nch):
            lo = i * CH
            gs[b, :, lo:lo + CH] = (gt[:, lo:lo + CH].astype(F32) * fac[i]).astype(BF)
            qs[b, :, lo:lo + CH] = (qt[:HD, lo:lo + CH].astype(F32) * (fac[i] * SCALE)).astype(BF)
        term[s, 1] = nt(probs[s], gs[b]).astype(BF)
        give(s, 1)
        if s == REACH:
            finish()
        for i in range(nch):
            lo = i * CH
            rows = live_rows(s, lo % BLK)
            cols = slice(lo, lo + CH)
            for r in range(rows.start, rows.stop, RB):
                piece = slice(r, r + RB)
                ds[b, piece, cols] = (probs[s, piece, cols].astype(F32) * (dprob[s, piece, cols] - delta[i])).astype(BF)
            blank(ds.at[b], rows, lo)
            part = nn(kvt[s, 0, :, rows], ds[b, rows, cols]) * fac[i]
            if s == REACH:
                dqt[:, lo:lo + CH] = part
            else:
                dqt[:, lo:lo + CH] = dqt[:, lo:lo + CH] + part
        term[s, 0] = nt(ds[b], qs[b]).astype(BF)
        give(s, 0)

    mine = pl.ds(pl.multiple_of(xl * QUART, QUART), QUART)
    other = pl.ds(pl.multiple_of((1 - xl) * QUART, QUART), QUART)
    other_rows = pl.ds(pl.multiple_of(core * 256 + (1 - xl) * QUART, QUART), QUART)

    def fold_c(s):
        for j in (1, 0):
            bc[s, j].wait_recv()
            xsend[s, j] = (term[s, j, other_rows].astype(F32) + cbuf[s, j, other].astype(F32)).astype(BF)
            bx[s, j] = send(xsend.at[s, j], xbuf.at[s, j], x_peer)
            hold[s, j] = term[s, j, my_rows].astype(F32) + cbuf[s, j, mine].astype(F32)


    def fold_c_last():
        for j in (1, 0):
            bc[0, j].wait_recv()
            xs0[j] = (term[0, j, half_rows].astype(F32) + cbuf[0, j].astype(F32)).astype(BF)
            bx[0, j] = send(xs0.at[j], xr0.at[j], x_peer)

    def settle_last(j, at, arrived, rows):
        total = xs0[j, at].astype(F32) + xr0[j, at].astype(F32) + arrived.astype(F32)
        stage[j, y, rows] = total.astype(BF)

    def finish_last():
        coming = c < n_ctx - 1
        for j in (1, 0):
            bx[0, j].wait_recv()
            for k in range(NSUB):
                rows = slice(k * SUB, (k + 1) * SUB)

                @pl.when(coming)
                def _():
                    bz[1, j, k].wait_recv()

                @pl.when(c == n_ctx - 1)
                def _():
                    zbuf[0, j, rows] = jnp.zeros((SUB, HD), BF)

                at = pl.ds(pl.multiple_of(xl * QUART + k * SUB, SUB), SUB)
                settle_last(j, at, zbuf[0, j, rows], sub_rows[k])
            piece = stage.at[j, y, my_rows]
            aup[j] = send(piece, piece, y_next)
            adn[j] = send(piece, piece, y_prev)
        for j in (1, 0):
            @pl.when(coming)
            def _():
                bd[j].wait_recv()

            @pl.when(c == n_ctx - 1)
            def _():
                zdiag[j] = jnp.zeros((QUART, HD), BF)

            settle_last(j, other, zdiag[j], other_rows)
            piece = stage.at[j, y, other_rows]
            xup[j] = send(piece, piece, y_next)
            xdn[j] = send(piece, piece, y_prev)

    def fold_x(s):
        for j in (1, 0):
            if s in STRAIGHT:
                for cp in bx[s, j]:
                    cp.wait_recv()
            else:
                bx[s, j].wait_recv()
            for k in range(NSUB):
                rows = slice(k * SUB, (k + 1) * SUB)
                if s in STRAIGHT:
                    near = dbuf.at[s - STRAIGHT[0], j]
                    total = term[s, j, sub_rows[k]].astype(F32) + near[0, rows].astype(F32)
                    total = total + near[1, rows].astype(F32) + near[2, rows].astype(F32)
                else:
                    total = hold[s, j, rows] + xbuf[s, j, rows].astype(F32)
                if s < REACH:
                    @pl.when((c >= s) & (c < n_ctx - 1))
                    def _():
                        bz[s + 1, j, k].wait_recv()

                    @pl.when((c < s) | (c == n_ctx - 1))
                    def _():
                        zbuf[s, j, rows] = jnp.zeros((SUB, HD), BF)

                    total = total + zbuf[s, j, rows].astype(F32)
                zsend[s, j, rows] = total.astype(BF)
                bz[s, j, k] = send(zsend.at[s, j, rows], zbuf.at[s - 1, j, rows], z_prev, c >= s)
        if s == 1:
            for j in (1, 0):
                bd[j] = send(zsend.at[1, j], zdiag.at[j], z_prev_x, c >= 1)

    aup, adn, xup, xdn, bd = {}, {}, {}, {}, {}

    kept = []

    def keep(src, dst):
        cp = pltpu.make_async_copy(src, dst, ksem.at[len(kept)])
        cp.start()
        kept.append(cp)

    first_part = len(sent)
    backward(4)
    backward(3)
    backward(2)
    settle(first_part)
    fold_x(4)
    backward(1)
    fold_c(2)
    backward(0)
    fold_x(3)
    fold_c(1)
    fold_c_last()
    for h in range(2):
        o_v[:, h * HD:(h + 1) * HD] = ot[:, h * BLK:(h + 1) * BLK].T
    keep(o_v, o_ref)
    fold_x(2)
    for h in range(2):
        dq_v[:, h * HD:(h + 1) * HD] = (dqt[:, h * BLK:(h + 1) * BLK] * SCALE).astype(BF).T
    keep(dq_v, dq_ref)
    second_part = len(sent)
    fold_x(1)
    settle(second_part)
    finish_last()

    below = (y + 3) % 4
    above = (y + 1) % 4

    def hrow(which, k):
        return pl.ds(pl.multiple_of(core * 256 + which * QUART + k * 64, 64), 64)

    fin = []

    def relay(j, which):
        up = stage.at[j, below, hrow(which, 0)]
        dn = stage.at[j, above, hrow(which, 1)]
        up_out = kvg_ref.at[j, below, hrow(which, 0)]
        dn_out = kvg_ref.at[j, above, hrow(which, 1)]
        fin.append(send(up, up_out, y_next))
        fin.append(send(dn, dn_out, y_prev))
        fin.append(send(up, up_out, y_next_o))
        fin.append(send(dn, dn_out, y_prev_o))

    def share(j, g):
        piece, out = stage.at[j, g, half_rows], kvg_ref.at[j, g, half_rows]
        fin.append(send(piece, out, c_peer))
        keep(piece, out)

    for j in (1, 0):
        share(j, y)
    for j in (1, 0):
        aup[j].wait_recv()
        adn[j].wait_recv()
        relay(j, xl)
    for j in (1, 0):
        xup[j].wait_recv()
        xdn[j].wait_recv()
        relay(j, 1 - xl)
        for cols in (below, above):
            share(j, cols)
    for cp in fin:
        cp.wait_recv()
    settle(len(sent))
    for cp in kept:
        cp.wait()
    assert len(sent) == N_SEND, len(sent)


def place_outputs(o_raw, dq_raw, kvg_raw, o_out, dq_out, dk_out, dv_out, o_v, dq_v, kvg_v, isem, osem):
    fetch = [pltpu.make_async_copy(o_raw, o_v, isem.at[0]), pltpu.make_async_copy(dq_raw, dq_v, isem.at[1])]
    store = [pltpu.make_async_copy(o_v, o_out, osem.at[0]), pltpu.make_async_copy(dq_v, dq_out, osem.at[1])]
    for j, out in enumerate((dk_out, dv_out)):
        for g in range(KVH):
            i = len(fetch)
            fetch.append(pltpu.make_async_copy(kvg_raw.at[j, g], kvg_v.at[j, g], isem.at[i]))
            store.append(pltpu.make_async_copy(kvg_v.at[j, g], out.at[:, g * HD:(g + 1) * HD], osem.at[i]))
    for cp in fetch:
        cp.start()
    for get, put in zip(fetch, store):
        get.wait()
        put.start()
    for cp in store:
        cp.wait()


N_SEND = 136


def solution(mesh):
    n_ctx = mesh.shape["ctx"]

    def per_device(queries, keys, values, out_grad, doc_lengths):
        steps = REACH + 1
        hbm = pl.BlockSpec(memory_space=pl.ANY)
        shapes = tuple(jax.ShapeDtypeStruct(a.shape, BF) for a in (queries, queries, keys, values))
        raw = pl.pallas_call(
            functools.partial(kernel, n_ctx, doc_lengths.shape[0]),
            out_shape=shapes[:2] + (jax.ShapeDtypeStruct((2, KVH, BLK, HD), BF),),
            in_specs=[hbm, hbm, hbm, hbm, pl.BlockSpec(memory_space=pltpu.SMEM)],
            out_specs=(hbm, hbm, hbm),
            scratch_shapes=[
                pltpu.VMEM((BLK, 256), BF),
                pltpu.VMEM((BLK, 256), BF),
                pltpu.VMEM((steps, 2, BLK, HD), BF),
                pltpu.VMEM((2 * HD, QN), BF),
                pltpu.VMEM((HD, QN), BF),
                pltpu.VMEM((steps, 1, HD, BLK), BF),
                pltpu.VMEM((2, HD + 8, BLK), BF),
                pltpu.VMEM((2, BLK, 2 * HD), BF),
                pltpu.VMEM((2, BLK, CH), F32),
                pltpu.VMEM((steps, BLK, QN), BF),
                pltpu.VMEM((steps, BLK, QN), F32),
                pltpu.VMEM((HD + 8, QN), F32),
                pltpu.VMEM((HD, QN), BF),
                pltpu.VMEM((HD, QN), F32),
                pltpu.VMEM((2, HD, QN), BF),
                pltpu.VMEM((2, HD, QN), BF),
                pltpu.VMEM((2, BLK, QN), BF),
                pltpu.VMEM((steps, 2, BLK, HD), BF),
                pltpu.VMEM((steps, 2, 256, HD), BF),
                pltpu.VMEM((len(STRAIGHT), 2, 3, QUART, HD), BF),
                pltpu.VMEM((steps, 2, QUART, HD), F32),
                pltpu.VMEM((steps, 2, QUART, HD), BF),
                pltpu.VMEM((steps, 2, QUART, HD), BF),
                pltpu.VMEM((REACH, 2, QUART, HD), BF),
                pltpu.VMEM((steps, 2, QUART, HD), BF),
                pltpu.VMEM((2, 256, HD), BF),
                pltpu.VMEM((2, 256, HD), BF),
                pltpu.VMEM((2, QUART, HD), BF),
                pltpu.VMEM((2, KVH, BLK, HD), BF),
                pltpu.VMEM((BLK, 256), BF),
                pltpu.VMEM((BLK, 256), BF),
                pltpu.SemaphoreType.DMA((8,)),
                pltpu.SemaphoreType.DMA((4,)),
                pltpu.SemaphoreType.DMA((N_SEND,)),
                pltpu.SemaphoreType.DMA((N_SEND,)),
            ],
            compiler_params=pltpu.CompilerParams(
                collective_id=0, has_side_effects=True, vmem_limit_bytes=60 * 1024 * 1024
            ),
        )(queries, keys, values, out_grad, doc_lengths)
        return pl.pallas_call(
            place_outputs,
            out_shape=shapes,
            in_specs=[hbm] * 3,
            out_specs=(hbm,) * 4,
            scratch_shapes=[
                pltpu.VMEM((BLK, 256), BF),
                pltpu.VMEM((BLK, 256), BF),
                pltpu.VMEM((2, KVH, BLK, HD), BF),
                pltpu.SemaphoreType.DMA((10,)),
                pltpu.SemaphoreType.DMA((10,)),
            ],
            compiler_params=pltpu.CompilerParams(vmem_limit_bytes=62 * 1024 * 1024),
        )(*raw)

    return jax.shard_map(
        per_device,
        mesh=mesh,
        in_specs=(P("ctx", "tp"), P("ctx", None), P("ctx", None), P("ctx", "tp"), P()),
        out_specs=(P("ctx", "tp"), P("ctx", "tp"), P("ctx", None), P("ctx", None)),
        check_vma=False,
    )
```

```python
import functools
import math

import jax
import jax.numpy as jnp
from jax import lax
from jax.experimental import pallas as pl
from jax.experimental.pallas import tpu as pltpu
from jax.sharding import PartitionSpec as P

MESH = pl.DeviceIdType.MESH
HD = 128
KVH = 4
REACH = 4
BLK = 512
QN = 1024
CH = 256
RB = 128
QUART = 128
NSUB = 2
SUB = QUART // NSUB
STRAIGHT = (3, 4)
NEG = -1e30
FLOOR = -1e9
SCALE = 1.0 / math.sqrt(HD)
EXPC = SCALE * math.log2(math.e)
F32 = jnp.float32
BF = jnp.bfloat16


def nt(a, b):
    return lax.dot_general(a, b, (((1,), (1,)), ((), ())), preferred_element_type=F32)


def nn(a, b):
    return jnp.dot(a, b, preferred_element_type=F32)


def kernel(n_ctx, ndoc, q_hbm, k_hbm, v_hbm, g_hbm, len_ref, o_ref, dq_ref, kvg_ref,
           q_in, g_in, kv, qt, gt, kvt, vtr, kx, sbuf, probs, dprob, acc, ot, dqt, gs, qs, ds,
           term, cbuf, dbuf, hold, xsend, xbuf, zbuf, zsend, xs0, xr0, zdiag, stage, o_v, dq_v, ksem, lsem, ssem, rsem):
    c = lax.axis_index("ctx")
    t = lax.axis_index("tp")
    half_ctx = n_ctx // 2
    y, xlo, core = t // 4, (t // 2) % 2, t % 2
    xhi = c // half_ctx
    xl = xlo + xhi - 2 * xlo * xhi

    def place(ctx, yy, xx, cc):
        hi = ctx // half_ctx
        lo = xx + hi - 2 * xx * hi
        return (ctx, yy * 4 + lo * 2 + cc)

    z_next = place((c + 1) % n_ctx, y, xl, core)
    z_prev = place((c + n_ctx - 1) % n_ctx, y, xl, core)
    x_peer = place(c, y, 1 - xl, core)
    c_peer = place(c, y, xl, 1 - core)
    y_next = place(c, (y + 1) % 4, xl, core)
    y_prev = place(c, (y + 3) % 4, xl, core)
    x_diag = place(c, y, 1 - xl, 1 - core)
    z_next_x = place((c + 1) % n_ctx, y, 1 - xl, core)
    z_prev_x = place((c + n_ctx - 1) % n_ctx, y, 1 - xl, core)
    y_next_o = place(c, (y + 1) % 4, xl, 1 - core)
    y_prev_o = place(c, (y + 3) % 4, xl, 1 - core)

    col = pl.ds(pl.multiple_of(y * HD, HD), HD)
    my_half = pl.multiple_of(core * 256, 256)
    my_rows = pl.ds(pl.multiple_of(core * 256 + xl * QUART, QUART), QUART)
    sub_rows = [pl.ds(pl.multiple_of(core * 256 + xl * QUART + k * SUB, SUB), SUB) for k in range(NSUB)]
    other_rows = pl.ds(pl.multiple_of(core * 256 + (1 - xl) * QUART, QUART), QUART)
    half_rows = pl.ds(my_half, 256)
    peer_half = pl.ds(pl.multiple_of((1 - core) * 256, 256), 256)

    loads = [
        pltpu.make_async_copy(q_hbm, q_in, lsem.at[0]),
        pltpu.make_async_copy(g_hbm, g_in, lsem.at[1]),
        pltpu.make_async_copy(k_hbm.at[:, col], kv.at[0, 0], lsem.at[2]),
        pltpu.make_async_copy(v_hbm.at[:, col], kv.at[0, 1], lsem.at[3]),
    ]
    for cp in loads:
        cp.start()

    barrier = pltpu.get_barrier_semaphore()
    peers = (x_peer, c_peer, y_next, y_prev, x_diag, y_next_o, y_prev_o)
    for dev, ok in ((z_next, c < n_ctx - 1), (z_prev, c > 0), (z_next_x, c < n_ctx - 1), (z_prev_x, c > 0)):
        @pl.when(ok)
        def _(dev=dev):
            pl.semaphore_signal(barrier, inc=1, device_id=dev, device_id_type=MESH)

    for dev in peers:
        pl.semaphore_signal(barrier, inc=1, device_id=dev, device_id_type=MESH)
    for cp in loads[2:]:
        cp.wait()
    pl.semaphore_wait(barrier, len(peers) + 2 * jnp.minimum(c, 1) + 2 * jnp.minimum(n_ctx - 1 - c, 1))

    sent = []

    def only(ok, act):
        if ok is None:
            act()
        else:
            pl.when(ok)(act)

    def send(src, dst, dev, ok=None):
        i = len(sent)
        cp = pltpu.make_async_remote_copy(src_ref=src, dst_ref=dst, send_sem=ssem.at[i], recv_sem=rsem.at[i],
                                          device_id=dev, device_id_type=MESH)
        only(ok, lambda: cp.start())
        sent.append((cp, ok))
        return cp

    settled = [0]

    def settle(upto):
        for cp, ok in sent[settled[0]:upto]:
            only(ok, lambda: cp.wait_send())
        settled[0] = upto

    zc, xc, cc, dc = {}, {}, {}, {}
    for j in range(2):
        for k in range(NSUB):
            zc[1, j, k] = send(kv.at[0, j, sub_rows[k]], kv.at[1, j, sub_rows[k]], z_next, c < n_ctx - 1)

    lane = lax.broadcasted_iota(jnp.int32, (1, BLK), 1)
    dlane = lax.broadcasted_iota(jnp.int32, (1, HD), 1)
    drow = lax.broadcasted_iota(jnp.int32, (HD, 1), 0)
    lo_l, hi_l = jnp.zeros((1, HD), jnp.int32), jnp.zeros((1, HD), jnp.int32)
    lo_r, hi_r = jnp.zeros((HD, 1), jnp.int32), jnp.zeros((HD, 1), jnp.int32)
    end = jnp.int32(0)
    for d in range(ndoc):
        lo_l, lo_r = jnp.where(dlane == d, end, lo_l), jnp.where(drow == d, end, lo_r)
        end = end + len_ref[d]
        hi_l, hi_r = jnp.where(dlane == d, end, hi_l), jnp.where(drow == d, end, hi_r)
    lo_l = jnp.where(dlane == ndoc, -(1 << 30), lo_l)
    pos = lane + c * BLK
    block_doc = jnp.where((pos >= lo_r) & (pos < hi_r), 0.0, NEG).astype(BF)
    kpos0 = lax.broadcasted_iota(jnp.int32, (BLK, HD), 0) + c * BLK
    krow = lax.broadcasted_iota(jnp.int32, (RB, CH), 0)
    for b in range(2):
        vtr[b, HD:] = jnp.ones((8, BLK), BF)

    for cp in loads[:2]:
        cp.wait()
    for h in range(2):
        qt[:HD, h * BLK:(h + 1) * BLK] = q_in[:, h * HD:(h + 1) * HD].T
        qt[HD:, h * BLK:(h + 1) * BLK] = block_doc
        gt[:, h * BLK:(h + 1) * BLK] = g_in[:, h * HD:(h + 1) * HD].T

    nch = QN // CH
    m_run = [jnp.full((1, CH), FLOOR, F32)] * nch
    m_at = {}

    def live_rows(s, off):
        if s == 0 and off + CH <= BLK // 2:
            return slice(0, BLK // 2)
        if s == REACH and off >= BLK // 2:
            return slice(BLK // 2, BLK)
        return slice(0, BLK)

    def blank(ref, rows, lo):
        if rows.stop - rows.start < BLK:
            skipped = slice(BLK // 2, BLK) if rows.start == 0 else slice(0, BLK // 2)
            ref[skipped, lo:lo + CH] = jnp.zeros((BLK // 2, CH), BF)

    def forward(s):
        b = s % 2
        kvt[s, 0] = kv[s, 0].T
        vtr[b, :HD] = kv[s, 1].T
        kx[b, :, :HD] = kv[s, 0]
        kpos = kpos0 - s * BLK
        kx[b, :, HD:] = jnp.where((kpos >= lo_l) & (kpos < hi_l), 1.0, 0.0).astype(BF)
        for i in range(nch):
            lo = i * CH
            off = (i * CH) % BLK
            cols = slice(lo, lo + CH)
            rows = live_rows(s, off)
            pieces = [slice(r, r + RB) for r in range(rows.start, rows.stop, RB)]
            top = m_run[i]
            for piece in pieces:
                sc = nn(kx[b, piece], qt[:, cols])
                if s == 0 and piece.stop > off:
                    sc = jnp.where(krow + piece.start <= lane[:, off:off + CH], sc, NEG)
                sbuf[i % 2, piece] = sc
                top = jnp.maximum(top, jnp.max(sc, axis=0, keepdims=True))
            scaled = top * EXPC
            for piece in pieces:
                probs[s, piece, cols] = jnp.exp2(sbuf[i % 2, piece] * EXPC - scaled).astype(BF)
            fade = jnp.exp2((m_run[i] - top) * EXPC)
            m_run[i] = top
            m_at[s, i] = top
            blank(probs.at[s], rows, lo)
            part = nn(vtr[b, :, rows], probs[s, rows, cols])
            if s == 0:
                acc[:, cols] = part
            else:
                acc[:, cols] = acc[:, cols] * fade + part
            for piece in pieces:
                dprob[s, piece, cols] = nn(kv[s, 1, piece], gt[:, cols])

    def take_z(s):
        for j in range(2):
            for k in range(NSUB):
                @pl.when(c >= s)
                def _():
                    zc[s, j, k].wait_recv()

                @pl.when(c < s)
                def _():
                    kv[s, j, sub_rows[k]] = jnp.zeros((SUB, HD), BF)

                if s < REACH:
                    zc[s + 1, j, k] = send(kv.at[s, j, sub_rows[k]], kv.at[s + 1, j, sub_rows[k]], z_next,
                                           (c >= s) & (c < n_ctx - 1))
            if s < REACH:
                piece = kv.at[s, j, my_rows]
                xc[s, j] = send(piece, piece, x_peer)
            else:
                @pl.when(c >= s)
                def _():
                    dc[s, j].wait_recv()

                @pl.when(c < s)
                def _():
                    kv[s, j, other_rows] = jnp.zeros((QUART, HD), BF)

                cc[s, j] = send(kv.at[s, j, half_rows], kv.at[s, j, half_rows], c_peer)
        if s == REACH - 1:
            for j in range(2):
                dc[s + 1, j] = send(kv.at[s, j, my_rows], kv.at[s + 1, j, my_rows], z_next_x,
                                    (c >= s) & (c < n_ctx - 1))

    def take_x(s):
        for j in range(2):
            xc[s, j].wait_recv()
            cc[s, j] = send(kv.at[s, j, half_rows], kv.at[s, j, half_rows], c_peer)

    def take_c(s):
        for j in range(2):
            cc[s, j].wait_recv()

    forward(0)
    take_z(1)
    take_z(2)
    take_x(1)
    take_z(3)
    take_x(2)
    take_c(1)
    forward(1)
    take_x(3)
    take_c(2)
    forward(2)
    take_z(4)
    take_c(3)
    forward(3)
    take_c(4)
    forward(4)

    inv, delta = [], []
    for i in range(nch):
        inv.append(1.0 / acc[HD:HD + 1, i * CH:(i + 1) * CH])

    def finish():
        for i in range(nch):
            lo = i * CH
            out = (acc[:HD, lo:lo + CH] * inv[i]).astype(BF)
            ot[:, lo:lo + CH] = out
            delta.append(jnp.sum(gt[:, lo:lo + CH].astype(F32) * out.astype(F32), axis=0, keepdims=True))

    bc, bx, bz = {}, {}, {}
    far_x = pl.ds(pl.multiple_of(core * 256 + (1 - xl) * QUART, QUART), QUART)
    far_c = pl.ds(pl.multiple_of((1 - core) * 256 + xl * QUART, QUART), QUART)
    far_d = pl.ds(pl.multiple_of((1 - core) * 256 + (1 - xl) * QUART, QUART), QUART)

    def give(s, j):
        if s in STRAIGHT:
            bx[s, j] = [send(term.at[s, j, rows], dbuf.at[s - STRAIGHT[0], j, i], dev)
                        for i, (rows, dev) in enumerate(((far_x, x_peer), (far_d, x_diag), (far_c, c_peer)))]
        else:
            bc[s, j] = send(term.at[s, j, peer_half], cbuf.at[s, j], c_peer)

    def backward(s):
        b = s % 2
        fac = [jnp.exp2((m_at[s, i] - m_run[i]) * EXPC) * inv[i] for i in range(nch)]
        for i in range(nch):
            lo = i * CH
            gs[b, :, lo:lo + CH] = (gt[:, lo:lo + CH].astype(F32) * fac[i]).astype(BF)
            qs[b, :, lo:lo + CH] = (qt[:HD, lo:lo + CH].astype(F32) * (fac[i] * SCALE)).astype(BF)
        term[s, 1] = nt(probs[s], gs[b]).astype(BF)
        give(s, 1)
        if s == REACH:
            finish()
        for i in range(nch):
            lo = i * CH
            rows = live_rows(s, lo % BLK)
            cols = slice(lo, lo + CH)
            for r in range(rows.start, rows.stop, RB):
                piece = slice(r, r + RB)
                ds[b, piece, cols] = (probs[s, piece, cols].astype(F32) * (dprob[s, piece, cols] - delta[i])).astype(BF)
            blank(ds.at[b], rows, lo)
            part = nn(kvt[s, 0, :, rows], ds[b, rows, cols]) * fac[i]
            if s == REACH:
                dqt[:, lo:lo + CH] = part
            else:
                dqt[:, lo:lo + CH] = dqt[:, lo:lo + CH] + part
        term[s, 0] = nt(ds[b], qs[b]).astype(BF)
        give(s, 0)

    mine = pl.ds(pl.multiple_of(xl * QUART, QUART), QUART)
    other = pl.ds(pl.multiple_of((1 - xl) * QUART, QUART), QUART)
    other_rows = pl.ds(pl.multiple_of(core * 256 + (1 - xl) * QUART, QUART), QUART)

    def fold_c(s):
        for j in (1, 0):
            bc[s, j].wait_recv()
            xsend[s, j] = (term[s, j, other_rows].astype(F32) + cbuf[s, j, other].astype(F32)).astype(BF)
            bx[s, j] = send(xsend.at[s, j], xbuf.at[s, j], x_peer)
            hold[s, j] = term[s, j, my_rows].astype(F32) + cbuf[s, j, mine].astype(F32)


    def fold_c_last():
        for j in (1, 0):
            bc[0, j].wait_recv()
            xs0[j] = (term[0, j, half_rows].astype(F32) + cbuf[0, j].astype(F32)).astype(BF)
            bx[0, j] = send(xs0.at[j], xr0.at[j], x_peer)

    def settle_last(j, at, arrived, rows):
        total = xs0[j, at].astype(F32) + xr0[j, at].astype(F32) + arrived.astype(F32)
        stage[j, y, rows] = total.astype(BF)

    def finish_last():
        coming = c < n_ctx - 1
        for j in (1, 0):
            bx[0, j].wait_recv()
            for k in range(NSUB):
                rows = slice(k * SUB, (k + 1) * SUB)

                @pl.when(coming)
                def _():
                    bz[1, j, k].wait_recv()

                @pl.when(c == n_ctx - 1)
                def _():
                    zbuf[0, j, rows] = jnp.zeros((SUB, HD), BF)

                at = pl.ds(pl.multiple_of(xl * QUART + k * SUB, SUB), SUB)
                settle_last(j, at, zbuf[0, j, rows], sub_rows[k])
            piece = stage.at[j, y, my_rows]
            aup[j] = send(piece, piece, y_next)
            adn[j] = send(piece, piece, y_prev)
        for j in (1, 0):
            @pl.when(coming)
            def _():
                bd[j].wait_recv()

            @pl.when(c == n_ctx - 1)
            def _():
                zdiag[j] = jnp.zeros((QUART, HD), BF)

            settle_last(j, other, zdiag[j], other_rows)
            piece = stage.at[j, y, other_rows]
            xup[j] = send(piece, piece, y_next)
            xdn[j] = send(piece, piece, y_prev)

    def fold_x(s):
        for j in (1, 0):
            if s in STRAIGHT:
                for cp in bx[s, j]:
                    cp.wait_recv()
            else:
                bx[s, j].wait_recv()
            for k in range(NSUB):
                rows = slice(k * SUB, (k + 1) * SUB)
                if s in STRAIGHT:
                    near = dbuf.at[s - STRAIGHT[0], j]
                    total = term[s, j, sub_rows[k]].astype(F32) + near[0, rows].astype(F32)
                    total = total + near[1, rows].astype(F32) + near[2, rows].astype(F32)
                else:
                    total = hold[s, j, rows] + xbuf[s, j, rows].astype(F32)
                if s < REACH:
                    @pl.when((c >= s) & (c < n_ctx - 1))
                    def _():
                        bz[s + 1, j, k].wait_recv()

                    @pl.when((c < s) | (c == n_ctx - 1))
                    def _():
                        zbuf[s, j, rows] = jnp.zeros((SUB, HD), BF)

                    total = total + zbuf[s, j, rows].astype(F32)
                zsend[s, j, rows] = total.astype(BF)
                bz[s, j, k] = send(zsend.at[s, j, rows], zbuf.at[s - 1, j, rows], z_prev, c >= s)
        if s == 1:
            for j in (1, 0):
                bd[j] = send(zsend.at[1, j], zdiag.at[j], z_prev_x, c >= 1)

    aup, adn, xup, xdn, bd = {}, {}, {}, {}, {}

    kept = []

    def keep(src, dst):
        cp = pltpu.make_async_copy(src, dst, ksem.at[len(kept)])
        cp.start()
        kept.append(cp)

    first_part = len(sent)
    backward(4)
    backward(3)
    backward(2)
    settle(first_part)
    fold_x(4)
    backward(1)
    fold_c(2)
    backward(0)
    fold_x(3)
    fold_c(1)
    fold_c_last()
    for h in range(2):
        o_v[:, h * HD:(h + 1) * HD] = ot[:, h * BLK:(h + 1) * BLK].T
    keep(o_v, o_ref)
    fold_x(2)
    for h in range(2):
        dq_v[:, h * HD:(h + 1) * HD] = (dqt[:, h * BLK:(h + 1) * BLK] * SCALE).astype(BF).T
    keep(dq_v, dq_ref)
    second_part = len(sent)
    fold_x(1)
    settle(second_part)
    finish_last()

    below = (y + 3) % 4
    above = (y + 1) % 4

    def hrow(which, k):
        return pl.ds(pl.multiple_of(core * 256 + which * QUART + k * 64, 64), 64)

    fin = []

    def relay(j, which):
        up = stage.at[j, below, hrow(which, 0)]
        dn = stage.at[j, above, hrow(which, 1)]
        up_out = kvg_ref.at[j, below, hrow(which, 0)]
        dn_out = kvg_ref.at[j, above, hrow(which, 1)]
        fin.append(send(up, up_out, y_next))
        fin.append(send(dn, dn_out, y_prev))
        fin.append(send(up, up_out, y_next_o))
        fin.append(send(dn, dn_out, y_prev_o))

    def share(j, g):
        piece, out = stage.at[j, g, half_rows], kvg_ref.at[j, g, half_rows]
        fin.append(send(piece, out, c_peer))
        keep(piece, out)

    for j in (1, 0):
        share(j, y)
    for j in (1, 0):
        aup[j].wait_recv()
        adn[j].wait_recv()
        relay(j, xl)
    for j in (1, 0):
        xup[j].wait_recv()
        xdn[j].wait_recv()
        relay(j, 1 - xl)
        for cols in (below, above):
            share(j, cols)
    for cp in fin:
        cp.wait_recv()
    settle(len(sent))
    for cp in kept:
        cp.wait()
    assert len(sent) == N_SEND, len(sent)


def place_outputs(o_raw, dq_raw, kvg_raw, o_out, dq_out, dk_out, dv_out, o_v, dq_v, kvg_v, isem, osem):
    fetch = [pltpu.make_async_copy(o_raw, o_v, isem.at[0]), pltpu.make_async_copy(dq_raw, dq_v, isem.at[1])]
    store = [pltpu.make_async_copy(o_v, o_out, osem.at[0]), pltpu.make_async_copy(dq_v, dq_out, osem.at[1])]
    for j, out in enumerate((dk_out, dv_out)):
        for g in range(KVH):
            i = len(fetch)
            fetch.append(pltpu.make_async_copy(kvg_raw.at[j, g], kvg_v.at[j, g], isem.at[i]))
            store.append(pltpu.make_async_copy(kvg_v.at[j, g], out.at[:, g * HD:(g + 1) * HD], osem.at[i]))
    for cp in fetch[2:] + fetch[:2]:
        cp.start()
    for get, put in zip(fetch[2:] + fetch[:2], store[2:] + store[:2]):
        get.wait()
        put.start()
    for cp in store:
        cp.wait()


N_SEND = 104


def solution(mesh):
    n_ctx = mesh.shape["ctx"]

    def per_device(queries, keys, values, out_grad, doc_lengths):
        steps = REACH + 1
        hbm = pl.BlockSpec(memory_space=pl.ANY)
        shapes = tuple(jax.ShapeDtypeStruct(a.shape, BF) for a in (queries, queries, keys, values))
        raw = pl.pallas_call(
            functools.partial(kernel, n_ctx, doc_lengths.shape[0]),
            out_shape=shapes[:2] + (jax.ShapeDtypeStruct((2, KVH, BLK, HD), BF),),
            in_specs=[hbm, hbm, hbm, hbm, pl.BlockSpec(memory_space=pltpu.SMEM)],
            out_specs=(hbm, hbm, hbm),
            scratch_shapes=[
                pltpu.VMEM((BLK, 256), BF),
                pltpu.VMEM((BLK, 256), BF),
                pltpu.VMEM((steps, 2, BLK, HD), BF),
                pltpu.VMEM((2 * HD, QN), BF),
                pltpu.VMEM((HD, QN), BF),
                pltpu.VMEM((steps, 1, HD, BLK), BF),
                pltpu.VMEM((2, HD + 8, BLK), BF),
                pltpu.VMEM((2, BLK, 2 * HD), BF),
                pltpu.VMEM((2, BLK, CH), F32),
                pltpu.VMEM((steps, BLK, QN), BF),
                pltpu.VMEM((steps, BLK, QN), F32),
                pltpu.VMEM((HD + 8, QN), F32),
                pltpu.VMEM((HD, QN), BF),
                pltpu.VMEM((HD, QN), F32),
                pltpu.VMEM((2, HD, QN), BF),
                pltpu.VMEM((2, HD, QN), BF),
                pltpu.VMEM((2, BLK, QN), BF),
                pltpu.VMEM((steps, 2, BLK, HD), BF),
                pltpu.VMEM((steps, 2, 256, HD), BF),
                pltpu.VMEM((len(STRAIGHT), 2, 3, QUART, HD), BF),
                pltpu.VMEM((steps, 2, QUART, HD), F32),
                pltpu.VMEM((steps, 2, QUART, HD), BF),
                pltpu.VMEM((steps, 2, QUART, HD), BF),
                pltpu.VMEM((REACH, 2, QUART, HD), BF),
                pltpu.VMEM((steps, 2, QUART, HD), BF),
                pltpu.VMEM((2, 256, HD), BF),
                pltpu.VMEM((2, 256, HD), BF),
                pltpu.VMEM((2, QUART, HD), BF),
                pltpu.VMEM((2, KVH, BLK, HD), BF),
                pltpu.VMEM((BLK, 256), BF),
                pltpu.VMEM((BLK, 256), BF),
                pltpu.SemaphoreType.DMA((8,)),
                pltpu.SemaphoreType.DMA((4,)),
                pltpu.SemaphoreType.DMA((N_SEND,)),
                pltpu.SemaphoreType.DMA((N_SEND,)),
            ],
            compiler_params=pltpu.CompilerParams(
                collective_id=0, has_side_effects=True, vmem_limit_bytes=60 * 1024 * 1024
            ),
        )(queries, keys, values, out_grad, doc_lengths)
        return pl.pallas_call(
            place_outputs,
            out_shape=shapes,
            in_specs=[hbm] * 3,
            out_specs=(hbm,) * 4,
            scratch_shapes=[
                pltpu.VMEM((BLK, 256), BF),
                pltpu.VMEM((BLK, 256), BF),
                pltpu.VMEM((2, KVH, BLK, HD), BF),
                pltpu.SemaphoreType.DMA((10,)),
                pltpu.SemaphoreType.DMA((10,)),
            ],
            compiler_params=pltpu.CompilerParams(vmem_limit_bytes=62 * 1024 * 1024),
        )(*raw)

    return jax.shard_map(
        per_device,
        mesh=mesh,
        in_specs=(P("ctx", "tp"), P("ctx", None), P("ctx", None), P("ctx", "tp"), P()),
        out_specs=(P("ctx", "tp"), P("ctx", "tp"), P("ctx", None), P("ctx", None)),
        check_vma=False,
    )
```
